32 devices in a mesh: loop: 16 (over z, x, core), rep: 2 (over y).
Axes of the slice: x: 2, y: 2, z: 4, core: 2. Of those that a mesh axis runs over, the one named last changes fastest.
Arguments:
- queries: bfloat16 [8192, 4096], P(('loop', 'rep')), may hold values from -2.5 to 2.5
- passages: bfloat16 [128, 4096], P('loop'), may hold values from -0.6 to 0.6
- index_rows: bfloat16 [8192, 4096], P(('loop', 'rep')), may hold values from -0.7 to 0.7
- positive: int32 [8192], P(('loop', 'rep')), may hold values from 0 to 127, as said below
- hard_rows: int32 [16, 32, 8], P('loop'), may hold values from 0 to 255
- hard_counts: int32 [16, 32], P('loop'), may hold values from 0 to 8, as said below
Outputs:
- query_grad: float32 [8192, 4096], P(('loop', 'rep'))
- passage_grad: float32 [128, 4096], P('loop')
- mean_loss: float32 [], replicated
The draws below stay inside these ranges and needn't reach their ends.
Inputs may be any that keep to these rules, and one draw needn't show every extreme that they name: `hard_counts`: in every draw some index shard takes 8 live slots from every query block. Every passage is the positive of exactly 64 queries.
All inputs are finite; a program needn't handle non-finite values.
Results may differ from the reference program's by a relative error of at most 0.0015.
Values may be sent and summed in bfloat16 or wider, within the bound.
No kernel may reach another device: no remote copies, remote signals or barrier semaphores. Data moves between devices by JAX's collectives and lax.ppermute only.
A program may use at most 128 MiB of HBM per device.

```python
import math
import jax
import jax.numpy as jnp
from jax import lax

D = 4096
QD = 256
CAP = 8
BANK_DEV = 256
GROUPS = 16
OWNERS = 32
NQ = 8192
NP = 128
BANK_ROWS = 8192
N_REP = 2


def passage_field(key):
    sigma = 1.8 / math.sqrt(D)
    base = jax.random.normal(jax.random.fold_in(key, 11), (NP, D), jnp.float32) * sigma
    return jnp.clip(base, -0.59375, 0.59375)


def draw_passages(key, part):
    return passage_field(key).astype(jnp.bfloat16)


def draw_queries(key, part):
    sigma = 1.8 / math.sqrt(D)
    row_ids = jnp.arange(NQ)
    spread = jnp.exp(jax.random.uniform(jax.random.fold_in(key, 21), (NQ, 1), jnp.float32, minval=math.log(0.4), maxval=math.log(4.0)))
    ramp = (1.0 + 2.0 * row_ids.astype(jnp.float32) / NQ)[:, None]
    noise = jax.random.normal(jax.random.fold_in(key, 23), (NQ, D), jnp.float32)
    values = noise * sigma * spread * ramp
    return jnp.clip(values, -2.5, 2.5).astype(jnp.bfloat16)


def draw_index_rows(key, part):
    sigma = 2.2 / math.sqrt(D)
    noise = jax.random.normal(jax.random.fold_in(key, 42), (BANK_ROWS, D), jnp.float32)
    return jnp.clip(noise * sigma, -0.69921875, 0.69921875).astype(jnp.bfloat16)


def draw_positive(key, part):
    order = jax.random.permutation(jax.random.fold_in(key, 51), NQ).astype(jnp.int32)
    return (order % NP).astype(jnp.int32)


def draw_hard_counts(key, part):
    counts = jax.random.randint(jax.random.fold_in(key, 31), (GROUPS, OWNERS), 0, CAP + 1, jnp.int32)
    busiest = jax.random.randint(jax.random.fold_in(key, 32), (), 0, OWNERS, jnp.int32)
    column = jnp.arange(OWNERS, dtype=jnp.int32)[None, :]
    return jnp.where(column == busiest, CAP, counts).astype(jnp.int32)


def with_ends(array, key, low, high):
    dims = array.shape
    place = [jax.random.randint(jax.random.fold_in(key, axis), (), 0, dims[axis]) for axis in range(len(dims))]
    array = array.at[tuple(place)].set(low)
    longest = dims.index(max(dims))
    place[longest] = (place[longest] + 1) % dims[longest]
    return array.at[tuple(place)].set(high)


def setup_inputs(seed: int = 0) -> dict:
    splits = jax.random.split(jax.random.key(seed), 7)
    queries = draw_queries(jax.random.fold_in(splits[6], 71), 0)
    passages = draw_passages(jax.random.fold_in(splits[6], 71), 0)
    index_rows = draw_index_rows(jax.random.fold_in(splits[6], 71), 0)
    positive = draw_positive(jax.random.fold_in(splits[6], 71), 0)
    hard_rows = with_ends(jax.random.randint(splits[4], (GROUPS, OWNERS, CAP), 0, BANK_DEV), jax.random.fold_in(splits[4], 1), 0, BANK_DEV - 1).astype(jnp.int32)
    hard_counts = draw_hard_counts(jax.random.fold_in(splits[6], 71), 0)
    return dict(queries=queries, passages=passages, index_rows=index_rows, positive=positive, hard_rows=hard_rows, hard_counts=hard_counts)


def reference(queries, passages, index_rows, positive, hard_rows, hard_counts):
    group_size = QD * N_REP
    query_groups = queries.reshape(GROUPS, group_size, D)
    positive_groups = positive.reshape(GROUPS, group_size)
    shard_base = (jnp.arange(OWNERS, dtype=jnp.int32) * BANK_DEV)[:, None]
    slot_ids = jnp.arange(CAP, dtype=jnp.int32)[None, :]
    passage_ids = jnp.arange(NP, dtype=jnp.int32)[None, :]

    def one_group(carry, inputs):
        grad_sum, loss_sum = carry
        group_queries, group_positive, group_rows, group_counts = inputs
        flat_ids = (shard_base + group_rows).reshape(-1).astype(jnp.int32)
        hard_block = index_rows[flat_ids]
        live_slots = (slot_ids < group_counts[:, None]).reshape(-1)
        scores = 50.0 * jnp.dot(group_queries, passages.T, preferred_element_type=jnp.float32)
        hard_scores = 50.0 * jnp.dot(group_queries, hard_block.T, preferred_element_type=jnp.float32)
        hard_scores = jnp.where(live_slots[None, :], hard_scores, -jnp.inf)
        row_top = jnp.maximum(jnp.max(scores, axis=1), jnp.max(hard_scores, axis=1))[:, None]
        log_total = row_top + jnp.log(jnp.sum(jnp.exp(scores - row_top), axis=1, keepdims=True)
                                      + jnp.sum(jnp.exp(hard_scores - row_top), axis=1, keepdims=True))
        onehot = (group_positive[:, None] == passage_ids).astype(jnp.float32)
        weights = (jnp.exp(scores - log_total) - onehot).astype(jnp.bfloat16)
        hard_weights = jnp.exp(hard_scores - log_total).astype(jnp.bfloat16)
        query_part = 50.0 * (jnp.dot(weights, passages, preferred_element_type=jnp.float32)
                             + jnp.dot(hard_weights, hard_block, preferred_element_type=jnp.float32))
        passage_part = 50.0 * jnp.dot(weights.T, group_queries, preferred_element_type=jnp.float32)
        loss_part = jnp.sum(log_total[:, 0] - jnp.sum(scores * onehot, axis=1))
        return (grad_sum + passage_part, loss_sum + loss_part), query_part

    start_carry = (jnp.zeros((NP, D), jnp.float32), jnp.zeros((), jnp.float32))
    final_carry, query_parts = lax.scan(one_group, start_carry,
                                        (query_groups, positive_groups, hard_rows, hard_counts))
    passage_grad, loss_sum = final_carry
    return query_parts.reshape(NQ, D), passage_grad, loss_sum / NQ
```

```python
import jax
import jax.numpy as jnp
from jax import lax
from jax.sharding import PartitionSpec as P

CHUNKS = 2


def exchange(value, axes, mask):
    size = 1
    for axis in axes:
        size *= lax.axis_size(axis)
    return lax.ppermute(value, axes, [(i, i ^ mask) for i in range(size)])


def shards(queries, passages, index_rows, positive, hard_rows, hard_counts):
    loop = lax.axis_size("loop")
    reps = lax.axis_size("rep")
    me = lax.axis_index("loop")
    rep = lax.axis_index("rep")
    far = 1 - rep
    width = queries.shape[1]
    block = passages.shape[0]
    slots = hard_rows.shape[2]
    half = width // 2
    step = width // CHUNKS

    wanted = hard_rows[0].reshape(loop, reps, slots)
    asked = lax.all_to_all(
        lax.dynamic_index_in_dim(wanted, rep, 1, keepdims=False),
        "loop", split_axis=0, concat_axis=0, tiled=True,
    )
    near_parts, far_parts = [], []
    for k in range(CHUNKS):
        found = index_rows[:, k * step:(k + 1) * step].at[asked].get(mode="promise_in_bounds")
        near = lax.all_to_all(found, "loop", split_axis=0, concat_axis=0, tiled=True)
        near = near.reshape(loop * slots, step)
        near_parts.append(near)
        far_parts.append(lax.ppermute(near, "rep", [(0, 1), (1, 0)]))

    counts = hard_counts[0].reshape(loop, reps)
    slot_ids = jnp.arange(slots, dtype=jnp.int32)[None, :]

    def live(plane):
        taken = lax.dynamic_index_in_dim(counts, plane, 1, keepdims=False)
        return (slot_ids < taken[:, None]).reshape(1, -1)

    rest = loop // 4
    quad = jnp.concatenate(
        [passages] + [exchange(passages, ("loop",), 4 * m) for m in range(1, rest)], axis=0
    )
    pair = jnp.concatenate([quad, exchange(quad, ("loop",), 2)], axis=0)
    gathered = jnp.concatenate([pair, exchange(pair, ("loop",), 1)], axis=0)
    place = jnp.arange(loop, dtype=jnp.int32)
    owner = ((place % rest) * 4 + (place // rest % 2) * 2 + place // (2 * rest)) ^ me
    ids = (owner[:, None] * block + jnp.arange(block, dtype=jnp.int32)[None, :]).reshape(1, -1)

    contract = (((1,), (1,)), ((), ()))

    def scored(parts):
        total = 0.0
        for k, part in enumerate(parts):
            total = total + lax.dot_general(
                queries[:, k * step:(k + 1) * step], part, contract,
                preferred_element_type=jnp.float32,
            )
        return 50.0 * total

    scores = 50.0 * lax.dot_general(queries, gathered, contract, preferred_element_type=jnp.float32)
    near_scores = jnp.where(live(rep), scored(near_parts), -jnp.inf)
    far_scores = jnp.where(live(far), scored(far_parts), -jnp.inf)
    row_top = jnp.maximum(
        jnp.max(scores, axis=1),
        jnp.maximum(jnp.max(near_scores, axis=1), jnp.max(far_scores, axis=1)),
    )[:, None]
    log_total = row_top + jnp.log(
        jnp.sum(jnp.exp(scores - row_top), axis=1, keepdims=True)
        + jnp.sum(jnp.exp(near_scores - row_top), axis=1, keepdims=True)
        + jnp.sum(jnp.exp(far_scores - row_top), axis=1, keepdims=True)
    )
    onehot = (positive[:, None] == ids).astype(jnp.float32)
    weights = (jnp.exp(scores - log_total) - onehot).astype(jnp.bfloat16)
    near_weights = jnp.exp(near_scores - log_total).astype(jnp.bfloat16)
    far_weights = jnp.exp(far_scores - log_total).astype(jnp.bfloat16)
    loss = jnp.sum(log_total[:, 0] - jnp.sum(scores * onehot, axis=1)).reshape(1, 1)
    loss = jnp.broadcast_to(loss, (1, 128))

    swapped = jnp.concatenate(
        [
            lax.dynamic_slice_in_dim(queries, rep * half, half, 1),
            lax.dynamic_slice_in_dim(queries, far * half, half, 1),
        ],
        axis=1,
    )

    def partial(columns):
        return 50.0 * lax.dot_general(
            columns, swapped, (((0,), (0,)), ((), ())), preferred_element_type=jnp.float32
        )

    rows = loop * block
    sent = exchange(partial(weights[:, rows // 2:]), ("loop",), 1)
    held = partial(weights[:, :rows // 2]) + sent
    loss = loss + exchange(loss, ("loop",), 1)
    quarter = rows // 4
    both = ("loop", "rep")
    step_x = exchange(held[quarter:, :half], both, 4)
    step_y = exchange(held[:quarter, half:], both, 1)
    step_xy = exchange(held[quarter:, half:], both, 5)
    loss = loss + exchange(loss, both, 4) + exchange(loss, both, 1) + exchange(loss, both, 5)
    held = held[:quarter, :half] + step_x + step_y + step_xy
    total = held[:block]
    loss_sum = loss
    for m in range(1, rest):
        total = total + exchange(held[m * block:(m + 1) * block], ("loop",), 4 * m)
        loss_sum = loss_sum + exchange(loss, ("loop",), 4 * m)
    other = exchange(total, ("rep",), 1)
    passage_grad = jnp.where(
        rep == 0,
        jnp.concatenate([total, other], axis=1),
        jnp.concatenate([other, total], axis=1),
    )
    mean_loss = loss_sum[0, 0] / (queries.shape[0] * loop * reps)

    query_grad = jnp.concatenate(
        [
            50.0 * (
                jnp.dot(weights, gathered[:, k * step:(k + 1) * step], preferred_element_type=jnp.float32)
                + jnp.dot(near_weights, near_parts[k], preferred_element_type=jnp.float32)
                + jnp.dot(far_weights, far_parts[k], preferred_element_type=jnp.float32)
            )
            for k in range(CHUNKS)
        ],
        axis=1,
    )
    return (query_grad, passage_grad, mean_loss)


def solution(mesh):
    placed = (
        P(("loop", "rep"), None),
        P("loop", None),
        P(("loop", "rep"), None),
        P(("loop", "rep")),
        P("loop", None, None),
        P("loop", None),
    )
    return jax.shard_map(
        shards,
        mesh=mesh,
        in_specs=placed,
        out_specs=(P(("loop", "rep"), None), P("loop", None), P()),
        check_vma=False,
    )
```

```python
import functools

import jax
import jax.numpy as jnp
from jax import lax
from jax.experimental import pallas as pl
from jax.experimental.pallas import tpu as pltpu
from jax.sharding import PartitionSpec as P


def budget(*arrays):
    total = sum(a.size * a.dtype.itemsize for a in arrays)
    return pltpu.CompilerParams(vmem_limit_bytes=total + total // 4 + 6 * 1024 * 1024)


WHOLE = pl.BlockSpec(memory_space=pltpu.VMEM)
SCALARS = pl.BlockSpec(memory_space=pltpu.SMEM)
LOSS = 128


def exchange(value, axes, mask):
    size = 1
    for axis in axes:
        size *= lax.axis_size(axis)
    return lax.ppermute(value, axes, [(i, i ^ mask) for i in range(size)])


def pick_rows(meta, asked, own, other, passages, passages_out, *pieces):
    me, rep = meta[0], meta[1]
    slots, owners = asked.shape[1:]
    lanes = lax.broadcasted_iota(jnp.int32, (slots, owners), 1)
    rows = lax.broadcasted_iota(jnp.int32, (slots, own.shape[0]), 1)

    def hot(owner):
        picked = []
        for m in range(len(pieces)):
            tile = asked[me ^ (2 * m)]
            column = jnp.sum(jnp.where(lanes == owner, tile, 0), axis=1, keepdims=True)
            picked.append(jnp.where(column == rows, 1.0, 0.0))
        return jnp.concatenate(picked, axis=0).astype(jnp.bfloat16)

    passages_out[...] = passages[...]
    hot_own = hot(me * 2 + rep)
    hot_other = hot((me ^ 1) * 2 + rep)
    width = own.shape[1]
    step = min(width, 512)
    for at in range(0, width, step):
        columns = pl.ds(at, step)
        got_own = jnp.dot(hot_own, own[:, columns], preferred_element_type=jnp.float32)
        got_other = jnp.dot(hot_other, other[:, columns], preferred_element_type=jnp.float32)
        for m, piece in enumerate(pieces):
            part = slice(m * slots, (m + 1) * slots)
            piece[:, columns] = jnp.concatenate(
                [got_own[part], got_other[part]], axis=0
            ).astype(jnp.bfloat16)


def score_kernel(count, meta, queries, gathered, positive, ids, live, *refs):
    pieces = refs[:count]
    weights_out, hard_out, send_out, hard = refs[count:]
    rep = meta[1]
    depth = pieces[0].shape[0]
    for i, piece in enumerate(pieces):
        hard[i * depth:(i + 1) * depth, :] = piece[...]
    contract = (((1,), (1,)), ((), ()))
    q = queries[...]
    scores = 50.0 * lax.dot_general(q, gathered[...], contract, preferred_element_type=jnp.float32)
    hard_scores = 50.0 * lax.dot_general(q, hard[...], contract, preferred_element_type=jnp.float32)
    hard_scores = jnp.where(live[...] > 0, hard_scores, -jnp.inf)
    row_top = jnp.maximum(
        jnp.max(scores, axis=1, keepdims=True), jnp.max(hard_scores, axis=1, keepdims=True)
    )
    log_total = row_top + jnp.log(
        jnp.sum(jnp.exp(scores - row_top), axis=1, keepdims=True)
        + jnp.sum(jnp.exp(hard_scores - row_top), axis=1, keepdims=True)
    )
    onehot = jnp.where(positive[...] == ids[...], 1.0, 0.0)
    weights = (jnp.exp(scores - log_total) - onehot).astype(jnp.bfloat16)
    weights_out[...] = weights
    hard_out[...] = jnp.exp(hard_scores - log_total).astype(jnp.bfloat16)
    loss = jnp.sum(log_total - jnp.sum(scores * onehot, axis=1, keepdims=True))
    rows = weights.shape[1] // 2
    project(send_out, weights[:, rows:], queries, rep, loss)


def project(out, weights, queries, rep, loss):
    half = queries.shape[1] // 2
    for i, side in enumerate((rep, 1 - rep)):
        product = lax.dot_general(
            weights, queries[:, pl.ds(pl.multiple_of(side * half, half), half)],
            (((0,), (0,)), ((), ())), preferred_element_type=jnp.float32,
        )
        at = i * (half + LOSS)
        out[:, at:at + half] = 50.0 * product
        out[:, at + half:at + half + LOSS] = jnp.full((out.shape[0], LOSS), loss, jnp.float32)


def keep_kernel(meta, weights, queries, send, out):
    rows = out.shape[0]
    half = queries.shape[1] // 2
    loss = send[0:1, half:half + 1]
    project(out, weights[:, :rows], queries, meta[1], loss)


def first_sum(kept, sent, own, to_x, to_y, to_xy):
    rows, columns = own.shape
    for out, down, across in ((own, 0, 0), (to_x, 1, 0), (to_y, 0, 1), (to_xy, 1, 1)):
        at = (pl.ds(down * rows, rows), pl.ds(across * columns, columns))
        out[...] = kept[at] + sent[at]


def second_sum(own, from_x, from_y, from_xy, after, *outs):
    rows = outs[0].shape[0]
    for i, out in enumerate(outs):
        at = pl.ds(i * rows, rows)
        out[...] = (own[at] + from_x[at]) + (from_y[at] + from_xy[at])


def grad_kernel(count, weights, hard_weights, gathered, *refs):
    pieces = refs[:count]
    out, done, hard = refs[count:]
    done[...] = jnp.zeros(done.shape, done.dtype)
    depth = pieces[0].shape[0]
    for i, piece in enumerate(pieces):
        hard[i * depth:(i + 1) * depth, :] = piece[...]
    out[...] = 50.0 * (
        jnp.dot(weights[...], gathered[...], preferred_element_type=jnp.float32)
        + jnp.dot(hard_weights[...], hard[...], preferred_element_type=jnp.float32)
    )


def shards(queries, passages, index_rows, positive, hard_rows, hard_counts):
    loop = lax.axis_size("loop")
    reps = lax.axis_size("rep")
    me = lax.axis_index("loop").astype(jnp.int32)
    rep = lax.axis_index("rep").astype(jnp.int32)
    count, width = queries.shape
    block = passages.shape[0]
    owners, slots = hard_rows.shape[1:]
    half = width // 2
    chips = loop // 2
    meta = jnp.stack([me, rep])
    both = ("loop", "rep")

    lanes = -owners % 128
    asked = lax.all_to_all(
        jnp.broadcast_to(
            jnp.pad(jnp.transpose(hard_rows, (0, 2, 1)), ((0, 0), (0, 0), (0, lanes))),
            (loop, slots, owners + lanes),
        ),
        "loop", split_axis=0, concat_axis=0, tiled=True,
    )
    other_rows = exchange(index_rows, ("loop",), 1)
    piece = jax.ShapeDtypeStruct((2 * slots, width), jnp.bfloat16)
    passages, *own_pieces = pl.pallas_call(
        pick_rows,
        out_shape=[jax.ShapeDtypeStruct(passages.shape, passages.dtype)] + [piece] * chips,
        in_specs=[SCALARS] + [WHOLE] * 4,
        out_specs=[WHOLE] * (1 + chips),
        compiler_params=budget(index_rows, index_rows, *[piece] * chips),
        cost_estimate=pl.CostEstimate(
            flops=4 * chips * slots * index_rows.shape[0] * width,
            bytes_accessed=3 * index_rows.size * 2, transcendentals=0,
        ),
    )(meta, asked, index_rows, other_rows, passages)
    near = [None] * chips
    far = [None] * chips
    near[0] = own_pieces[0]
    for m in reversed(range(1, chips)):
        near[m] = exchange(own_pieces[m], ("loop",), 2 * m)
    for m in range(chips):
        far[m] = exchange(near[m], ("rep",), 1)

    place = jnp.arange(chips * 2, dtype=jnp.int32)
    source = (place // 2 * 2) ^ (place % 2) ^ me
    hits = (source[:, None] * reps + jnp.stack([rep, 1 - rep])[None, :]).T.reshape(-1)
    spread = hits[:, None] == jnp.arange(owners, dtype=jnp.int32)[None, :]
    taken = jnp.sum(jnp.where(spread, hard_counts, 0), axis=1)
    live = (jnp.arange(slots, dtype=jnp.int32)[None, :] < taken[:, None])
    live = live.astype(jnp.int32).reshape(1, -1)

    rest = loop // 4
    gathered = passages
    bits = [loop // 2 >> i for i in range(loop.bit_length() - 3)] + [2, 1]
    for bit in bits:
        gathered = jnp.concatenate([gathered, exchange(gathered, ("loop",), bit)], axis=0)
    orders = [0]
    for bit in bits:
        orders = orders + [o | bit for o in orders]
    owner = jnp.array(orders, jnp.int32) ^ me
    ids = (owner[:, None] * block + jnp.arange(block, dtype=jnp.int32)[None, :]).reshape(1, -1)

    rows = loop * block
    hard_count = owners * slots
    pieces = near + far
    hard_all = jax.ShapeDtypeStruct((hard_count, width), jnp.bfloat16)
    payload = jax.ShapeDtypeStruct((rows // 2, width + 2 * LOSS), jnp.float32)
    weights, hard_weights, send = pl.pallas_call(
        functools.partial(score_kernel, 2 * chips),
        out_shape=[
            jax.ShapeDtypeStruct((count, rows), jnp.bfloat16),
            jax.ShapeDtypeStruct((count, hard_count), jnp.bfloat16),
            jax.ShapeDtypeStruct((rows // 2, width + 2 * LOSS), jnp.float32),
        ],
        in_specs=[SCALARS] + [WHOLE] * (5 + 2 * chips),
        out_specs=[WHOLE] * 3,
        scratch_shapes=[pltpu.VMEM((hard_count, width), jnp.bfloat16)],
        compiler_params=budget(queries, gathered, hard_all, hard_all, payload),
        cost_estimate=pl.CostEstimate(
            flops=2 * count * (rows + hard_count + rows // 2) * width,
            bytes_accessed=2 * (count + rows + hard_count) * width + 2 * rows * width,
            transcendentals=2 * count * (rows + hard_count),
        ),
    )(meta, queries, gathered, positive.reshape(count, 1), ids, live, *pieces)

    sent = exchange(send, ("loop",), 1)
    kept = pl.pallas_call(
        keep_kernel,
        out_shape=jax.ShapeDtypeStruct((rows // 2, width + 2 * LOSS), jnp.float32),
        in_specs=[SCALARS] + [WHOLE] * 3,
        out_specs=WHOLE,
        compiler_params=budget(queries, payload, payload),
        cost_estimate=pl.CostEstimate(
            flops=count * rows * width,
            bytes_accessed=2 * count * width + 2 * rows * width, transcendentals=0,
        ),
    )(meta, weights, queries, send)
    query_grad, done = pl.pallas_call(
        functools.partial(grad_kernel, 2 * chips),
        out_shape=[
            jax.ShapeDtypeStruct((count, width), jnp.float32),
            jax.ShapeDtypeStruct((8, 128), jnp.float32),
        ],
        in_specs=[WHOLE] * (3 + 2 * chips),
        out_specs=[WHOLE] * 2,
        scratch_shapes=[pltpu.VMEM((hard_count, width), jnp.bfloat16)],
        compiler_params=budget(queries, queries, gathered, hard_all, hard_all),
        cost_estimate=pl.CostEstimate(
            flops=2 * count * (rows + hard_count) * width,
            bytes_accessed=2 * (rows + hard_count) * width + 4 * count * width,
            transcendentals=0,
        ),
    )(weights, hard_weights, gathered, *pieces)
    part = half + LOSS
    quarter = rows // 4
    first = jax.ShapeDtypeStruct((quarter, part), jnp.float32)
    own, *going = pl.pallas_call(
        first_sum,
        out_shape=[first] * 4,
        in_specs=[WHOLE] * 2,
        out_specs=[WHOLE] * 4,
        compiler_params=budget(payload, payload, payload),
        cost_estimate=pl.CostEstimate(
            flops=payload.size, bytes_accessed=12 * payload.size, transcendentals=0
        ),
    )(kept, sent)
    came = [exchange(value, both, mask) for value, mask in zip(going, (4, 1, 5))]
    second = jax.ShapeDtypeStruct((block, part), jnp.float32)
    total, *going = pl.pallas_call(
        second_sum,
        out_shape=[second] * rest,
        in_specs=[WHOLE] * 5,
        out_specs=[WHOLE] * rest,
        compiler_params=budget(payload, payload),
        cost_estimate=pl.CostEstimate(
            flops=4 * first.size, bytes_accessed=20 * first.size, transcendentals=0
        ),
    )(own, *came, done)
    for value, order in zip(going, orders[1:rest]):
        total = total + exchange(value, ("loop",), order)
    mean_loss = total[0, half] / (count * loop * reps)
    total = total[:, :half]
    opposite = exchange(total, ("rep",), 1)
    passage_grad = jnp.where(
        rep == 0,
        jnp.concatenate([total, opposite], axis=1),
        jnp.concatenate([opposite, total], axis=1),
    )

    return (query_grad, passage_grad, mean_loss)


def solution(mesh):
    placed = (
        P(("loop", "rep"), None),
        P("loop", None),
        P(("loop", "rep"), None),
        P(("loop", "rep")),
        P("loop", None, None),
        P("loop", None),
    )
    return jax.shard_map(
        shards,
        mesh=mesh,
        in_specs=placed,
        out_specs=(P(("loop", "rep"), None), P("loop", None), P()),
        check_vma=False,
    )
```

```python
import functools

import jax
import jax.numpy as jnp
from jax import lax
from jax.experimental import pallas as pl
from jax.experimental.pallas import tpu as pltpu
from jax.sharding import PartitionSpec as P


def budget(*arrays):
    total = sum(a.size * a.dtype.itemsize for a in arrays)
    return pltpu.CompilerParams(vmem_limit_bytes=total + total // 4 + 6 * 1024 * 1024)


WHOLE = pl.BlockSpec(memory_space=pltpu.VMEM)
SCALARS = pl.BlockSpec(memory_space=pltpu.SMEM)
LOSS = 128


def exchange(value, axes, mask):
    size = 1
    for axis in axes:
        size *= lax.axis_size(axis)
    return lax.ppermute(value, axes, [(i, i ^ mask) for i in range(size)])


def ask_kernel(wanted, asked):
    owners = wanted.shape[2]
    asked[...] = jnp.zeros(asked.shape, asked.dtype)
    asked[:, :, :owners] = jnp.broadcast_to(wanted[...], asked.shape[:2] + (owners,))


def pick_rows(meta, asked, other, own_hbm, known, known_out, *refs):
    *pieces, own, arrived = refs
    load = pltpu.make_async_copy(own_hbm, own, arrived)
    load.start()
    me, rep = meta[0], meta[1]
    slots, owners = asked.shape[1:]
    lanes = lax.broadcasted_iota(jnp.int32, (slots, owners), 1)
    rows = lax.broadcasted_iota(jnp.int32, (slots, own.shape[0]), 1)

    def hot(owner):
        picked = []
        for m in range(len(pieces)):
            tile = asked[me ^ (2 * m)]
            column = jnp.sum(jnp.where(lanes == owner, tile, 0), axis=1, keepdims=True)
            picked.append(jnp.where(column == rows, 1.0, 0.0))
        return jnp.concatenate(picked, axis=0).astype(jnp.bfloat16)

    hot_own = hot(me * 2 + rep)
    hot_other = hot((me ^ 1) * 2 + rep)
    known_out[...] = known[...]
    for piece in pieces[1:4]:
        piece[2 * slots:, :] = known[...]
    got_other = jnp.dot(hot_other, other[...], preferred_element_type=jnp.float32)
    load.wait()
    got_own = jnp.dot(hot_own, own[...], preferred_element_type=jnp.float32)
    for m, piece in enumerate(pieces):
        part = slice(m * slots, (m + 1) * slots)
        piece[:2 * slots, :] = jnp.concatenate(
            [got_own[part], got_other[part]], axis=0
        ).astype(jnp.bfloat16)


def pack_kernel(layouts, *refs):
    ins, outs = refs[:-len(layouts)], refs[-len(layouts):]
    for layout, out in zip(layouts, outs):
        at = 0
        for which, first, rows in layout:
            out[at:at + rows, :] = ins[which][first:first + rows, :]
            at += rows


def pack(layouts, *arrays):
    shapes = [
        jax.ShapeDtypeStruct((sum(rows for _, _, rows in layout), arrays[0].shape[1]), arrays[0].dtype)
        for layout in layouts
    ]
    size = sum(shape.size for shape in shapes)
    return pl.pallas_call(
        functools.partial(pack_kernel, layouts),
        out_shape=shapes,
        in_specs=[WHOLE] * len(arrays),
        out_specs=[WHOLE] * len(layouts),
        compiler_params=budget(*shapes, *arrays),
        cost_estimate=pl.CostEstimate(flops=size, bytes_accessed=4 * size, transcendentals=0),
    )(*arrays)


def stack(refs, out):
    at = 0
    for ref in refs:
        out[at:at + ref.shape[0], :] = ref[...]
        at += ref.shape[0]


def score_kernel(count, meta, queries, positive, ids, live, *refs):
    weights_out, hard_out, send_out, gathered, hard = refs[count:]
    rep = meta[1]
    stack(refs[:2], gathered)
    stack(refs[2:count], hard)
    contract = (((1,), (1,)), ((), ()))
    q = queries[...]
    scores = 50.0 * lax.dot_general(q, gathered[...], contract, preferred_element_type=jnp.float32)
    hard_scores = 50.0 * lax.dot_general(q, hard[...], contract, preferred_element_type=jnp.float32)
    hard_scores = jnp.where(live[...] > 0, hard_scores, -jnp.inf)
    row_top = jnp.maximum(
        jnp.max(scores, axis=1, keepdims=True), jnp.max(hard_scores, axis=1, keepdims=True)
    )
    log_total = row_top + jnp.log(
        jnp.sum(jnp.exp(scores - row_top), axis=1, keepdims=True)
        + jnp.sum(jnp.exp(hard_scores - row_top), axis=1, keepdims=True)
    )
    onehot = jnp.where(positive[...] == ids[...], 1.0, 0.0)
    weights = (jnp.exp(scores - log_total) - onehot).astype(jnp.bfloat16)
    weights_out[...] = weights
    hard_out[...] = jnp.exp(hard_scores - log_total).astype(jnp.bfloat16)
    loss = jnp.sum(log_total - jnp.sum(scores * onehot, axis=1, keepdims=True))
    rows = weights.shape[1] // 2
    project(send_out, weights[:, rows:], queries, rep, loss)


def project(out, weights, queries, rep, loss):
    half = queries.shape[1] // 2
    for i, side in enumerate((rep, 1 - rep)):
        product = lax.dot_general(
            weights, queries[:, pl.ds(pl.multiple_of(side * half, half), half)],
            (((0,), (0,)), ((), ())), preferred_element_type=jnp.float32,
        )
        at = i * (half + LOSS)
        out[:, at:at + half] = 50.0 * product
        out[:, at + half:at + half + LOSS] = jnp.full((out.shape[0], LOSS), loss, jnp.float32)


def keep_kernel(meta, weights, queries, send, out):
    rows = out.shape[0]
    half = queries.shape[1] // 2
    loss = send[0:1, half:half + 1]
    project(out, weights[:, :rows], queries, meta[1], loss)


def first_sum(kept, sent, own, to_x, to_y, to_xy):
    rows, columns = own.shape
    half = columns - LOSS
    lanes = lax.broadcasted_iota(jnp.int32, (rows, LOSS), 1)
    for out, down, across in ((own, 0, 0), (to_x, 1, 0), (to_y, 0, 1), (to_xy, 1, 1)):
        at = pl.ds(down * rows, rows)
        data = pl.ds(across * columns, half)
        out[:, :half] = (kept[at, data] + sent[at, data]).astype(out.dtype)
        tile = pl.ds(across * columns + half, LOSS)
        loss = kept[at, tile] + sent[at, tile]
        high = loss.astype(jnp.bfloat16).astype(jnp.float32)
        out[:, half:] = jnp.where(lanes < LOSS // 2, high, loss - high).astype(out.dtype)


def second_sum(own, from_x, from_y, from_xy, after, *outs):
    rows = outs[0].shape[0]
    for i, out in enumerate(outs):
        at = pl.ds(i * rows, rows)
        out[...] = (own[at] + from_x[at].astype(jnp.float32)) + (
            from_y[at].astype(jnp.float32) + from_xy[at].astype(jnp.float32)
        )


def grad_kernel(count, weights, hard_weights, *refs):
    out, done, gathered, hard = refs[count:]
    done[...] = jnp.zeros(done.shape, done.dtype)
    stack(refs[:2], gathered)
    stack(refs[2:count], hard)
    out[...] = 50.0 * (
        jnp.dot(weights[...], gathered[...], preferred_element_type=jnp.float32)
        + jnp.dot(hard_weights[...], hard[...], preferred_element_type=jnp.float32)
    )


def shards(queries, passages, index_rows, positive, hard_rows, hard_counts):
    loop = lax.axis_size("loop")
    reps = lax.axis_size("rep")
    me = lax.axis_index("loop").astype(jnp.int32)
    rep = lax.axis_index("rep").astype(jnp.int32)
    count, width = queries.shape
    block = passages.shape[0]
    owners, slots = hard_rows.shape[1:]
    half = width // 2
    chips = loop // 2
    meta = jnp.stack([me, rep])
    both = ("loop", "rep")

    other_rows = exchange(index_rows, ("loop",), 1)
    request = jax.ShapeDtypeStruct((loop, slots, owners + -owners % 128), jnp.int32)
    request = pl.pallas_call(
        ask_kernel,
        out_shape=request,
        in_specs=[WHOLE],
        out_specs=WHOLE,
        compiler_params=budget(request),
        cost_estimate=pl.CostEstimate(
            flops=request.size, bytes_accessed=8 * request.size, transcendentals=0
        ),
    )(jnp.transpose(hard_rows, (0, 2, 1)))
    asked = lax.all_to_all(request, "loop", split_axis=0, concat_axis=0, tiled=True)

    bits = [loop // 2 >> i for i in range(loop.bit_length() - 4)] + [4, 2, 1]
    orders = [0]
    for bit in bits:
        orders = orders + [o | bit for o in orders]
    known = passages
    for bit in bits[:-3]:
        known = jnp.concatenate([known, exchange(known, ("loop",), bit)], axis=0)

    depth = 2 * slots
    have = known.shape[0]
    pieces = [
        jax.ShapeDtypeStruct((depth + have * (m in (1, 2, 3)), width), jnp.bfloat16) for m in range(chips)
    ]
    known, *sends = pl.pallas_call(
        pick_rows,
        out_shape=[jax.ShapeDtypeStruct(known.shape, known.dtype)] + pieces,
        in_specs=[SCALARS, WHOLE, WHOLE, pl.BlockSpec(memory_space=pltpu.HBM), WHOLE],
        out_specs=[WHOLE] * (1 + chips),
        scratch_shapes=[
            pltpu.VMEM(index_rows.shape, index_rows.dtype), pltpu.SemaphoreType.DMA
        ],
        compiler_params=budget(index_rows, index_rows, index_rows, *pieces, *pieces),
        cost_estimate=pl.CostEstimate(
            flops=4 * chips * slots * index_rows.shape[0] * width,
            bytes_accessed=3 * index_rows.size * 2, transcendentals=0,
        ),
    )(meta, asked, other_rows, index_rows, known)

    def send(m, value):
        return exchange(value, ("loop",), 2 * m)

    groups = (
        tuple(range(chips // 2)),
        tuple(range(chips // 2, chips * 3 // 4)),
        tuple(range(chips * 3 // 4, chips)),
    )
    early = [sends[0]] + [send(m, sends[m]) for m in groups[0][1:]]
    middle = [send(m, sends[m]) for m in groups[1]]
    count_early, count_late = len(groups[0]), len(groups[2])
    first, pair, *late = pack(
        [[(i, 0, depth) for i in range(count_early)],
         [(count_early, 0, have)] + [(i, depth, have) for i in (2, 1, 3)]]
        + [[(count_early + 1 + i, 0, depth)] for i in range(count_late)],
        *early, known, *[sends[m] for m in groups[2]],
    )
    late = [send(m, value) for m, value in zip(groups[2], late)]
    second, pair = pack(
        [[(i, 0, depth) for i in range(len(middle))], [(len(middle), 0, 4 * have)]], *middle, pair
    )
    far_first = exchange(first, ("rep",), 1)
    third, = pack([[(i, 0, depth) for i in range(count_late)]], *late, far_first)
    gathered = [pair, exchange(pair, ("loop",), 1)]
    batches = [first, far_first]
    for batch in (second, third):
        batches += [batch, exchange(batch, ("rep",), 1)]

    shards_of = [(2 * m) ^ c for group in groups for _ in range(2) for m in group for c in range(2)]
    planes = [p for group in groups for p in range(2) for _ in group for _ in range(2)]
    hits = (jnp.array(shards_of, jnp.int32) ^ me) * reps + (jnp.array(planes, jnp.int32) ^ rep)
    spread = hits[:, None] == jnp.arange(owners, dtype=jnp.int32)[None, :]
    taken = jnp.sum(jnp.where(spread, hard_counts, 0), axis=1)
    live = (jnp.arange(slots, dtype=jnp.int32)[None, :] < taken[:, None])
    live = live.astype(jnp.int32).reshape(1, -1)

    owner = jnp.array(orders, jnp.int32) ^ me
    ids = (owner[:, None] * block + jnp.arange(block, dtype=jnp.int32)[None, :]).reshape(1, -1)

    rest = loop // 4
    rows = loop * block
    hard_count = owners * slots
    table = gathered + batches
    pass_all = jax.ShapeDtypeStruct((rows, width), jnp.bfloat16)
    hard_all = jax.ShapeDtypeStruct((hard_count, width), jnp.bfloat16)
    payload = jax.ShapeDtypeStruct((rows // 2, width + 2 * LOSS), jnp.float32)
    weights, hard_weights, send = pl.pallas_call(
        functools.partial(score_kernel, len(table)),
        out_shape=[
            jax.ShapeDtypeStruct((count, rows), jnp.bfloat16),
            jax.ShapeDtypeStruct((count, hard_count), jnp.bfloat16),
            jax.ShapeDtypeStruct((rows // 2, width + 2 * LOSS), jnp.float32),
        ],
        in_specs=[SCALARS] + [WHOLE] * (4 + len(table)),
        out_specs=[WHOLE] * 3,
        scratch_shapes=[pltpu.VMEM(a.shape, a.dtype) for a in (pass_all, hard_all)],
        compiler_params=budget(queries, pass_all, pass_all, hard_all, hard_all, payload),
        cost_estimate=pl.CostEstimate(
            flops=2 * count * (rows + hard_count + rows // 2) * width,
            bytes_accessed=2 * (count + rows + hard_count) * width + 2 * rows * width,
            transcendentals=2 * count * (rows + hard_count),
        ),
    )(meta, queries, positive.reshape(count, 1), ids, live, *table)

    sent = exchange(send, ("loop",), 1)
    kept = pl.pallas_call(
        keep_kernel,
        out_shape=jax.ShapeDtypeStruct((rows // 2, width + 2 * LOSS), jnp.float32),
        in_specs=[SCALARS] + [WHOLE] * 3,
        out_specs=WHOLE,
        compiler_params=budget(queries, payload, payload),
        cost_estimate=pl.CostEstimate(
            flops=count * rows * width,
            bytes_accessed=2 * count * width + 2 * rows * width, transcendentals=0,
        ),
    )(meta, weights, queries, send)
    query_grad, done = pl.pallas_call(
        functools.partial(grad_kernel, len(table)),
        out_shape=[
            jax.ShapeDtypeStruct((count, width), jnp.float32),
            jax.ShapeDtypeStruct((8, 128), jnp.float32),
        ],
        in_specs=[WHOLE] * (2 + len(table)),
        out_specs=[WHOLE] * 2,
        scratch_shapes=[pltpu.VMEM(a.shape, a.dtype) for a in (pass_all, hard_all)],
        compiler_params=budget(queries, queries, pass_all, pass_all, hard_all, hard_all),
        cost_estimate=pl.CostEstimate(
            flops=2 * count * (rows + hard_count) * width,
            bytes_accessed=2 * (rows + hard_count) * width + 4 * count * width,
            transcendentals=0,
        ),
    )(weights, hard_weights, *table)
    part = half + LOSS
    quarter = rows // 4
    first = jax.ShapeDtypeStruct((quarter, part), jnp.float32)
    short = jax.ShapeDtypeStruct(first.shape, jnp.bfloat16)
    own, *going = pl.pallas_call(
        first_sum,
        out_shape=[first, short, first, short],
        in_specs=[WHOLE] * 2,
        out_specs=[WHOLE] * 4,
        compiler_params=budget(payload, payload, payload),
        cost_estimate=pl.CostEstimate(
            flops=payload.size, bytes_accessed=12 * payload.size, transcendentals=0
        ),
    )(kept, sent)
    came = [exchange(value, both, mask) for value, mask in zip(going, (4, 1, 5))]
    second = jax.ShapeDtypeStruct((block, part), jnp.float32)
    total, *going = pl.pallas_call(
        second_sum,
        out_shape=[second] * rest,
        in_specs=[WHOLE] * 5,
        out_specs=[WHOLE] * rest,
        compiler_params=budget(payload, payload),
        cost_estimate=pl.CostEstimate(
            flops=4 * first.size, bytes_accessed=20 * first.size, transcendentals=0
        ),
    )(own, *came, done)
    for value, order in zip(going, orders[1:rest]):
        total = total + exchange(value, ("loop",), order)
    mean_loss = (total[0, half] + total[0, half + LOSS // 2]) / (count * loop * reps)
    total = total[:, :half]
    opposite = exchange(total, ("rep",), 1)
    passage_grad = jnp.where(
        rep == 0,
        jnp.concatenate([total, opposite], axis=1),
        jnp.concatenate([opposite, total], axis=1),
    )

    return (query_grad, passage_grad, mean_loss)


def solution(mesh):
    placed = (
        P(("loop", "rep"), None),
        P("loop", None),
        P(("loop", "rep"), None),
        P(("loop", "rep")),
        P("loop", None, None),
        P("loop", None),
    )
    return jax.shard_map(
        shards,
        mesh=mesh,
        in_specs=placed,
        out_specs=(P(("loop", "rep"), None), P("loop", None), P()),
        check_vma=False,
    )
```

```python
import functools

import jax
import jax.numpy as jnp
from jax import lax
from jax.experimental import pallas as pl
from jax.experimental.pallas import tpu as pltpu
from jax.sharding import PartitionSpec as P


def budget(*arrays):
    total = sum(a.size * a.dtype.itemsize for a in arrays)
    return pltpu.CompilerParams(vmem_limit_bytes=total + total // 4 + 6 * 1024 * 1024)


WHOLE = pl.BlockSpec(memory_space=pltpu.VMEM)
SCALARS = pl.BlockSpec(memory_space=pltpu.SMEM)
LOSS = 128


def exchange(value, axes, mask):
    size = 1
    for axis in axes:
        size *= lax.axis_size(axis)
    return lax.ppermute(value, axes, [(i, i ^ mask) for i in range(size)])


def ask_kernel(wanted, asked):
    owners = wanted.shape[2]
    asked[...] = jnp.zeros(asked.shape, asked.dtype)
    asked[:, :, :owners] = jnp.broadcast_to(wanted[...], asked.shape[:2] + (owners,))


def pick_rows(meta, asked, other, own, known, more, ahead, *pieces):
    me, rep = meta[0], meta[1]
    slots, owners = asked.shape[1:]
    lanes = lax.broadcasted_iota(jnp.int32, (slots, owners), 1)
    rows = lax.broadcasted_iota(jnp.int32, (slots, own.shape[0]), 1)

    def hot(owner):
        picked = []
        for m in range(len(pieces)):
            tile = asked[me ^ (2 * m)]
            column = jnp.sum(jnp.where(lanes == owner, tile, 0), axis=1, keepdims=True)
            picked.append(jnp.where(column == rows, 1.0, 0.0))
        return jnp.concatenate(picked, axis=0).astype(jnp.bfloat16)

    hot_own = hot(me * 2 + rep)
    hot_other = hot((me ^ 1) * 2 + rep)
    have = known.shape[0]
    ahead[2 * slots:2 * slots + have, :] = known[...]
    ahead[2 * slots + have:, :] = more[...]
    got_other = jnp.dot(hot_other, other[...], preferred_element_type=jnp.float32)
    got_own = jnp.dot(hot_own, own[...], preferred_element_type=jnp.float32)
    for m, piece in enumerate(pieces):
        part = slice(m * slots, (m + 1) * slots)
        value = jnp.concatenate([got_own[part], got_other[part]], axis=0).astype(jnp.bfloat16)
        piece[...] = value
        if m == 1:
            ahead[:2 * slots, :] = value


def pack_kernel(layouts, *refs):
    ins, outs = refs[:-len(layouts)], refs[-len(layouts):]
    for layout, out in zip(layouts, outs):
        at = 0
        for which, first, rows in layout:
            out[at:at + rows, :] = ins[which][first:first + rows, :]
            at += rows


def pack(layouts, *arrays):
    shapes = [
        jax.ShapeDtypeStruct((sum(rows for _, _, rows in layout), arrays[0].shape[1]), arrays[0].dtype)
        for layout in layouts
    ]
    size = sum(shape.size for shape in shapes)
    return pl.pallas_call(
        functools.partial(pack_kernel, layouts),
        out_shape=shapes,
        in_specs=[WHOLE] * len(arrays),
        out_specs=[WHOLE] * len(layouts),
        compiler_params=budget(*shapes, *arrays),
        cost_estimate=pl.CostEstimate(flops=size, bytes_accessed=4 * size, transcendentals=0),
    )(*arrays)


def stack(refs, out):
    at = 0
    for ref in refs:
        out[at:at + ref.shape[0], :] = ref[...]
        at += ref.shape[0]


def scored(queries, refs, rows):
    stack(refs, rows)
    return 50.0 * lax.dot_general(
        queries[...], rows[...], (((1,), (1,)), ((), ())), preferred_element_type=jnp.float32
    )


def early_kernel(queries, *refs):
    *batches, scores_out, hard_out, passages, hard = refs
    scores_out[...] = scored(queries, batches[:2], passages)
    hard_out[...] = scored(queries, batches[2:-1], hard)


def score_kernel(meta, queries, positive, ids, live_1, live_2, scores_ref, hard_ref, *refs):
    *batches, weights_out, hard_1_out, hard_2_out, send_out, hard = refs
    scores = scores_ref[...]
    hard_1 = jnp.where(live_1[...] > 0, hard_ref[...], -jnp.inf)
    hard_2 = jnp.where(live_2[...] > 0, scored(queries, batches, hard), -jnp.inf)
    row_top = jnp.max(scores, axis=1, keepdims=True)
    for value in (hard_1, hard_2):
        row_top = jnp.maximum(row_top, jnp.max(value, axis=1, keepdims=True))
    sums = [
        jnp.sum(jnp.exp(value - row_top), axis=1, keepdims=True)
        for value in (scores, hard_1, hard_2)
    ]
    log_total = row_top + jnp.log(sums[0] + (sums[1] + sums[2]))
    onehot = jnp.where(positive[...] == ids[...], 1.0, 0.0)
    weights = (jnp.exp(scores - log_total) - onehot).astype(jnp.bfloat16)
    loss = jnp.sum(log_total - jnp.sum(scores * onehot, axis=1, keepdims=True))
    rows = weights.shape[1] // 2
    project(send_out, weights[:, rows:], queries, meta[1], loss)
    weights_out[...] = weights
    hard_1_out[...] = jnp.exp(hard_1 - log_total).astype(jnp.bfloat16)
    hard_2_out[...] = jnp.exp(hard_2 - log_total).astype(jnp.bfloat16)


def project(out, weights, queries, rep, loss):
    half = queries.shape[1] // 2
    for i, side in enumerate((rep, 1 - rep)):
        product = lax.dot_general(
            weights, queries[:, pl.ds(pl.multiple_of(side * half, half), half)],
            (((0,), (0,)), ((), ())), preferred_element_type=jnp.float32,
        )
        at = i * (half + LOSS)
        out[:, at:at + half] = 50.0 * product
        out[:, at + half:at + half + LOSS] = jnp.full((out.shape[0], LOSS), loss, jnp.float32)


def keep_kernel(meta, weights, queries, send, out):
    rows = out.shape[0]
    half = queries.shape[1] // 2
    loss = send[0:1, half:half + 1]
    project(out, weights[:, :rows], queries, meta[1], loss)


def first_sum(kept, sent, own, to_x, to_y, to_xy):
    rows, columns = own.shape
    half = columns - LOSS
    lanes = lax.broadcasted_iota(jnp.int32, (rows, LOSS), 1)
    for out, down, across in ((own, 0, 0), (to_x, 1, 0), (to_y, 0, 1), (to_xy, 1, 1)):
        at = pl.ds(down * rows, rows)
        data = pl.ds(across * columns, half)
        out[:, :half] = (kept[at, data] + sent[at, data]).astype(out.dtype)
        tile = pl.ds(across * columns + half, LOSS)
        loss = kept[at, tile] + sent[at, tile]
        high = loss.astype(jnp.bfloat16).astype(jnp.float32)
        out[:, half:] = jnp.where(lanes < LOSS // 2, high, loss - high).astype(out.dtype)


def second_sum(own, from_x, from_y, from_xy, after, *outs):
    rows = outs[0].shape[0]
    for i, out in enumerate(outs):
        at = pl.ds(i * rows, rows)
        out[...] = (own[at] + from_x[at].astype(jnp.float32)) + (
            from_y[at].astype(jnp.float32) + from_xy[at].astype(jnp.float32)
        )


def grad_kernel(weights, hard_1, hard_2, *refs):
    *batches, out, done, gathered, hard = refs
    done[...] = jnp.zeros(done.shape, done.dtype)
    split = hard_1.shape[1]
    stack(batches[:2], gathered)
    stack(batches[2:], hard)
    out[...] = 50.0 * (
        jnp.dot(weights[...], gathered[...], preferred_element_type=jnp.float32)
        + jnp.dot(hard_1[...], hard[:split, :], preferred_element_type=jnp.float32)
        + jnp.dot(hard_2[...], hard[split:, :], preferred_element_type=jnp.float32)
    )


def shards(queries, passages, index_rows, positive, hard_rows, hard_counts):
    loop = lax.axis_size("loop")
    reps = lax.axis_size("rep")
    me = lax.axis_index("loop").astype(jnp.int32)
    rep = lax.axis_index("rep").astype(jnp.int32)
    count, width = queries.shape
    block = passages.shape[0]
    owners, slots = hard_rows.shape[1:]
    half = width // 2
    chips = loop // 2
    meta = jnp.stack([me, rep])
    both = ("loop", "rep")

    other_rows = exchange(index_rows, ("loop",), 1)
    request = jax.ShapeDtypeStruct((loop, slots, owners + -owners % 128), jnp.int32)
    request = pl.pallas_call(
        ask_kernel,
        out_shape=request,
        in_specs=[WHOLE],
        out_specs=WHOLE,
        compiler_params=budget(request),
        cost_estimate=pl.CostEstimate(
            flops=request.size, bytes_accessed=8 * request.size, transcendentals=0
        ),
    )(jnp.transpose(hard_rows, (0, 2, 1)))
    asked = lax.all_to_all(request, "loop", split_axis=0, concat_axis=0, tiled=True)

    bits = [loop // 2 >> i for i in range(loop.bit_length() - 4)] + [4, 2, 1]
    orders = [0]
    for bit in bits:
        orders = orders + [o | bit for o in orders]
    known = passages
    for i, bit in enumerate(bits[:-3]):
        got = exchange(known, ("loop",), bit)
        known, = pack([[(0, 0, got.shape[0]), (1, 0, got.shape[0])]], known, got, index_rows)
    more = exchange(known, ("loop",), bits[-3])

    depth = 2 * slots
    have = known.shape[0]
    pieces = [jax.ShapeDtypeStruct((depth, width), jnp.bfloat16)] * chips
    ahead = jax.ShapeDtypeStruct((depth + 2 * have, width), jnp.bfloat16)
    ahead, *sends = pl.pallas_call(
        pick_rows,
        out_shape=[ahead] + pieces,
        in_specs=[SCALARS] + [WHOLE] * 5,
        out_specs=[WHOLE] * (1 + chips),
        compiler_params=budget(index_rows, index_rows, ahead, *pieces, *pieces),
        cost_estimate=pl.CostEstimate(
            flops=4 * chips * slots * index_rows.shape[0] * width,
            bytes_accessed=3 * index_rows.size * 2, transcendentals=0,
        ),
    )(meta, asked, other_rows, index_rows, known, more)

    def send(m, value):
        return exchange(value, ("loop",), 2 * m)

    def whole(count, first=0):
        return [(first + i, 0, depth) for i in range(count)]

    top = chips // 2
    groups = (
        range(1), range(1, top), range(top, top + top // 2), range(top + top // 2, chips)
    )
    batches = [sends[0], exchange(sends[0], ("rep",), 1)]
    inner = [send(1, ahead)] + [send(m, sends[m]) for m in groups[1][1:]]
    middle = [send(m, sends[m]) for m in groups[2]]
    near, last = len(inner), len(groups[3])
    batch, pair, *late = pack(
        [whole(near), [(near, 0, have), (near + 1, 0, have), (0, depth, 2 * have)]]
        + [whole(1, near + 2 + i) for i in range(last)],
        *inner, known, more, *[sends[m] for m in groups[3]], batches[1],
    )
    batches += [batch, exchange(batch, ("rep",), 1)]
    late = [send(m, value) for m, value in zip(groups[3], late)]
    passed = [exchange(value, ("rep",), 1) for value in middle]
    batch, pair = pack(
        [whole(last), [(last, 0, 4 * have)]], *late, pair, batches[3], *passed
    )
    gathered = [pair, exchange(pair, ("loop",), 1)]
    early, late = batches, middle + passed + [batch, exchange(batch, ("rep",), 1)]

    order = [(m, p) for group in groups for p in range(2) for m in group]
    shards_of = [(2 * m) ^ c for m, _ in order for c in range(2)]
    planes = [p for _, p in order for _ in range(2)]
    hits = (jnp.array(shards_of, jnp.int32) ^ me) * reps + (jnp.array(planes, jnp.int32) ^ rep)
    spread = hits[:, None] == jnp.arange(owners, dtype=jnp.int32)[None, :]
    taken = jnp.sum(jnp.where(spread, hard_counts, 0), axis=1)
    live = (jnp.arange(slots, dtype=jnp.int32)[None, :] < taken[:, None])
    live = live.astype(jnp.int32).reshape(1, -1)
    split = 2 * depth * top
    live_1, live_2 = live[:, :split], live[:, split:]

    owner = jnp.array(orders, jnp.int32) ^ me
    ids = (owner[:, None] * block + jnp.arange(block, dtype=jnp.int32)[None, :]).reshape(1, -1)

    rest = loop // 4
    rows = loop * block
    hard_count = owners * slots
    table = gathered + early + late
    pass_all = jax.ShapeDtypeStruct((rows, width), jnp.bfloat16)
    hard_all = jax.ShapeDtypeStruct((hard_count, width), jnp.bfloat16)
    payload = jax.ShapeDtypeStruct((rows // 2, width + 2 * LOSS), jnp.float32)
    hard_1 = jax.ShapeDtypeStruct((split, width), jnp.bfloat16)
    hard_2 = jax.ShapeDtypeStruct((hard_count - split, width), jnp.bfloat16)
    scores, hard_scores = pl.pallas_call(
        early_kernel,
        out_shape=[
            jax.ShapeDtypeStruct((count, rows), jnp.float32),
            jax.ShapeDtypeStruct((count, split), jnp.float32),
        ],
        in_specs=[WHOLE] * (4 + len(early)),
        out_specs=[WHOLE] * 2,
        scratch_shapes=[pltpu.VMEM(a.shape, a.dtype) for a in (pass_all, hard_1)],
        compiler_params=budget(queries, pass_all, pass_all, hard_1, hard_1),
        cost_estimate=pl.CostEstimate(
            flops=2 * count * (rows + split) * width,
            bytes_accessed=2 * (count + rows + split) * width, transcendentals=0,
        ),
    )(queries, *gathered, *early, late[-1])
    weights, weights_1, weights_2, send = pl.pallas_call(
        score_kernel,
        out_shape=[
            jax.ShapeDtypeStruct((count, rows), jnp.bfloat16),
            jax.ShapeDtypeStruct((count, split), jnp.bfloat16),
            jax.ShapeDtypeStruct((count, hard_count - split), jnp.bfloat16),
            payload,
        ],
        in_specs=[SCALARS] + [WHOLE] * (7 + len(late)),
        out_specs=[WHOLE] * 4,
        scratch_shapes=[pltpu.VMEM(hard_2.shape, hard_2.dtype)],
        compiler_params=budget(queries, hard_2, hard_2, payload),
        cost_estimate=pl.CostEstimate(
            flops=2 * count * (hard_count - split + rows // 2) * width,
            bytes_accessed=2 * (count + hard_count - split) * width + 2 * rows * width,
            transcendentals=2 * count * (rows + hard_count),
        ),
    )(
        meta, queries, positive.reshape(count, 1), ids, live_1, live_2,
        scores, hard_scores, *late,
    )

    sent = exchange(send, ("loop",), 1)
    kept = pl.pallas_call(
        keep_kernel,
        out_shape=jax.ShapeDtypeStruct((rows // 2, width + 2 * LOSS), jnp.float32),
        in_specs=[SCALARS] + [WHOLE] * 3,
        out_specs=WHOLE,
        compiler_params=budget(queries, payload, payload),
        cost_estimate=pl.CostEstimate(
            flops=count * rows * width,
            bytes_accessed=2 * count * width + 2 * rows * width, transcendentals=0,
        ),
    )(meta, weights, queries, send)
    query_grad, done = pl.pallas_call(
        grad_kernel,
        out_shape=[
            jax.ShapeDtypeStruct((count, width), jnp.float32),
            jax.ShapeDtypeStruct((8, 128), jnp.float32),
        ],
        in_specs=[WHOLE] * (3 + len(table)),
        out_specs=[WHOLE] * 2,
        scratch_shapes=[pltpu.VMEM(a.shape, a.dtype) for a in (pass_all, hard_all)],
        compiler_params=budget(queries, queries, pass_all, pass_all, hard_all, hard_all),
        cost_estimate=pl.CostEstimate(
            flops=2 * count * (rows + hard_count) * width,
            bytes_accessed=2 * (rows + hard_count) * width + 4 * count * width,
            transcendentals=0,
        ),
    )(weights, weights_1, weights_2, *table)
    part = half + LOSS
    quarter = rows // 4
    first = jax.ShapeDtypeStruct((quarter, part), jnp.float32)
    short = jax.ShapeDtypeStruct(first.shape, jnp.bfloat16)
    own, *going = pl.pallas_call(
        first_sum,
        out_shape=[first, short, first, short],
        in_specs=[WHOLE] * 2,
        out_specs=[WHOLE] * 4,
        compiler_params=budget(payload, payload, payload),
        cost_estimate=pl.CostEstimate(
            flops=payload.size, bytes_accessed=12 * payload.size, transcendentals=0
        ),
    )(kept, sent)
    came = [exchange(value, both, mask) for value, mask in zip(going, (4, 1, 5))]
    second = jax.ShapeDtypeStruct((block, part), jnp.float32)
    total, *going = pl.pallas_call(
        second_sum,
        out_shape=[second] * rest,
        in_specs=[WHOLE] * 5,
        out_specs=[WHOLE] * rest,
        compiler_params=budget(payload, payload),
        cost_estimate=pl.CostEstimate(
            flops=4 * first.size, bytes_accessed=20 * first.size, transcendentals=0
        ),
    )(own, *came, done)
    for value, order in zip(going, orders[1:rest]):
        total = total + exchange(value, ("loop",), order)
    mean_loss = (total[0, half] + total[0, half + LOSS // 2]) / (count * loop * reps)
    total = total[:, :half]
    opposite = exchange(total, ("rep",), 1)
    passage_grad = jnp.where(
        rep == 0,
        jnp.concatenate([total, opposite], axis=1),
        jnp.concatenate([opposite, total], axis=1),
    )

    return (query_grad, passage_grad, mean_loss)


def solution(mesh):
    placed = (
        P(("loop", "rep"), None),
        P("loop", None),
        P(("loop", "rep"), None),
        P(("loop", "rep")),
        P("loop", None, None),
        P("loop", None),
    )
    return jax.shard_map(
        shards,
        mesh=mesh,
        in_specs=placed,
        out_specs=(P(("loop", "rep"), None), P("loop", None), P()),
        check_vma=False,
    )
```

```python
import functools

import jax
import jax.numpy as jnp
from jax import lax
from jax.experimental import pallas as pl
from jax.experimental.pallas import tpu as pltpu
from jax.sharding import PartitionSpec as P


def budget(*arrays):
    total = sum(a.size * a.dtype.itemsize for a in arrays)
    return pltpu.CompilerParams(vmem_limit_bytes=total + total // 4 + 6 * 1024 * 1024)


WHOLE = pl.BlockSpec(memory_space=pltpu.VMEM)
SCALARS = pl.BlockSpec(memory_space=pltpu.SMEM)
LOSS = 128


def exchange(value, axes, mask):
    size = 1
    for axis in axes:
        size *= lax.axis_size(axis)
    return lax.ppermute(value, axes, [(i, i ^ mask) for i in range(size)])


def ask_kernel(wanted, asked):
    owners = wanted.shape[2]
    asked[...] = jnp.zeros(asked.shape, asked.dtype)
    asked[:, :, :owners] = jnp.broadcast_to(wanted[...], asked.shape[:2] + (owners,))


def pick_rows(count, meta, asked, other, own, after, plane, *pieces):
    me, rep = meta[0], meta[1]
    slots, owners = asked.shape[1:]
    lanes = lax.broadcasted_iota(jnp.int32, (slots, owners), 1)
    rows = lax.broadcasted_iota(jnp.int32, (slots, own.shape[0]), 1)

    def hot(owner):
        picked = []
        for m in range(count + len(pieces)):
            tile = asked[me ^ (2 * m)]
            column = jnp.sum(jnp.where(lanes == owner, tile, 0), axis=1, keepdims=True)
            picked.append(jnp.where(column == rows, 1.0, 0.0))
        return jnp.concatenate(picked, axis=0).astype(jnp.bfloat16)

    hot_own = hot(me * 2 + rep)
    hot_other = hot((me ^ 1) * 2 + rep)
    got_other = jnp.dot(hot_other, other[...], preferred_element_type=jnp.float32)
    got_own = jnp.dot(hot_own, own[...], preferred_element_type=jnp.float32)
    for m in range(count + len(pieces)):
        part = slice(m * slots, (m + 1) * slots)
        value = jnp.concatenate([got_own[part], got_other[part]], axis=0).astype(jnp.bfloat16)
        if m < count:
            plane[m * 2 * slots:(m + 1) * 2 * slots, :] = value
        else:
            pieces[m - count][...] = value


def pack_kernel(layouts, *refs):
    ins, outs = refs[:-len(layouts)], refs[-len(layouts):]
    for layout, out in zip(layouts, outs):
        at = 0
        for which, first, rows in layout:
            out[at:at + rows, :] = ins[which][first:first + rows, :]
            at += rows


def pack(layouts, *arrays):
    shapes = [
        jax.ShapeDtypeStruct((sum(rows for _, _, rows in layout), arrays[0].shape[1]), arrays[0].dtype)
        for layout in layouts
    ]
    size = sum(shape.size for shape in shapes)
    return pl.pallas_call(
        functools.partial(pack_kernel, layouts),
        out_shape=shapes,
        in_specs=[WHOLE] * len(arrays),
        out_specs=[WHOLE] * len(layouts),
        compiler_params=budget(*shapes, *arrays),
        cost_estimate=pl.CostEstimate(flops=size, bytes_accessed=4 * size, transcendentals=0),
    )(*arrays)


def stack(counts, refs, out):
    at = 0
    for rows, ref in zip(counts, refs):
        out[at:at + rows, :] = ref[:rows, :]
        at += rows


def scored(queries, rows):
    return 50.0 * lax.dot_general(
        queries[...], rows[...], (((1,), (1,)), ((), ())), preferred_element_type=jnp.float32
    )


def early_kernel(counts, queries, passages, *refs):
    *batches, scores_out, hard_out, hard = refs
    scores_out[...] = scored(queries, passages)
    stack(counts, batches, hard)
    hard_out[...] = scored(queries, hard)


def score_kernel(
    counts, meta, queries, positive, ids_1, ids_2, live_1, live_2, scores_ref, hard_ref, passages, *refs
):
    *batches, out_1, out_2, hard_1_out, hard_2_out, send_out, hard = refs
    stack(counts, batches, hard)
    scores_1 = scores_ref[...]
    scores_2 = scored(queries, passages)
    hard_1 = jnp.where(live_1[...] > 0, hard_ref[...], -jnp.inf)
    hard_2 = jnp.where(live_2[...] > 0, scored(queries, hard), -jnp.inf)
    parts = (scores_1, scores_2, hard_1, hard_2)
    tops = [jnp.max(value, axis=1, keepdims=True) for value in parts]
    row_top = jnp.maximum(jnp.maximum(tops[0], tops[1]), jnp.maximum(tops[2], tops[3]))
    sums = [jnp.sum(jnp.exp(value - row_top), axis=1, keepdims=True) for value in parts]
    log_total = row_top + jnp.log((sums[0] + sums[1]) + (sums[2] + sums[3]))
    wanted = 0.0
    weights = []
    for scores, ids in ((scores_1, ids_1), (scores_2, ids_2)):
        onehot = jnp.where(positive[...] == ids[...], 1.0, 0.0)
        weights.append((jnp.exp(scores - log_total) - onehot).astype(jnp.bfloat16))
        wanted = wanted + jnp.sum(scores * onehot, axis=1, keepdims=True)
    project(send_out, weights[1], queries, meta[1], jnp.sum(log_total - wanted))
    out_1[...] = weights[0]
    out_2[...] = weights[1]
    hard_1_out[...] = jnp.exp(hard_1 - log_total).astype(jnp.bfloat16)
    hard_2_out[...] = jnp.exp(hard_2 - log_total).astype(jnp.bfloat16)


def project(out, weights, queries, rep, loss):
    half = queries.shape[1] // 2
    for i, side in enumerate((rep, 1 - rep)):
        product = lax.dot_general(
            weights, queries[:, pl.ds(pl.multiple_of(side * half, half), half)],
            (((0,), (0,)), ((), ())), preferred_element_type=jnp.float32,
        )
        at = i * (half + LOSS)
        out[:, at:at + half] = 50.0 * product
        out[:, at + half:at + half + LOSS] = jnp.full((out.shape[0], LOSS), loss, jnp.float32)


def keep_kernel(meta, weights, queries, send, out):
    half = queries.shape[1] // 2
    project(out, weights[...], queries, meta[1], send[0:1, half:half + 1])


def first_sum(kept, sent, own, to_x, to_y, to_xy):
    rows, columns = own.shape
    half = columns - LOSS
    lanes = lax.broadcasted_iota(jnp.int32, (rows, LOSS), 1)
    for out, down, across in ((own, 0, 0), (to_x, 1, 0), (to_y, 0, 1), (to_xy, 1, 1)):
        at = pl.ds(down * rows, rows)
        data = pl.ds(across * columns, half)
        out[:, :half] = (kept[at, data] + sent[at, data]).astype(out.dtype)
        tile = pl.ds(across * columns + half, LOSS)
        loss = kept[at, tile] + sent[at, tile]
        high = loss.astype(jnp.bfloat16).astype(jnp.float32)
        out[:, half:] = jnp.where(lanes < LOSS // 2, high, loss - high).astype(out.dtype)


def second_sum(own, from_x, from_y, from_xy, after, *outs):
    rows = outs[0].shape[0]
    for i, out in enumerate(outs):
        at = pl.ds(i * rows, rows)
        out[...] = (own[at] + from_x[at].astype(jnp.float32)) + (
            from_y[at].astype(jnp.float32) + from_xy[at].astype(jnp.float32)
        )


def grad_kernel(
    counts, weights_1, weights_2, hard_1, hard_2, passages_1, passages_2, *refs
):
    *batches, out, done, hard = refs
    done[...] = jnp.zeros(done.shape, done.dtype)
    stack(counts, batches, hard)
    split = hard_1.shape[1]
    total = jnp.dot(hard_1[...], hard[:split, :], preferred_element_type=jnp.float32)
    for weights, rows in (
        (hard_2, hard[split:, :]), (weights_1, passages_1[...]), (weights_2, passages_2[...])
    ):
        total += jnp.dot(weights[...], rows, preferred_element_type=jnp.float32)
    out[...] = 50.0 * total


def shards(queries, passages, index_rows, positive, hard_rows, hard_counts):
    loop = lax.axis_size("loop")
    reps = lax.axis_size("rep")
    me = lax.axis_index("loop").astype(jnp.int32)
    rep = lax.axis_index("rep").astype(jnp.int32)
    count, width = queries.shape
    block = passages.shape[0]
    owners, slots = hard_rows.shape[1:]
    half = width // 2
    chips = loop // 2
    meta = jnp.stack([me, rep])
    both = ("loop", "rep")

    other_rows = exchange(index_rows, ("loop",), 1)
    request = jax.ShapeDtypeStruct((loop, slots, owners + -owners % 128), jnp.int32)
    request = pl.pallas_call(
        ask_kernel,
        out_shape=request,
        in_specs=[WHOLE],
        out_specs=WHOLE,
        compiler_params=budget(request),
        cost_estimate=pl.CostEstimate(
            flops=request.size, bytes_accessed=8 * request.size, transcendentals=0
        ),
    )(jnp.transpose(hard_rows, (0, 2, 1)))
    asked = lax.all_to_all(request, "loop", split_axis=0, concat_axis=0, tiled=True)

    bits = [loop // 2 >> i for i in range(loop.bit_length() - 4)] + [4, 2, 1]
    orders = [0]
    for bit in bits:
        orders = orders + [o | bit for o in orders]
    known = passages
    for i, bit in enumerate(bits[:-3]):
        got = exchange(known, ("loop",), bit)
        known, = pack([[(0, 0, got.shape[0]), (1, 0, got.shape[0])]], known, got, index_rows)

    depth = 2 * slots
    have = known.shape[0]
    top = chips // 2
    outs = [jax.ShapeDtypeStruct((top * depth, width), jnp.bfloat16)]
    outs += [jax.ShapeDtypeStruct((depth, width), jnp.bfloat16)] * top
    plane, *sends = pl.pallas_call(
        functools.partial(pick_rows, top),
        out_shape=outs,
        in_specs=[SCALARS] + [WHOLE] * 4,
        out_specs=[WHOLE] * (1 + top),
        compiler_params=budget(index_rows, index_rows, *outs, *outs),
        cost_estimate=pl.CostEstimate(
            flops=4 * chips * slots * index_rows.shape[0] * width,
            bytes_accessed=3 * index_rows.size * 2, transcendentals=0,
        ),
    )(meta, asked, other_rows, index_rows, known)

    def send(m, value):
        return exchange(value, ("loop",), 2 * m)

    def over(value):
        return exchange(value, ("rep",), 1)

    def cut(arrays, *pieces):
        return [
            (next(i for i, a in enumerate(arrays) if a is array), first, rows)
            for array, first, rows in pieces
        ]

    half_top = top // 2
    inner, outer = range(1, half_top + 1), range(half_top + 1, top)
    opposite_plane = over(plane)
    middle = [send(top + i, sends[i]) for i in range(half_top)]
    more = exchange(known, ("loop",), 4)

    arrays = [plane, opposite_plane, known, more, *middle, *sends[half_top:]]
    quad = [(known, 0, have), (more, 0, have)]
    batch, *going = pack(
        [cut(arrays, *[(value, 0, depth) for value in middle])]
        + [
            cut(arrays, (plane, m * depth, depth), (opposite_plane, m * depth, depth),
                *(quad if m == 1 else []))
            for m in inner
        ]
        + [cut(arrays, (value, 0, depth)) for value in sends[half_top:]],
        *arrays,
    )
    near_batch, far_batch = batch, over(batch)
    came = [send(m, value) for m, value in zip(inner, going)]
    late = [
        send(top + half_top + i, value) for i, value in enumerate(going[len(inner):])
    ]

    arrays = [plane, opposite_plane, known, more, *late, *came]
    batch, pair, *going = pack(
        [cut(arrays, *[(value, 0, depth) for value in late]),
         cut(arrays, *quad, (came[0], 2 * depth, 2 * have))]
        + [
            cut(arrays, (plane, m * depth, depth), (opposite_plane, m * depth, depth))
            for m in outer
        ],
        *arrays, far_batch,
    )
    last = [send(m, value) for m, value in zip(outer, going)] + [over(batch)]
    other_pair = exchange(pair, ("loop",), 1)

    first_rows = [(plane, depth), (opposite_plane, depth)]
    first_rows += [(value, 2 * depth) for value in came]
    first_rows += [(value, value.shape[0]) for value in (near_batch, far_batch, batch)]
    last_rows = [(value, value.shape[0]) for value in last]
    middle_masks = range(top, top + half_top)
    late_masks = range(top + half_top, chips)
    order = [(m, p) for m in (0, *inner) for p in range(2)]
    order += [(m, p) for p in range(2) for m in middle_masks] + [(m, 0) for m in late_masks]
    split = len(order) * depth
    order += [(m, p) for m in outer for p in range(2)] + [(m, 1) for m in late_masks]

    shards_of = [(2 * m) ^ c for m, _ in order for c in range(2)]
    planes = [p for _, p in order for _ in range(2)]
    hits = (jnp.array(shards_of, jnp.int32) ^ me) * reps + (jnp.array(planes, jnp.int32) ^ rep)
    spread = hits[:, None] == jnp.arange(owners, dtype=jnp.int32)[None, :]
    taken = jnp.sum(jnp.where(spread, hard_counts, 0), axis=1)
    live = (jnp.arange(slots, dtype=jnp.int32)[None, :] < taken[:, None])
    live = live.astype(jnp.int32).reshape(1, -1)
    live_1, live_2 = live[:, :split], live[:, split:]

    owner = jnp.array(orders, jnp.int32) ^ me
    ids = (owner[:, None] * block + jnp.arange(block, dtype=jnp.int32)[None, :]).reshape(1, -1)

    rest = loop // 4
    rows = loop * block
    side = rows // 2
    hard_count = owners * slots
    hard_1 = jax.ShapeDtypeStruct((split, width), jnp.bfloat16)
    hard_2 = jax.ShapeDtypeStruct((hard_count - split, width), jnp.bfloat16)
    hard_all = jax.ShapeDtypeStruct((hard_count, width), jnp.bfloat16)
    payload = jax.ShapeDtypeStruct((side, width + 2 * LOSS), jnp.float32)
    first_counts = tuple(n for _, n in first_rows)
    last_counts = tuple(n for _, n in last_rows)
    scores, hard_scores = pl.pallas_call(
        functools.partial(early_kernel, first_counts),
        out_shape=[
            jax.ShapeDtypeStruct((count, side), jnp.float32),
            jax.ShapeDtypeStruct((count, split), jnp.float32),
        ],
        in_specs=[WHOLE] * (2 + len(first_rows)),
        out_specs=[WHOLE] * 2,
        scratch_shapes=[pltpu.VMEM(hard_1.shape, hard_1.dtype)],
        compiler_params=budget(queries, pair, hard_1, hard_1),
        cost_estimate=pl.CostEstimate(
            flops=2 * count * (side + split) * width,
            bytes_accessed=2 * (count + side + split) * width, transcendentals=0,
        ),
    )(queries, pair, *[value for value, _ in first_rows])
    weights_1, weights_2, hard_w1, hard_w2, send_part = pl.pallas_call(
        functools.partial(score_kernel, last_counts),
        out_shape=[
            jax.ShapeDtypeStruct((count, side), jnp.bfloat16),
            jax.ShapeDtypeStruct((count, side), jnp.bfloat16),
            jax.ShapeDtypeStruct((count, split), jnp.bfloat16),
            jax.ShapeDtypeStruct((count, hard_count - split), jnp.bfloat16),
            payload,
        ],
        in_specs=[SCALARS] + [WHOLE] * (9 + len(last_rows)),
        out_specs=[WHOLE] * 5,
        scratch_shapes=[pltpu.VMEM(hard_2.shape, hard_2.dtype)],
        compiler_params=budget(queries, pair, hard_2, hard_2, payload),
        cost_estimate=pl.CostEstimate(
            flops=2 * count * (hard_count - split + rows) * width,
            bytes_accessed=2 * (count + hard_count - split) * width + 2 * rows * width,
            transcendentals=2 * count * (rows + hard_count),
        ),
    )(
        meta, queries, positive.reshape(count, 1), ids[:, :side], ids[:, side:],
        live_1, live_2, scores, hard_scores, other_pair, *[value for value, _ in last_rows],
    )

    sent = exchange(send_part, ("loop",), 1)
    kept = pl.pallas_call(
        keep_kernel,
        out_shape=jax.ShapeDtypeStruct((rows // 2, width + 2 * LOSS), jnp.float32),
        in_specs=[SCALARS] + [WHOLE] * 3,
        out_specs=WHOLE,
        compiler_params=budget(queries, payload, payload),
        cost_estimate=pl.CostEstimate(
            flops=count * rows * width,
            bytes_accessed=2 * count * width + 2 * rows * width, transcendentals=0,
        ),
    )(meta, weights_1, queries, send_part)
    query_grad, done = pl.pallas_call(
        functools.partial(grad_kernel, first_counts + last_counts),
        out_shape=[
            jax.ShapeDtypeStruct((count, width), jnp.float32),
            jax.ShapeDtypeStruct((8, 128), jnp.float32),
        ],
        in_specs=[WHOLE] * (6 + len(first_rows + last_rows)),
        out_specs=[WHOLE] * 2,
        scratch_shapes=[pltpu.VMEM(hard_all.shape, hard_all.dtype)],
        compiler_params=budget(queries, queries, pair, pair, hard_all, hard_all),
        cost_estimate=pl.CostEstimate(
            flops=2 * count * (rows + hard_count) * width,
            bytes_accessed=2 * (rows + hard_count) * width + 4 * count * width,
            transcendentals=0,
        ),
    )(
        weights_1, weights_2, hard_w1, hard_w2, pair, other_pair,
        *[value for value, _ in first_rows + last_rows],
    )
    part = half + LOSS
    quarter = rows // 4
    first = jax.ShapeDtypeStruct((quarter, part), jnp.float32)
    short = jax.ShapeDtypeStruct(first.shape, jnp.bfloat16)
    own, *going = pl.pallas_call(
        first_sum,
        out_shape=[first, short, first, short],
        in_specs=[WHOLE] * 2,
        out_specs=[WHOLE] * 4,
        compiler_params=budget(payload, payload, payload),
        cost_estimate=pl.CostEstimate(
            flops=payload.size, bytes_accessed=12 * payload.size, transcendentals=0
        ),
    )(kept, sent)
    came = [exchange(value, both, mask) for value, mask in zip(going, (4, 1, 5))]
    second = jax.ShapeDtypeStruct((block, part), jnp.float32)
    total, *going = pl.pallas_call(
        second_sum,
        out_shape=[second] * rest,
        in_specs=[WHOLE] * 5,
        out_specs=[WHOLE] * rest,
        compiler_params=budget(payload, payload),
        cost_estimate=pl.CostEstimate(
            flops=4 * first.size, bytes_accessed=20 * first.size, transcendentals=0
        ),
    )(own, *came, done)
    for value, order in zip(going, orders[1:rest]):
        total = total + exchange(value, ("loop",), order)
    mean_loss = (total[0, half] + total[0, half + LOSS // 2]) / (count * loop * reps)
    total = total[:, :half]
    opposite = exchange(total, ("rep",), 1)
    passage_grad = jnp.where(
        rep == 0,
        jnp.concatenate([total, opposite], axis=1),
        jnp.concatenate([opposite, total], axis=1),
    )

    return (query_grad, passage_grad, mean_loss)


def solution(mesh):
    placed = (
        P(("loop", "rep"), None),
        P("loop", None),
        P(("loop", "rep"), None),
        P(("loop", "rep")),
        P("loop", None, None),
        P("loop", None),
    )
    return jax.shard_map(
        shards,
        mesh=mesh,
        in_specs=placed,
        out_specs=(P(("loop", "rep"), None), P("loop", None), P()),
        check_vma=False,
    )
```

```python
import functools

import jax
import jax.numpy as jnp
from jax import lax
from jax.experimental import pallas as pl
from jax.experimental.pallas import tpu as pltpu
from jax.sharding import PartitionSpec as P


def budget(*arrays):
    total = sum(a.size * a.dtype.itemsize for a in arrays)
    return pltpu.CompilerParams(vmem_limit_bytes=total + total // 4 + 6 * 1024 * 1024)


WHOLE = pl.BlockSpec(memory_space=pltpu.VMEM)
SCALARS = pl.BlockSpec(memory_space=pltpu.SMEM)
LOSS = 128


def exchange(value, axes, mask):
    size = 1
    for axis in axes:
        size *= lax.axis_size(axis)
    return lax.ppermute(value, axes, [(i, i ^ mask) for i in range(size)])


def pick_rows(count, meta, asked, asked_x, other, own, passages, passages_z, known, plane, *pieces):
    me, rep = meta[0], meta[1]
    have = passages.shape[0]
    known[:have, :] = passages[...]
    known[have:, :] = passages_z[...]
    owners = asked.shape[1]
    slots = plane.shape[0] // (2 * count)
    lanes = lax.broadcasted_iota(jnp.int32, (slots, owners), 1)
    rows = lax.broadcasted_iota(jnp.int32, (slots, own.shape[0]), 1)

    def hot(owner):
        picked = []
        for m in range(count + len(pieces)):
            at = m // 2 * slots
            tile = (asked_x if m % 2 else asked)[at:at + slots, :]
            column = jnp.sum(jnp.where(lanes == owner, tile, 0), axis=1, keepdims=True)
            picked.append(jnp.where(column == rows, 1.0, 0.0))
        return jnp.concatenate(picked, axis=0).astype(jnp.bfloat16)

    hot_own = hot(me * 2 + rep)
    hot_other = hot((me ^ 1) * 2 + rep)
    got_other = jnp.dot(hot_other, other[...], preferred_element_type=jnp.float32)
    got_own = jnp.dot(hot_own, own[...], preferred_element_type=jnp.float32)
    for m in range(count + len(pieces)):
        part = slice(m * slots, (m + 1) * slots)
        value = jnp.concatenate([got_own[part], got_other[part]], axis=0).astype(jnp.bfloat16)
        if m < count:
            plane[m * 2 * slots:(m + 1) * 2 * slots, :] = value
        else:
            pieces[m - count][...] = value


def pack_kernel(layouts, *refs):
    ins, outs = refs[:-len(layouts)], refs[-len(layouts):]
    for layout, out in zip(layouts, outs):
        at = 0
        for which, first, rows in layout:
            out[at:at + rows, :] = ins[which][first:first + rows, :]
            at += rows


def pack(layouts, *arrays):
    shapes = [
        jax.ShapeDtypeStruct((sum(rows for _, _, rows in layout), arrays[0].shape[1]), arrays[0].dtype)
        for layout in layouts
    ]
    size = sum(shape.size for shape in shapes)
    return pl.pallas_call(
        functools.partial(pack_kernel, layouts),
        out_shape=shapes,
        in_specs=[WHOLE] * len(arrays),
        out_specs=[WHOLE] * len(layouts),
        compiler_params=budget(*shapes, *arrays),
        cost_estimate=pl.CostEstimate(flops=size, bytes_accessed=4 * size, transcendentals=0),
    )(*arrays)


def stack(counts, refs, out):
    at = 0
    for rows, ref in zip(counts, refs):
        out[at:at + rows, :] = ref[:rows, :]
        at += rows


def scored(queries, rows):
    return 50.0 * lax.dot_general(
        queries[...], rows[...], (((1,), (1,)), ((), ())), preferred_element_type=jnp.float32
    )


def early_kernel(counts, queries, *refs):
    *batches, scores_out, rows = refs
    stack(counts, batches, rows)
    scores_out[...] = scored(queries, rows)


def lookup(index, values):
    total = jnp.zeros_like(index)
    for i, value in enumerate(values):
        total = jnp.where(index == i, value, total)
    return total


def score_kernel(
    counts, columns, slots, meta, hard_counts, queries, positive, scores_ref, *refs
):
    *batches, out_1, out_2, rows, send_out = refs
    me, rep = meta[0], meta[1]
    stack(counts, batches, rows)
    side = send_out.shape[0]
    block = side // len(columns[0][0])
    blocks = [scores_ref[...], scored(queries, rows)]
    wanted = jnp.broadcast_to(positive[...].astype(jnp.float32), (8, positive.shape[1]))
    wanted = jnp.transpose(wanted)[:, :1]
    onehots = []
    for i, (order, places) in enumerate(columns):
        lane = lax.broadcasted_iota(jnp.int32, (1, blocks[i].shape[1]), 1)
        passage = lane < side
        ids = (lookup(lane // block, order) * block + lane % block) ^ (me * block)
        spot = jnp.where(passage, 0, lane - side)
        owner = lookup(spot // (2 * slots), [4 * m + p for m, p in places])
        owner = (owner + spot // slots % 2 * 2) ^ (me * 2 + rep)
        taken = lookup(owner, [hard_counts[0, o] for o in range(hard_counts.shape[1])])
        live = passage | (spot % slots < taken)
        onehots.append(
            jnp.where((wanted == ids.astype(jnp.float32)) & passage, 1.0, 0.0)
        )
        blocks[i] = jnp.where(live, blocks[i], -jnp.inf)
    tops = [jnp.max(value, axis=1, keepdims=True) for value in blocks]
    row_top = jnp.maximum(tops[0], tops[1])
    sums = [jnp.sum(jnp.exp(value - row_top), axis=1, keepdims=True) for value in blocks]
    log_total = row_top + jnp.log(sums[0] + sums[1])
    weights = [
        (jnp.exp(value - log_total) - onehot).astype(jnp.bfloat16)
        for value, onehot in zip(blocks, onehots)
    ]
    hit = sum(
        jnp.sum(jnp.where(onehot > 0, value, 0.0), axis=1, keepdims=True)
        for value, onehot in zip(blocks, onehots)
    )
    project(send_out, weights[1][:, :side], queries, meta[1], jnp.sum(log_total - hit))
    out_1[...] = weights[0]
    out_2[...] = weights[1]


def project(out, weights, queries, rep, loss):
    half = queries.shape[1] // 2
    for i, side in enumerate((rep, 1 - rep)):
        product = lax.dot_general(
            weights, queries[:, pl.ds(pl.multiple_of(side * half, half), half)],
            (((0,), (0,)), ((), ())), preferred_element_type=jnp.float32,
        )
        at = i * (half + LOSS)
        out[:, at:at + half] = 50.0 * product
        out[:, at + half:at + half + LOSS] = jnp.full((out.shape[0], LOSS), loss, jnp.float32)


def keep_kernel(meta, weights, queries, send, out):
    half = queries.shape[1] // 2
    project(
        out, weights[:, :out.shape[0]], queries, meta[1], send[0:1, half:half + 1]
    )


def first_sum(kept, sent, own, to_x, to_y, to_xy):
    rows, columns = own.shape
    half = columns - LOSS
    lanes = lax.broadcasted_iota(jnp.int32, (rows, LOSS), 1)
    for out, down, across in ((own, 0, 0), (to_x, 1, 0), (to_y, 0, 1), (to_xy, 1, 1)):
        at = pl.ds(down * rows, rows)
        data = pl.ds(across * columns, half)
        out[:, :half] = (kept[at, data] + sent[at, data]).astype(out.dtype)
        tile = pl.ds(across * columns + half, LOSS)
        loss = kept[at, tile] + sent[at, tile]
        high = loss.astype(jnp.bfloat16).astype(jnp.float32)
        out[:, half:] = jnp.where(lanes < LOSS // 2, high, loss - high).astype(out.dtype)


def second_sum(own, from_x, from_y, from_xy, after, *outs):
    rows = outs[0].shape[0]
    for i, out in enumerate(outs):
        at = pl.ds(i * rows, rows)
        out[...] = (own[at] + from_x[at].astype(jnp.float32)) + (
            from_y[at].astype(jnp.float32) + from_xy[at].astype(jnp.float32)
        )


def grad_kernel(weights_1, weights_2, rows_1, rows_2, out, done):
    done[...] = jnp.zeros(done.shape, done.dtype)
    out[...] = 50.0 * (
        jnp.dot(weights_1[...], rows_1[...], preferred_element_type=jnp.float32)
        + jnp.dot(weights_2[...], rows_2[...], preferred_element_type=jnp.float32)
    )


def shards(queries, passages, index_rows, positive, hard_rows, hard_counts):
    loop = lax.axis_size("loop")
    reps = lax.axis_size("rep")
    me = lax.axis_index("loop").astype(jnp.int32)
    rep = lax.axis_index("rep").astype(jnp.int32)
    count, width = queries.shape
    block = passages.shape[0]
    owners, slots = hard_rows.shape[1:]
    half = width // 2
    chips = loop // 2
    meta = jnp.stack([me, rep])
    both = ("loop", "rep")

    other_rows = exchange(index_rows, ("loop",), 1)
    rest = loop // 4
    wanted = jnp.transpose(hard_rows, (0, 2, 1)).reshape(slots, owners)
    wanted = [wanted] + [exchange(wanted, ("loop",), 4 * k) for k in range(1, rest)]
    asked, = pack([[(k, 0, slots) for k in range(rest)]], *wanted)
    asked_x = exchange(asked, ("loop",), 2)

    bits = [loop // 2 >> i for i in range(loop.bit_length() - 4)] + [4, 2, 1]
    orders = [0]
    for bit in bits:
        orders = orders + [o | bit for o in orders]
    for bit in bits[:-4]:
        passages = jnp.concatenate([passages, exchange(passages, ("loop",), bit)], axis=0)
    passages_z = exchange(passages, ("loop",), bits[-4])

    depth = 2 * slots
    have = 2 * passages.shape[0]
    top = chips // 2
    outs = [jax.ShapeDtypeStruct((top * depth, width), jnp.bfloat16)]
    outs += [jax.ShapeDtypeStruct((depth, width), jnp.bfloat16)] * top
    known = jax.ShapeDtypeStruct((have, width), jnp.bfloat16)
    known, plane, *sends = pl.pallas_call(
        functools.partial(pick_rows, top),
        out_shape=[known] + outs,
        in_specs=[SCALARS] + [WHOLE] * 6,
        out_specs=[WHOLE] * (2 + top),
        compiler_params=budget(index_rows, index_rows, *outs, *outs),
        cost_estimate=pl.CostEstimate(
            flops=4 * chips * slots * index_rows.shape[0] * width,
            bytes_accessed=3 * index_rows.size * 2, transcendentals=0,
        ),
    )(meta, asked, asked_x, other_rows, index_rows, passages, passages_z)

    def send(m, value):
        return exchange(value, ("loop",), 2 * m)

    def over(value):
        return exchange(value, ("rep",), 1)

    def cut(arrays, *pieces):
        return [
            (next(i for i, a in enumerate(arrays) if a is array), first, rows)
            for array, first, rows in pieces
        ]

    half_top = top // 2
    inner, outer = range(1, half_top + 1), range(half_top + 1, top)
    opposite_plane = over(plane)
    middle = [send(top + i, sends[i]) for i in range(half_top)]
    more = exchange(known, ("loop",), 4)

    arrays = [plane, opposite_plane, known, more, *middle, *sends[half_top:]]
    quad = [(known, 0, have), (more, 0, have)]
    batch, *going = pack(
        [cut(arrays, *[(value, 0, depth) for value in middle])]
        + [
            cut(arrays, (plane, m * depth, depth), (opposite_plane, m * depth, depth),
                *(quad if m == 1 else []))
            for m in inner
        ]
        + [cut(arrays, (value, 0, depth)) for value in sends[half_top:]],
        *arrays,
    )
    near_batch, far_batch = batch, over(batch)
    came = [send(m, value) for m, value in zip(inner, going)]
    late = [
        send(top + half_top + i, value) for i, value in enumerate(going[len(inner):])
    ]

    arrays = [plane, opposite_plane, known, more, *late, *came]
    batch, pair, *going = pack(
        [cut(arrays, *[(value, 0, depth) for value in late]),
         cut(arrays, *quad, (came[0], 2 * depth, 2 * have))]
        + [
            cut(arrays, (plane, m * depth, depth), (opposite_plane, m * depth, depth))
            for m in outer
        ],
        *arrays, far_batch,
    )
    last = [send(m, value) for m, value in zip(outer, going)] + [over(batch)]
    other_pair = exchange(pair, ("loop",), 1)

    first_rows = [(pair, 4 * have), (plane, depth), (opposite_plane, depth)]
    first_rows += [(value, 2 * depth) for value in came]
    first_rows += [(value, value.shape[0]) for value in (near_batch, far_batch, batch)]
    last_rows = [(value, value.shape[0]) for value in (other_pair, *last)]
    middle_masks = range(top, top + half_top)
    late_masks = range(top + half_top, chips)
    first_places = [(m, p) for m in (0, *inner) for p in range(2)]
    first_places += [(m, p) for p in range(2) for m in middle_masks]
    first_places += [(m, 0) for m in late_masks]
    last_places = [(m, p) for m in outer for p in range(2)] + [(m, 1) for m in late_masks]
    side = loop * block // 2
    columns = (
        (tuple(orders[:loop // 2]), tuple(first_places)),
        (tuple(orders[loop // 2:]), tuple(last_places)),
    )
    first_counts = tuple(n for _, n in first_rows)
    last_counts = tuple(n for _, n in last_rows)

    rows = loop * block
    rows_1 = jax.ShapeDtypeStruct((sum(first_counts), width), jnp.bfloat16)
    rows_2 = jax.ShapeDtypeStruct((sum(last_counts), width), jnp.bfloat16)
    payload = jax.ShapeDtypeStruct((side, width + 2 * LOSS), jnp.float32)
    scores, rows_1 = pl.pallas_call(
        functools.partial(early_kernel, first_counts),
        out_shape=[jax.ShapeDtypeStruct((count, rows_1.shape[0]), jnp.float32), rows_1],
        in_specs=[WHOLE] * (1 + len(first_rows)),
        out_specs=[WHOLE] * 2,
        compiler_params=budget(queries, rows_1, rows_1),
        cost_estimate=pl.CostEstimate(
            flops=2 * count * rows_1.size,
            bytes_accessed=2 * (queries.size + 2 * rows_1.size), transcendentals=0,
        ),
    )(queries, *[value for value, _ in first_rows])
    weights_1, weights_2, rows_2, send_part = pl.pallas_call(
        functools.partial(score_kernel, last_counts, columns, slots),
        out_shape=[
            jax.ShapeDtypeStruct((count, rows_1.shape[0]), jnp.bfloat16),
            jax.ShapeDtypeStruct((count, rows_2.shape[0]), jnp.bfloat16),
            rows_2, payload,
        ],
        in_specs=[SCALARS] * 2 + [WHOLE] * (3 + len(last_rows)),
        out_specs=[WHOLE] * 4,
        compiler_params=budget(queries, rows_2, rows_2, payload, payload),
        cost_estimate=pl.CostEstimate(
            flops=2 * count * (rows_2.size + payload.size),
            bytes_accessed=2 * (queries.size + 2 * rows_2.size) + 4 * payload.size,
            transcendentals=2 * count * (rows_1.shape[0] + rows_2.shape[0]),
        ),
    )(
        meta, hard_counts, queries, positive.reshape(1, count), scores,
        *[value for value, _ in last_rows],
    )

    sent = exchange(send_part, ("loop",), 1)
    kept = pl.pallas_call(
        keep_kernel,
        out_shape=jax.ShapeDtypeStruct((rows // 2, width + 2 * LOSS), jnp.float32),
        in_specs=[SCALARS] + [WHOLE] * 3,
        out_specs=WHOLE,
        compiler_params=budget(queries, payload, payload),
        cost_estimate=pl.CostEstimate(
            flops=count * rows * width,
            bytes_accessed=2 * count * width + 2 * rows * width, transcendentals=0,
        ),
    )(meta, weights_1, queries, send_part)
    query_grad, done = pl.pallas_call(
        grad_kernel,
        out_shape=[
            jax.ShapeDtypeStruct((count, width), jnp.float32),
            jax.ShapeDtypeStruct((8, 128), jnp.float32),
        ],
        in_specs=[WHOLE] * 4,
        out_specs=[WHOLE] * 2,
        compiler_params=budget(queries, queries, rows_1, rows_2),
        cost_estimate=pl.CostEstimate(
            flops=2 * count * (rows_1.size + rows_2.size),
            bytes_accessed=2 * (rows_1.size + rows_2.size) + 4 * count * width,
            transcendentals=0,
        ),
    )(weights_1, weights_2, rows_1, rows_2)
    part = half + LOSS
    quarter = rows // 4
    first = jax.ShapeDtypeStruct((quarter, part), jnp.float32)
    short = jax.ShapeDtypeStruct(first.shape, jnp.bfloat16)
    own, *going = pl.pallas_call(
        first_sum,
        out_shape=[first, short, first, short],
        in_specs=[WHOLE] * 2,
        out_specs=[WHOLE] * 4,
        compiler_params=budget(payload, payload, payload),
        cost_estimate=pl.CostEstimate(
            flops=payload.size, bytes_accessed=12 * payload.size, transcendentals=0
        ),
    )(kept, sent)
    came = [exchange(value, both, mask) for value, mask in zip(going, (4, 1, 5))]
    second = jax.ShapeDtypeStruct((block, part), jnp.float32)
    total, *going = pl.pallas_call(
        second_sum,
        out_shape=[second] * rest,
        in_specs=[WHOLE] * 5,
        out_specs=[WHOLE] * rest,
        compiler_params=budget(payload, payload),
        cost_estimate=pl.CostEstimate(
            flops=4 * first.size, bytes_accessed=20 * first.size, transcendentals=0
        ),
    )(own, *came, done)
    for value, order in zip(going, orders[1:rest]):
        total = total + exchange(value, ("loop",), order)
    mean_loss = (total[0, half] + total[0, half + LOSS // 2]) / (count * loop * reps)
    total = total[:, :half]
    opposite = exchange(total, ("rep",), 1)
    passage_grad = jnp.where(
        rep == 0,
        jnp.concatenate([total, opposite], axis=1),
        jnp.concatenate([opposite, total], axis=1),
    )

    return (query_grad, passage_grad, mean_loss)


def solution(mesh):
    placed = (
        P(("loop", "rep"), None),
        P("loop", None),
        P(("loop", "rep"), None),
        P(("loop", "rep")),
        P("loop", None, None),
        P("loop", None),
    )
    return jax.shard_map(
        shards,
        mesh=mesh,
        in_specs=placed,
        out_specs=(P(("loop", "rep"), None), P("loop", None), P()),
        check_vma=False,
    )
```

```python
import functools

import jax
import jax.numpy as jnp
from jax import lax
from jax.experimental import pallas as pl
from jax.experimental.pallas import tpu as pltpu
from jax.sharding import PartitionSpec as P


def budget(*arrays):
    total = sum(a.size * a.dtype.itemsize for a in arrays)
    return pltpu.CompilerParams(vmem_limit_bytes=total + total // 4 + 6 * 1024 * 1024)


WHOLE = pl.BlockSpec(memory_space=pltpu.VMEM)
SCALARS = pl.BlockSpec(memory_space=pltpu.SMEM)
LOSS = 128


def exchange(value, axes, mask):
    size = 1
    for axis in axes:
        size *= lax.axis_size(axis)
    return lax.ppermute(value, axes, [(i, i ^ mask) for i in range(size)])


def pick_rows(count, meta, asked, asked_x, other, own, passages, passages_z, known, plane, *pieces):
    me, rep = meta[0], meta[1]
    have = passages.shape[0]
    known[:have, :] = passages[...]
    known[have:, :] = passages_z[...]
    owners = asked.shape[1]
    slots = plane.shape[0] // (2 * count)
    lanes = lax.broadcasted_iota(jnp.int32, (slots, owners), 1)
    rows = lax.broadcasted_iota(jnp.int32, (slots, own.shape[0]), 1)

    def hot(owner):
        picked = []
        for m in range(count + len(pieces)):
            at = m // 2 * slots
            tile = (asked_x if m % 2 else asked)[at:at + slots, :]
            column = jnp.sum(jnp.where(lanes == owner, tile, 0), axis=1, keepdims=True)
            picked.append(jnp.where(column == rows, 1.0, 0.0))
        return jnp.concatenate(picked, axis=0).astype(jnp.bfloat16)

    hot_own = hot(me * 2 + rep)
    hot_other = hot((me ^ 1) * 2 + rep)
    got_other = jnp.dot(hot_other, other[...], preferred_element_type=jnp.float32)
    got_own = jnp.dot(hot_own, own[...], preferred_element_type=jnp.float32)
    for m in range(count + len(pieces)):
        part = slice(m * slots, (m + 1) * slots)
        value = jnp.concatenate([got_own[part], got_other[part]], axis=0).astype(jnp.bfloat16)
        if m < count:
            plane[m * 2 * slots:(m + 1) * 2 * slots, :] = value
        else:
            pieces[m - count][...] = value


def pack_kernel(layouts, *refs):
    ins, outs = refs[:-len(layouts)], refs[-len(layouts):]
    for layout, out in zip(layouts, outs):
        at = 0
        for which, first, rows in layout:
            out[at:at + rows, :] = ins[which][first:first + rows, :]
            at += rows


def pack(layouts, *arrays):
    shapes = [
        jax.ShapeDtypeStruct((sum(rows for _, _, rows in layout), arrays[0].shape[1]), arrays[0].dtype)
        for layout in layouts
    ]
    size = sum(shape.size for shape in shapes)
    return pl.pallas_call(
        functools.partial(pack_kernel, layouts),
        out_shape=shapes,
        in_specs=[WHOLE] * len(arrays),
        out_specs=[WHOLE] * len(layouts),
        compiler_params=budget(*shapes, *arrays),
        cost_estimate=pl.CostEstimate(flops=size, bytes_accessed=4 * size, transcendentals=0),
    )(*arrays)


def stack(counts, refs, out):
    at = 0
    for rows, ref in zip(counts, refs):
        out[at:at + rows, :] = ref[:rows, :]
        at += rows


def scored(queries, rows):
    return 50.0 * lax.dot_general(
        queries[...], rows[...], (((1,), (1,)), ((), ())), preferred_element_type=jnp.float32
    )


def early_kernel(counts, queries, *refs):
    *batches, scores_out, rows = refs
    stack(counts, batches, rows)
    scores_out[...] = scored(queries, rows)


def lookup(index, values):
    total = jnp.zeros_like(index)
    for i, value in enumerate(values):
        total = jnp.where(index == i, value, total)
    return total


def score_kernel(
    counts, columns, slots, meta, hard_counts, queries, positive, scores_ref, *refs
):
    *batches, out_1, out_2, rows, send_out = refs
    me, rep = meta[0], meta[1]
    stack(counts, batches, rows)
    side = send_out.shape[0]
    block = side // len(columns[0][0])
    blocks = [scores_ref[...], scored(queries, rows)]
    wanted = jnp.broadcast_to(positive[...].astype(jnp.float32), (8, positive.shape[1]))
    wanted = jnp.transpose(wanted)[:, :1]
    onehots = []
    for i, (order, places) in enumerate(columns):
        lane = lax.broadcasted_iota(jnp.int32, (1, blocks[i].shape[1]), 1)
        passage = lane < side
        ids = (lookup(lane // block, order) * block + lane % block) ^ (me * block)
        spot = jnp.where(passage, 0, lane - side)
        owner = lookup(spot // (2 * slots), [4 * m + p for m, p in places])
        owner = (owner + spot // slots % 2 * 2) ^ (me * 2 + rep)
        taken = lookup(owner, [hard_counts[0, o] for o in range(hard_counts.shape[1])])
        live = passage | (spot % slots < taken)
        onehots.append(
            jnp.where((wanted == ids.astype(jnp.float32)) & passage, 1.0, 0.0)
        )
        blocks[i] = jnp.where(live, blocks[i], -jnp.inf)
    tops = [jnp.max(value, axis=1, keepdims=True) for value in blocks]
    row_top = jnp.maximum(tops[0], tops[1])
    sums = [jnp.sum(jnp.exp(value - row_top), axis=1, keepdims=True) for value in blocks]
    log_total = row_top + jnp.log(sums[0] + sums[1])
    weights = [
        (jnp.exp(value - log_total) - onehot).astype(jnp.bfloat16)
        for value, onehot in zip(blocks, onehots)
    ]
    hit = sum(
        jnp.sum(jnp.where(onehot > 0, value, 0.0), axis=1, keepdims=True)
        for value, onehot in zip(blocks, onehots)
    )
    project(send_out, weights[1][:, :side], queries, meta[1], jnp.sum(log_total - hit))
    out_1[...] = weights[0]
    out_2[...] = weights[1]


def project(out, weights, queries, rep, loss):
    half = queries.shape[1] // 2
    for i, side in enumerate((rep, 1 - rep)):
        product = lax.dot_general(
            weights, queries[:, pl.ds(pl.multiple_of(side * half, half), half)],
            (((0,), (0,)), ((), ())), preferred_element_type=jnp.float32,
        )
        at = i * (half + LOSS)
        out[:, at:at + half] = 50.0 * product
        out[:, at + half:at + half + LOSS] = jnp.full((out.shape[0], LOSS), loss, jnp.float32)


def keep_kernel(meta, weights, queries, send, out):
    half = queries.shape[1] // 2
    project(
        out, weights[:, :out.shape[0]], queries, meta[1], send[0:1, half:half + 1]
    )


def first_sum(kept, sent, own, to_x, to_y, to_xy):
    rows, columns = own.shape
    half = columns - LOSS
    lanes = lax.broadcasted_iota(jnp.int32, (rows, LOSS), 1)
    for out, down, across in ((own, 0, 0), (to_x, 1, 0), (to_y, 0, 1), (to_xy, 1, 1)):
        at = pl.ds(down * rows, rows)
        data = pl.ds(across * columns, half)
        out[:, :half] = (kept[at, data] + sent[at, data]).astype(out.dtype)
        tile = pl.ds(across * columns + half, LOSS)
        loss = kept[at, tile] + sent[at, tile]
        high = loss.astype(jnp.bfloat16).astype(jnp.float32)
        out[:, half:] = jnp.where(lanes < LOSS // 2, high, loss - high).astype(out.dtype)


def second_sum(own, from_x, from_y, from_xy, after, *outs):
    rows = outs[0].shape[0]
    for i, out in enumerate(outs):
        at = pl.ds(i * rows, rows)
        out[...] = (own[at] + from_x[at].astype(jnp.float32)) + (
            from_y[at].astype(jnp.float32) + from_xy[at].astype(jnp.float32)
        )


def grad_kernel(weights_1, weights_2, rows_1, rows_2, out, done):
    done[...] = jnp.zeros(done.shape, done.dtype)
    out[...] = 50.0 * (
        jnp.dot(weights_1[...], rows_1[...], preferred_element_type=jnp.float32)
        + jnp.dot(weights_2[...], rows_2[...], preferred_element_type=jnp.float32)
    )


def shards(queries, passages, index_rows, positive, hard_rows, hard_counts):
    loop = lax.axis_size("loop")
    reps = lax.axis_size("rep")
    me = lax.axis_index("loop").astype(jnp.int32)
    rep = lax.axis_index("rep").astype(jnp.int32)
    count, width = queries.shape
    block = passages.shape[0]
    owners, slots = hard_rows.shape[1:]
    half = width // 2
    chips = loop // 2
    meta = jnp.stack([me, rep])
    both = ("loop", "rep")

    other_rows = exchange(index_rows, ("loop",), 1)
    own_rows = exchange(index_rows, ("loop",), 0)
    rest = loop // 4
    wanted = jnp.transpose(hard_rows, (0, 2, 1)).reshape(slots, owners)
    wanted = [wanted] + [exchange(wanted, ("loop",), 4 * k) for k in range(1, rest)]
    asked, = pack([[(k, 0, slots) for k in range(rest)]], *wanted)
    asked_x = exchange(asked, ("loop",), 2)

    bits = [loop // 2 >> i for i in range(loop.bit_length() - 4)] + [4, 2, 1]
    orders = [0]
    for bit in bits:
        orders = orders + [o | bit for o in orders]
    for bit in bits[:-4]:
        passages = jnp.concatenate([passages, exchange(passages, ("loop",), bit)], axis=0)
    passages_z = exchange(passages, ("loop",), bits[-4])
    passages = exchange(passages, ("loop",), 0)

    depth = 2 * slots
    have = 2 * passages.shape[0]
    top = chips // 2
    outs = [jax.ShapeDtypeStruct((top * depth, width), jnp.bfloat16)]
    outs += [jax.ShapeDtypeStruct((depth, width), jnp.bfloat16)] * top
    known = jax.ShapeDtypeStruct((have, width), jnp.bfloat16)
    known, plane, *sends = pl.pallas_call(
        functools.partial(pick_rows, top),
        out_shape=[known] + outs,
        in_specs=[SCALARS] + [WHOLE] * 6,
        out_specs=[WHOLE] * (2 + top),
        compiler_params=budget(index_rows, index_rows, *outs, *outs),
        cost_estimate=pl.CostEstimate(
            flops=4 * chips * slots * index_rows.shape[0] * width,
            bytes_accessed=3 * index_rows.size * 2, transcendentals=0,
        ),
    )(meta, asked, asked_x, other_rows, own_rows, passages, passages_z)

    def send(m, value):
        return exchange(value, ("loop",), 2 * m)

    def over(value):
        return exchange(value, ("rep",), 1)

    def cut(arrays, *pieces):
        return [
            (next(i for i, a in enumerate(arrays) if a is array), first, rows)
            for array, first, rows in pieces
        ]

    half_top = top // 2
    inner, outer = range(1, half_top + 1), range(half_top + 1, top)
    opposite_plane = over(plane)
    middle_masks, late_masks = range(top + 1, chips, 2), range(top, chips, 2)
    sends = dict(zip(range(top, chips), sends))
    middle = [send(m, sends[m]) for m in middle_masks]
    held_back = [sends[m] for m in late_masks]
    more = exchange(known, ("loop",), 4)

    arrays = [plane, opposite_plane, known, more, *middle, *held_back]
    quad = [(known, 0, have), (more, 0, have)]
    batch, *going = pack(
        [cut(arrays, *[(value, 0, depth) for value in middle])]
        + [
            cut(arrays, (plane, m * depth, depth), (opposite_plane, m * depth, depth),
                *(quad if m == 1 else []))
            for m in inner
        ]
        + [cut(arrays, (value, 0, depth)) for value in held_back],
        *arrays,
    )
    near_batch, far_batch = batch, over(batch)
    came = [send(m, value) for m, value in zip(inner, going)]
    late = [send(m, value) for m, value in zip(late_masks, going[len(inner):])]

    arrays = [plane, opposite_plane, known, more, *late, *came]
    batch, pair, *going = pack(
        [cut(arrays, *[(value, 0, depth) for value in late]),
         cut(arrays, *quad, (came[0], 2 * depth, 2 * have))]
        + [
            cut(arrays, (plane, m * depth, depth), (opposite_plane, m * depth, depth))
            for m in outer
        ],
        *arrays, far_batch,
    )
    last = [send(m, value) for m, value in zip(outer, going)] + [over(batch)]
    other_pair = exchange(pair, ("loop",), 1)

    first_rows = [(pair, 4 * have), (plane, depth), (opposite_plane, depth)]
    first_rows += [(value, 2 * depth) for value in came]
    first_rows += [(value, value.shape[0]) for value in (near_batch, far_batch, batch)]
    last_rows = [(value, value.shape[0]) for value in (other_pair, *last)]
    first_places = [(m, p) for m in (0, *inner) for p in range(2)]
    first_places += [(m, p) for p in range(2) for m in middle_masks]
    first_places += [(m, 0) for m in late_masks]
    last_places = [(m, p) for m in outer for p in range(2)] + [(m, 1) for m in late_masks]
    side = loop * block // 2
    columns = (
        (tuple(orders[:loop // 2]), tuple(first_places)),
        (tuple(orders[loop // 2:]), tuple(last_places)),
    )
    first_counts = tuple(n for _, n in first_rows)
    last_counts = tuple(n for _, n in last_rows)

    rows = loop * block
    rows_1 = jax.ShapeDtypeStruct((sum(first_counts), width), jnp.bfloat16)
    rows_2 = jax.ShapeDtypeStruct((sum(last_counts), width), jnp.bfloat16)
    payload = jax.ShapeDtypeStruct((side, width + 2 * LOSS), jnp.float32)
    scores, rows_1 = pl.pallas_call(
        functools.partial(early_kernel, first_counts),
        out_shape=[jax.ShapeDtypeStruct((count, rows_1.shape[0]), jnp.float32), rows_1],
        in_specs=[WHOLE] * (1 + len(first_rows)),
        out_specs=[WHOLE] * 2,
        compiler_params=budget(queries, rows_1, rows_1),
        cost_estimate=pl.CostEstimate(
            flops=2 * count * rows_1.size,
            bytes_accessed=2 * (queries.size + 2 * rows_1.size), transcendentals=0,
        ),
    )(queries, *[value for value, _ in first_rows])
    weights_1, weights_2, rows_2, send_part = pl.pallas_call(
        functools.partial(score_kernel, last_counts, columns, slots),
        out_shape=[
            jax.ShapeDtypeStruct((count, rows_1.shape[0]), jnp.bfloat16),
            jax.ShapeDtypeStruct((count, rows_2.shape[0]), jnp.bfloat16),
            rows_2, payload,
        ],
        in_specs=[SCALARS] * 2 + [WHOLE] * (3 + len(last_rows)),
        out_specs=[WHOLE] * 4,
        compiler_params=budget(queries, rows_2, rows_2, payload, payload),
        cost_estimate=pl.CostEstimate(
            flops=2 * count * (rows_2.size + payload.size),
            bytes_accessed=2 * (queries.size + 2 * rows_2.size) + 4 * payload.size,
            transcendentals=2 * count * (rows_1.shape[0] + rows_2.shape[0]),
        ),
    )(
        meta, hard_counts, queries, positive.reshape(1, count), scores,
        *[value for value, _ in last_rows],
    )

    sent = exchange(send_part, ("loop",), 1)
    kept = pl.pallas_call(
        keep_kernel,
        out_shape=jax.ShapeDtypeStruct((rows // 2, width + 2 * LOSS), jnp.float32),
        in_specs=[SCALARS] + [WHOLE] * 3,
        out_specs=WHOLE,
        compiler_params=budget(queries, payload, payload),
        cost_estimate=pl.CostEstimate(
            flops=count * rows * width,
            bytes_accessed=2 * count * width + 2 * rows * width, transcendentals=0,
        ),
    )(meta, weights_1, queries, send_part)
    query_grad, done = pl.pallas_call(
        grad_kernel,
        out_shape=[
            jax.ShapeDtypeStruct((count, width), jnp.float32),
            jax.ShapeDtypeStruct((8, 128), jnp.float32),
        ],
        in_specs=[WHOLE] * 4,
        out_specs=[WHOLE] * 2,
        compiler_params=budget(queries, queries, rows_1, rows_2),
        cost_estimate=pl.CostEstimate(
            flops=2 * count * (rows_1.size + rows_2.size),
            bytes_accessed=2 * (rows_1.size + rows_2.size) + 4 * count * width,
            transcendentals=0,
        ),
    )(weights_1, weights_2, rows_1, rows_2)
    part = half + LOSS
    quarter = rows // 4
    first = jax.ShapeDtypeStruct((quarter, part), jnp.float32)
    short = jax.ShapeDtypeStruct(first.shape, jnp.bfloat16)
    own, *going = pl.pallas_call(
        first_sum,
        out_shape=[first, short, first, short],
        in_specs=[WHOLE] * 2,
        out_specs=[WHOLE] * 4,
        compiler_params=budget(payload, payload, payload),
        cost_estimate=pl.CostEstimate(
            flops=payload.size, bytes_accessed=12 * payload.size, transcendentals=0
        ),
    )(kept, sent)
    came = [exchange(value, both, mask) for value, mask in zip(going, (4, 1, 5))]
    second = jax.ShapeDtypeStruct((block, part), jnp.float32)
    total, *going = pl.pallas_call(
        second_sum,
        out_shape=[second] * rest,
        in_specs=[WHOLE] * 5,
        out_specs=[WHOLE] * rest,
        compiler_params=budget(payload, payload),
        cost_estimate=pl.CostEstimate(
            flops=4 * first.size, bytes_accessed=20 * first.size, transcendentals=0
        ),
    )(own, *came, done)
    for value, order in zip(going, orders[1:rest]):
        total = total + exchange(value, ("loop",), order)
    mean_loss = (total[0, half] + total[0, half + LOSS // 2]) / (count * loop * reps)
    total = total[:, :half]
    opposite = exchange(total, ("rep",), 1)
    passage_grad = jnp.where(
        rep == 0,
        jnp.concatenate([total, opposite], axis=1),
        jnp.concatenate([opposite, total], axis=1),
    )

    return (query_grad, passage_grad, mean_loss)


def solution(mesh):
    placed = (
        P(("loop", "rep"), None),
        P("loop", None),
        P(("loop", "rep"), None),
        P(("loop", "rep")),
        P("loop", None, None),
        P("loop", None),
    )
    return jax.shard_map(
        shards,
        mesh=mesh,
        in_specs=placed,
        out_specs=(P(("loop", "rep"), None), P("loop", None), P()),
        check_vma=False,
    )
```

```python
import functools

import jax
import jax.numpy as jnp
from jax import lax
from jax.experimental import pallas as pl
from jax.experimental.pallas import tpu as pltpu
from jax.sharding import PartitionSpec as P


def budget(*arrays):
    total = sum(a.size * a.dtype.itemsize for a in arrays)
    return pltpu.CompilerParams(vmem_limit_bytes=total + total // 4 + 6 * 1024 * 1024)


WHOLE = pl.BlockSpec(memory_space=pltpu.VMEM)
SCALARS = pl.BlockSpec(memory_space=pltpu.SMEM)
LOSS = 128


def exchange(value, axes, mask):
    size = 1
    for axis in axes:
        size *= lax.axis_size(axis)
    return lax.ppermute(value, axes, [(i, i ^ mask) for i in range(size)])


def pick_rows(count, meta, asked, asked_x, other, own, after, plane, *pieces):
    me, rep = meta[0], meta[1]
    owners = asked.shape[1]
    slots = plane.shape[0] // (2 * count)
    lanes = lax.broadcasted_iota(jnp.int32, (slots, owners), 1)
    rows = lax.broadcasted_iota(jnp.int32, (slots, own.shape[0]), 1)

    def hot(owner):
        picked = []
        for m in range(count + len(pieces)):
            at = m // 2 * slots
            tile = (asked_x if m % 2 else asked)[at:at + slots, :]
            column = jnp.sum(jnp.where(lanes == owner, tile, 0), axis=1, keepdims=True)
            picked.append(jnp.where(column == rows, 1.0, 0.0))
        return jnp.concatenate(picked, axis=0).astype(jnp.bfloat16)

    hot_own = hot(me * 2 + rep)
    hot_other = hot((me ^ 1) * 2 + rep)
    got_other = jnp.dot(hot_other, other[...], preferred_element_type=jnp.float32)
    got_own = jnp.dot(hot_own, own[...], preferred_element_type=jnp.float32)
    for m in range(count + len(pieces)):
        part = slice(m * slots, (m + 1) * slots)
        value = jnp.concatenate([got_own[part], got_other[part]], axis=0).astype(jnp.bfloat16)
        if m < count:
            plane[m * 2 * slots:(m + 1) * 2 * slots, :] = value
        else:
            pieces[m - count][...] = value


def pack_kernel(layouts, *refs):
    ins, outs = refs[:-len(layouts)], refs[-len(layouts):]
    for layout, out in zip(layouts, outs):
        at = 0
        for which, first, rows in layout:
            out[at:at + rows, :] = ins[which][first:first + rows, :]
            at += rows


def pack(layouts, *arrays):
    shapes = [
        jax.ShapeDtypeStruct((sum(rows for _, _, rows in layout), arrays[0].shape[1]), arrays[0].dtype)
        for layout in layouts
    ]
    size = sum(shape.size for shape in shapes)
    return pl.pallas_call(
        functools.partial(pack_kernel, layouts),
        out_shape=shapes,
        in_specs=[WHOLE] * len(arrays),
        out_specs=[WHOLE] * len(layouts),
        compiler_params=budget(*shapes, *arrays),
        cost_estimate=pl.CostEstimate(flops=size, bytes_accessed=4 * size, transcendentals=0),
    )(*arrays)


def stack(counts, refs, out):
    at = 0
    for rows, ref in zip(counts, refs):
        out[at:at + rows, :] = ref[:rows, :]
        at += rows


def scored(queries, rows):
    return 50.0 * lax.dot_general(
        queries[...], rows[...], (((1,), (1,)), ((), ())), preferred_element_type=jnp.float32
    )


def early_kernel(counts, queries, *refs):
    *batches, scores_out, rows = refs
    stack(counts, batches, rows)
    scores_out[...] = scored(queries, rows)


def lookup(index, values):
    total = jnp.zeros_like(index)
    for i, value in enumerate(values):
        total = jnp.where(index == i, value, total)
    return total


def score_kernel(
    counts, passages, columns, slots, meta, hard_counts, queries, positive, scores_ref, *refs
):
    *batches, out_1, out_2, rows, send_out = refs
    batches = batches[-passages:] + batches[:-passages]
    me, rep = meta[0], meta[1]
    stack(counts, batches, rows)
    side = send_out.shape[0]
    block = side // len(columns[0][0])
    blocks = [scores_ref[...], scored(queries, rows)]
    wanted = jnp.broadcast_to(positive[...].astype(jnp.float32), (8, positive.shape[1]))
    wanted = jnp.transpose(wanted)[:, :1]
    onehots = []
    for i, (order, places) in enumerate(columns):
        lane = lax.broadcasted_iota(jnp.int32, (1, blocks[i].shape[1]), 1)
        passage = lane < side
        ids = (lookup(lane // block, order) * block + lane % block) ^ (me * block)
        spot = jnp.where(passage, 0, lane - side)
        owner = lookup(spot // (2 * slots), [4 * m + p for m, p in places])
        owner = (owner + spot // slots % 2 * 2) ^ (me * 2 + rep)
        taken = lookup(owner, [hard_counts[0, o] for o in range(hard_counts.shape[1])])
        live = passage | (spot % slots < taken)
        onehots.append(
            jnp.where((wanted == ids.astype(jnp.float32)) & passage, 1.0, 0.0)
        )
        blocks[i] = jnp.where(live, blocks[i], -jnp.inf)
    tops = [jnp.max(value, axis=1, keepdims=True) for value in blocks]
    row_top = jnp.maximum(tops[0], tops[1])
    sums = [jnp.sum(jnp.exp(value - row_top), axis=1, keepdims=True) for value in blocks]
    log_total = row_top + jnp.log(sums[0] + sums[1])
    weights = [
        (jnp.exp(value - log_total) - onehot).astype(jnp.bfloat16)
        for value, onehot in zip(blocks, onehots)
    ]
    hit = sum(
        jnp.sum(jnp.where(onehot > 0, value, 0.0), axis=1, keepdims=True)
        for value, onehot in zip(blocks, onehots)
    )
    project(send_out, weights[1][:, :side], queries, meta[1], jnp.sum(log_total - hit))
    out_1[...] = weights[0]
    out_2[...] = weights[1]


def project(out, weights, queries, rep, loss):
    half = queries.shape[1] // 2
    for i, side in enumerate((rep, 1 - rep)):
        product = lax.dot_general(
            weights, queries[:, pl.ds(pl.multiple_of(side * half, half), half)],
            (((0,), (0,)), ((), ())), preferred_element_type=jnp.float32,
        )
        at = i * (half + LOSS)
        out[:, at:at + half] = 50.0 * product
        out[:, at + half:at + half + LOSS] = jnp.full((out.shape[0], LOSS), loss, jnp.float32)


def keep_kernel(meta, weights, queries, send, out):
    half = queries.shape[1] // 2
    project(
        out, weights[:, :out.shape[0]], queries, meta[1], send[0:1, half:half + 1]
    )


def first_sum(kept, sent, own, to_x, to_y, to_xy):
    rows, columns = own.shape
    half = columns - LOSS
    lanes = lax.broadcasted_iota(jnp.int32, (rows, LOSS), 1)
    for out, down, across in ((own, 0, 0), (to_x, 1, 0), (to_y, 0, 1), (to_xy, 1, 1)):
        at = pl.ds(down * rows, rows)
        data = pl.ds(across * columns, half)
        out[:, :half] = (kept[at, data] + sent[at, data]).astype(out.dtype)
        tile = pl.ds(across * columns + half, LOSS)
        loss = kept[at, tile] + sent[at, tile]
        high = loss.astype(jnp.bfloat16).astype(jnp.float32)
        out[:, half:] = jnp.where(lanes < LOSS // 2, high, loss - high).astype(out.dtype)


def second_sum(own, from_x, from_y, from_xy, after, *outs):
    rows = outs[0].shape[0]
    for i, out in enumerate(outs):
        at = pl.ds(i * rows, rows)
        out[...] = (own[at] + from_x[at].astype(jnp.float32)) + (
            from_y[at].astype(jnp.float32) + from_xy[at].astype(jnp.float32)
        )


def grad_kernel(weights_1, weights_2, rows_1, rows_2, out, done):
    done[...] = jnp.zeros(done.shape, done.dtype)
    out[...] = 50.0 * (
        jnp.dot(weights_1[...], rows_1[...], preferred_element_type=jnp.float32)
        + jnp.dot(weights_2[...], rows_2[...], preferred_element_type=jnp.float32)
    )


def shards(queries, passages, index_rows, positive, hard_rows, hard_counts):
    loop = lax.axis_size("loop")
    reps = lax.axis_size("rep")
    me = lax.axis_index("loop").astype(jnp.int32)
    rep = lax.axis_index("rep").astype(jnp.int32)
    count, width = queries.shape
    block = passages.shape[0]
    owners, slots = hard_rows.shape[1:]
    half = width // 2
    chips = loop // 2
    meta = jnp.stack([me, rep])
    both = ("loop", "rep")

    other_rows = exchange(index_rows, ("loop",), 1)
    rest = loop // 4
    wanted = jnp.transpose(hard_rows, (0, 2, 1)).reshape(slots, owners)
    wanted = [wanted] + [exchange(wanted, ("loop",), 4 * k) for k in range(1, rest)]
    asked, = pack([[(k, 0, slots) for k in range(rest)]], *wanted)
    asked_x = exchange(asked, ("loop",), 2)

    bits = [loop // 2 >> i for i in range(loop.bit_length() - 4)] + [4, 2, 1]
    orders = [0]
    for bit in bits:
        orders = orders + [o | bit for o in orders]
    for bit in bits[:-4]:
        passages = jnp.concatenate([passages, exchange(passages, ("loop",), bit)], axis=0)
    passages_z = exchange(passages, ("loop",), bits[-4])

    depth = 2 * slots
    have = 2 * passages.shape[0]
    top = chips // 2
    outs = [jax.ShapeDtypeStruct((top * depth, width), jnp.bfloat16)]
    outs += [jax.ShapeDtypeStruct((depth, width), jnp.bfloat16)] * top
    known = jnp.concatenate([passages, passages_z], axis=0)
    plane, *sends = pl.pallas_call(
        functools.partial(pick_rows, top),
        out_shape=outs,
        in_specs=[SCALARS] + [WHOLE] * 5,
        out_specs=[WHOLE] * (1 + top),
        compiler_params=budget(index_rows, index_rows, *outs, *outs),
        cost_estimate=pl.CostEstimate(
            flops=4 * chips * slots * index_rows.shape[0] * width,
            bytes_accessed=3 * index_rows.size * 2, transcendentals=0,
        ),
    )(meta, asked, asked_x, other_rows, index_rows, passages_z)

    def send(m, value):
        return exchange(value, ("loop",), 2 * m)

    def over(value):
        return exchange(value, ("rep",), 1)

    def cut(arrays, *pieces):
        return [
            (next(i for i, a in enumerate(arrays) if a is array), first, rows)
            for array, first, rows in pieces
        ]

    half_top = top // 2
    inner, outer = range(1, half_top + 1), range(half_top + 1, top)
    opposite_plane = over(plane)
    middle_masks, late_masks = range(top + 1, chips, 2), range(top, chips, 2)
    sends = dict(zip(range(top, chips), sends))
    middle = [send(m, sends[m]) for m in middle_masks]
    held_back = [sends[m] for m in late_masks]
    more = exchange(known, ("loop",), 4)

    arrays = [plane, opposite_plane, *middle, known, more, *held_back]
    quad = [(known, 0, have), (more, 0, have)]
    batch, *going = pack(
        [cut(arrays, *[(value, 0, depth) for value in middle])]
        + [
            cut(arrays, (plane, m * depth, depth), (opposite_plane, m * depth, depth),
                *(quad if m == 1 else []))
            for m in inner
        ]
        + [cut(arrays, (value, 0, depth)) for value in held_back],
        *arrays,
    )
    near_batch, far_batch = batch, over(batch)
    came = [send(m, value) for m, value in zip(inner, going)]
    late = [send(m, value) for m, value in zip(late_masks, going[len(inner):])]

    arrays = [plane, opposite_plane, going[0], *late, *came]
    batch, *pair_and_going = pack(
        [cut(arrays, *[(value, 0, depth) for value in late]),
         cut(arrays, (going[0], 2 * depth, 2 * have)),
         cut(arrays, (came[0], 2 * depth, 2 * have))]
        + [
            cut(arrays, (plane, m * depth, depth), (opposite_plane, m * depth, depth))
            for m in outer
        ],
        *arrays, far_batch,
    )
    pair, going = pair_and_going[:2], pair_and_going[2:]
    last = [send(m, value) for m, value in zip(outer, going)] + [over(batch)]
    other_pair = [exchange(value, ("loop",), 1) for value in pair]

    first_rows = [(value, 2 * have) for value in pair]
    first_rows += [(plane, depth), (opposite_plane, depth)]
    first_rows += [(value, 2 * depth) for value in came]
    first_rows += [(value, value.shape[0]) for value in (near_batch, far_batch, batch)]
    last_rows = [(value, value.shape[0]) for value in (*other_pair, *last)]
    first_places = [(m, p) for m in (0, *inner) for p in range(2)]
    first_places += [(m, p) for p in range(2) for m in middle_masks]
    first_places += [(m, 0) for m in late_masks]
    last_places = [(m, p) for m in outer for p in range(2)] + [(m, 1) for m in late_masks]
    side = loop * block // 2
    columns = (
        (tuple(orders[:loop // 2]), tuple(first_places)),
        (tuple(orders[loop // 2:]), tuple(last_places)),
    )
    first_counts = tuple(n for _, n in first_rows)
    last_counts = tuple(n for _, n in last_rows)

    rows = loop * block
    rows_1 = jax.ShapeDtypeStruct((sum(first_counts), width), jnp.bfloat16)
    rows_2 = jax.ShapeDtypeStruct((sum(last_counts), width), jnp.bfloat16)
    payload = jax.ShapeDtypeStruct((side, width + 2 * LOSS), jnp.float32)
    scores, rows_1 = pl.pallas_call(
        functools.partial(early_kernel, first_counts),
        out_shape=[jax.ShapeDtypeStruct((count, rows_1.shape[0]), jnp.float32), rows_1],
        in_specs=[WHOLE] * (1 + len(first_rows)),
        out_specs=[WHOLE] * 2,
        compiler_params=budget(queries, rows_1, rows_1),
        cost_estimate=pl.CostEstimate(
            flops=2 * count * rows_1.size,
            bytes_accessed=2 * (queries.size + 2 * rows_1.size), transcendentals=0,
        ),
    )(queries, *[value for value, _ in first_rows])
    weights_1, weights_2, rows_2, send_part = pl.pallas_call(
        functools.partial(score_kernel, last_counts, len(other_pair), columns, slots),
        out_shape=[
            jax.ShapeDtypeStruct((count, rows_1.shape[0]), jnp.bfloat16),
            jax.ShapeDtypeStruct((count, rows_2.shape[0]), jnp.bfloat16),
            rows_2, payload,
        ],
        in_specs=[SCALARS] * 2 + [WHOLE] * (3 + len(last_rows)),
        out_specs=[WHOLE] * 4,
        compiler_params=budget(queries, rows_2, rows_2, payload, payload),
        cost_estimate=pl.CostEstimate(
            flops=2 * count * (rows_2.size + payload.size),
            bytes_accessed=2 * (queries.size + 2 * rows_2.size) + 4 * payload.size,
            transcendentals=2 * count * (rows_1.shape[0] + rows_2.shape[0]),
        ),
    )(
        meta, hard_counts, queries, positive.reshape(1, count), scores,
        *last, *other_pair,
    )

    sent = exchange(send_part, ("loop",), 1)
    kept = pl.pallas_call(
        keep_kernel,
        out_shape=jax.ShapeDtypeStruct((rows // 2, width + 2 * LOSS), jnp.float32),
        in_specs=[SCALARS] + [WHOLE] * 3,
        out_specs=WHOLE,
        compiler_params=budget(queries, payload, payload),
        cost_estimate=pl.CostEstimate(
            flops=count * rows * width,
            bytes_accessed=2 * count * width + 2 * rows * width, transcendentals=0,
        ),
    )(meta, weights_1, queries, send_part)
    query_grad, done = pl.pallas_call(
        grad_kernel,
        out_shape=[
            jax.ShapeDtypeStruct((count, width), jnp.float32),
            jax.ShapeDtypeStruct((8, 128), jnp.float32),
        ],
        in_specs=[WHOLE] * 4,
        out_specs=[WHOLE] * 2,
        compiler_params=budget(queries, queries, rows_1, rows_2),
        cost_estimate=pl.CostEstimate(
            flops=2 * count * (rows_1.size + rows_2.size),
            bytes_accessed=2 * (rows_1.size + rows_2.size) + 4 * count * width,
            transcendentals=0,
        ),
    )(weights_1, weights_2, rows_1, rows_2)
    part = half + LOSS
    quarter = rows // 4
    first = jax.ShapeDtypeStruct((quarter, part), jnp.float32)
    short = jax.ShapeDtypeStruct(first.shape, jnp.bfloat16)
    own, *going = pl.pallas_call(
        first_sum,
        out_shape=[first, short, first, short],
        in_specs=[WHOLE] * 2,
        out_specs=[WHOLE] * 4,
        compiler_params=budget(payload, payload, payload),
        cost_estimate=pl.CostEstimate(
            flops=payload.size, bytes_accessed=12 * payload.size, transcendentals=0
        ),
    )(kept, sent)
    came = [exchange(value, both, mask) for value, mask in zip(going, (4, 1, 5))]
    second = jax.ShapeDtypeStruct((block, part), jnp.float32)
    total, *going = pl.pallas_call(
        second_sum,
        out_shape=[second] * rest,
        in_specs=[WHOLE] * 5,
        out_specs=[WHOLE] * rest,
        compiler_params=budget(payload, payload),
        cost_estimate=pl.CostEstimate(
            flops=4 * first.size, bytes_accessed=20 * first.size, transcendentals=0
        ),
    )(own, *came, done)
    for value, order in zip(going, orders[1:rest]):
        total = total + exchange(value, ("loop",), order)
    mean_loss = (total[0, half] + total[0, half + LOSS // 2]) / (count * loop * reps)
    total = total[:, :half]
    opposite = exchange(total, ("rep",), 1)
    passage_grad = jnp.where(
        rep == 0,
        jnp.concatenate([total, opposite], axis=1),
        jnp.concatenate([opposite, total], axis=1),
    )

    return (query_grad, passage_grad, mean_loss)


def solution(mesh):
    placed = (
        P(("loop", "rep"), None),
        P("loop", None),
        P(("loop", "rep"), None),
        P(("loop", "rep")),
        P("loop", None, None),
        P("loop", None),
    )
    return jax.shard_map(
        shards,
        mesh=mesh,
        in_specs=placed,
        out_specs=(P(("loop", "rep"), None), P("loop", None), P()),
        check_vma=False,
    )
```

```python
import functools

import jax
import jax.numpy as jnp
from jax import lax
from jax.experimental import pallas as pl
from jax.experimental.pallas import tpu as pltpu
from jax.sharding import PartitionSpec as P


def budget(*arrays):
    total = sum(a.size * a.dtype.itemsize for a in arrays)
    return pltpu.CompilerParams(vmem_limit_bytes=total + total // 4 + 6 * 1024 * 1024)


WHOLE = pl.BlockSpec(memory_space=pltpu.VMEM)
SCALARS = pl.BlockSpec(memory_space=pltpu.SMEM)
LOSS = 128


def exchange(value, axes, mask):
    size = 1
    for axis in axes:
        size *= lax.axis_size(axis)
    return lax.ppermute(value, axes, [(i, i ^ mask) for i in range(size)])


def pick_rows(count, reach, meta, other, own, after, *refs):
    asked, (plane, *pieces) = refs[:reach], refs[reach:]
    me, rep = meta[0], meta[1]
    owners = asked[0].shape[1]
    slots = plane.shape[0] // (2 * count)
    lanes = lax.broadcasted_iota(jnp.int32, (slots, owners), 1)
    rows = lax.broadcasted_iota(jnp.int32, (slots, own.shape[0]), 1)

    def hot(owner):
        picked = []
        for m in range(count + len(pieces)):
            at = m % 2 * slots
            tile = asked[m // 2][at:at + slots, :]
            column = jnp.sum(jnp.where(lanes == owner, tile, 0), axis=1, keepdims=True)
            picked.append(jnp.where(column == rows, 1.0, 0.0))
        return jnp.concatenate(picked, axis=0).astype(jnp.bfloat16)

    hot_own = hot(me * 2 + rep)
    hot_other = hot((me ^ 1) * 2 + rep)
    got_other = jnp.dot(hot_other, other[...], preferred_element_type=jnp.float32)
    got_own = jnp.dot(hot_own, own[...], preferred_element_type=jnp.float32)
    for m in range(count + len(pieces)):
        part = slice(m * slots, (m + 1) * slots)
        value = jnp.concatenate([got_own[part], got_other[part]], axis=0).astype(jnp.bfloat16)
        if m < count:
            plane[m * 2 * slots:(m + 1) * 2 * slots, :] = value
        else:
            pieces[m - count][...] = value


def pack_kernel(layouts, *refs):
    ins, outs = refs[:-len(layouts)], refs[-len(layouts):]
    for layout, out in zip(layouts, outs):
        at = 0
        for which, first, rows in layout:
            out[at:at + rows, :] = ins[which][first:first + rows, :]
            at += rows


def pack(layouts, *arrays):
    shapes = [
        jax.ShapeDtypeStruct((sum(rows for _, _, rows in layout), arrays[0].shape[1]), arrays[0].dtype)
        for layout in layouts
    ]
    size = sum(shape.size for shape in shapes)
    return pl.pallas_call(
        functools.partial(pack_kernel, layouts),
        out_shape=shapes,
        in_specs=[WHOLE] * len(arrays),
        out_specs=[WHOLE] * len(layouts),
        compiler_params=budget(*shapes, *arrays),
        cost_estimate=pl.CostEstimate(flops=size, bytes_accessed=4 * size, transcendentals=0),
    )(*arrays)


def stack(counts, refs, out):
    at = 0
    for rows, ref in zip(counts, refs):
        out[at:at + rows, :] = ref[:rows, :]
        at += rows


def scored(queries, rows):
    return 50.0 * lax.dot_general(
        queries[...], rows[...], (((1,), (1,)), ((), ())), preferred_element_type=jnp.float32
    )


def early_kernel(counts, queries, *refs):
    *batches, scores_out, rows = refs
    stack(counts, batches, rows)
    scores_out[...] = scored(queries, rows)


def lookup(index, values):
    total = jnp.zeros_like(index)
    for i, value in enumerate(values):
        total = jnp.where(index == i, value, total)
    return total


def score_kernel(
    counts, passages, columns, slots, meta, hard_counts, queries, positive, scores_ref, *refs
):
    *batches, out_1, out_2, rows, send_out = refs
    batches = batches[-passages:] + batches[:-passages]
    me, rep = meta[0], meta[1]
    stack(counts, batches, rows)
    side = send_out.shape[0]
    block = side // len(columns[0][0])
    blocks = [scores_ref[...], scored(queries, rows)]
    wanted = jnp.broadcast_to(positive[...].astype(jnp.float32), (8, positive.shape[1]))
    wanted = jnp.transpose(wanted)[:, :1]
    onehots = []
    for i, (order, places) in enumerate(columns):
        lane = lax.broadcasted_iota(jnp.int32, (1, blocks[i].shape[1]), 1)
        passage = lane < side
        ids = (lookup(lane // block, order) * block + lane % block) ^ (me * block)
        spot = jnp.where(passage, 0, lane - side)
        owner = lookup(spot // (2 * slots), [4 * m + p for m, p in places])
        owner = (owner + spot // slots % 2 * 2) ^ (me * 2 + rep)
        taken = lookup(owner, [hard_counts[0, o] for o in range(hard_counts.shape[1])])
        live = passage | (spot % slots < taken)
        onehots.append(
            jnp.where((wanted == ids.astype(jnp.float32)) & passage, 1.0, 0.0)
        )
        blocks[i] = jnp.where(live, blocks[i], -jnp.inf)
    tops = [jnp.max(value, axis=1, keepdims=True) for value in blocks]
    row_top = jnp.maximum(tops[0], tops[1])
    sums = [jnp.sum(jnp.exp(value - row_top), axis=1, keepdims=True) for value in blocks]
    log_total = row_top + jnp.log(sums[0] + sums[1])
    weights = [
        (jnp.exp(value - log_total) - onehot).astype(jnp.bfloat16)
        for value, onehot in zip(blocks, onehots)
    ]
    hit = sum(
        jnp.sum(jnp.where(onehot > 0, value, 0.0), axis=1, keepdims=True)
        for value, onehot in zip(blocks, onehots)
    )
    project(send_out, weights[1][:, :side], queries, meta[1], jnp.sum(log_total - hit))
    out_1[...] = weights[0]
    out_2[...] = weights[1]


def project(out, weights, queries, rep, loss):
    half = queries.shape[1] // 2
    for i, side in enumerate((rep, 1 - rep)):
        product = lax.dot_general(
            weights, queries[:, pl.ds(pl.multiple_of(side * half, half), half)],
            (((0,), (0,)), ((), ())), preferred_element_type=jnp.float32,
        )
        at = i * (half + LOSS)
        out[:, at:at + half] = 50.0 * product
        out[:, at + half:at + half + LOSS] = jnp.full((out.shape[0], LOSS), loss, jnp.float32)


def keep_kernel(meta, weights, queries, send, out):
    half = queries.shape[1] // 2
    project(
        out, weights[:, :out.shape[0]], queries, meta[1], send[0:1, half:half + 1]
    )


def first_sum(kept, sent, own, to_x, to_y, to_xy):
    rows, columns = own.shape
    half = columns - LOSS
    lanes = lax.broadcasted_iota(jnp.int32, (rows, LOSS), 1)
    for out, down, across in ((own, 0, 0), (to_x, 1, 0), (to_y, 0, 1), (to_xy, 1, 1)):
        at = pl.ds(down * rows, rows)
        data = pl.ds(across * columns, half)
        out[:, :half] = (kept[at, data] + sent[at, data]).astype(out.dtype)
        tile = pl.ds(across * columns + half, LOSS)
        loss = kept[at, tile] + sent[at, tile]
        high = loss.astype(jnp.bfloat16).astype(jnp.float32)
        out[:, half:] = jnp.where(lanes < LOSS // 2, high, loss - high).astype(out.dtype)


def second_sum(own, from_x, from_y, from_xy, after, *outs):
    rows = outs[0].shape[0]
    for i, out in enumerate(outs):
        at = pl.ds(i * rows, rows)
        out[...] = (own[at] + from_x[at].astype(jnp.float32)) + (
            from_y[at].astype(jnp.float32) + from_xy[at].astype(jnp.float32)
        )


def grad_kernel(weights_1, weights_2, rows_1, rows_2, out, done):
    done[...] = jnp.zeros(done.shape, done.dtype)
    out[...] = 50.0 * (
        jnp.dot(weights_1[...], rows_1[...], preferred_element_type=jnp.float32)
        + jnp.dot(weights_2[...], rows_2[...], preferred_element_type=jnp.float32)
    )


def shards(queries, passages, index_rows, positive, hard_rows, hard_counts):
    loop = lax.axis_size("loop")
    reps = lax.axis_size("rep")
    me = lax.axis_index("loop").astype(jnp.int32)
    rep = lax.axis_index("rep").astype(jnp.int32)
    count, width = queries.shape
    block = passages.shape[0]
    owners, slots = hard_rows.shape[1:]
    half = width // 2
    chips = loop // 2
    meta = jnp.stack([me, rep])
    both = ("loop", "rep")

    other_rows = exchange(index_rows, ("loop",), 1)
    rest = loop // 4
    wanted = jnp.transpose(hard_rows, (0, 2, 1)).reshape(slots, owners)
    asked, = pack([[(0, 0, slots), (1, 0, slots)]], wanted, exchange(wanted, ("loop",), 2))
    asked = [asked] + [exchange(asked, ("loop",), 4 * k) for k in range(1, rest)]
    own_rows, = pack([[(0, 0, index_rows.shape[0])]], index_rows)

    bits = [loop // 2 >> i for i in range(loop.bit_length() - 4)] + [4, 2, 1]
    orders = [0]
    for bit in bits:
        orders = orders + [o | bit for o in orders]
    for bit in bits[:-4]:
        passages = jnp.concatenate([passages, exchange(passages, ("loop",), bit)], axis=0)
    passages_z = exchange(passages, ("loop",), bits[-4])

    depth = 2 * slots
    have = 2 * passages.shape[0]
    top = chips // 2
    outs = [jax.ShapeDtypeStruct((top * depth, width), jnp.bfloat16)]
    outs += [jax.ShapeDtypeStruct((depth, width), jnp.bfloat16)] * top
    known = jnp.concatenate([passages, passages_z], axis=0)
    plane, *sends = pl.pallas_call(
        functools.partial(pick_rows, top, rest),
        out_shape=outs,
        in_specs=[SCALARS] + [WHOLE] * (3 + rest),
        out_specs=[WHOLE] * (1 + top),
        compiler_params=budget(index_rows, index_rows, *outs, *outs),
        cost_estimate=pl.CostEstimate(
            flops=4 * chips * slots * index_rows.shape[0] * width,
            bytes_accessed=3 * index_rows.size * 2, transcendentals=0,
        ),
    )(meta, other_rows, own_rows, passages_z, *asked)

    def send(m, value):
        return exchange(value, ("loop",), 2 * m)

    def over(value):
        return exchange(value, ("rep",), 1)

    def cut(arrays, *pieces):
        return [
            (next(i for i, a in enumerate(arrays) if a is array), first, rows)
            for array, first, rows in pieces
        ]

    half_top = top // 2
    inner, outer = range(1, half_top + 1), range(half_top + 1, top)
    opposite_plane = over(plane)
    middle_masks, late_masks = range(top + 1, chips, 2), range(top, chips, 2)
    sends = dict(zip(range(top, chips), sends))
    middle = [send(m, sends[m]) for m in middle_masks]
    held_back = [sends[m] for m in late_masks]
    more = exchange(known, ("loop",), 4)

    arrays = [plane, opposite_plane, *middle, known, more, *held_back]
    quad = [(known, 0, have), (more, 0, have)]
    batch, *going = pack(
        [cut(arrays, *[(value, 0, depth) for value in middle])]
        + [
            cut(arrays, (plane, m * depth, depth), (opposite_plane, m * depth, depth),
                *(quad if m == 1 else []))
            for m in inner
        ]
        + [cut(arrays, (value, 0, depth)) for value in held_back],
        *arrays,
    )
    near_batch, far_batch = batch, over(batch)
    came = [send(m, value) for m, value in zip(inner, going)]
    late = [send(m, value) for m, value in zip(late_masks, going[len(inner):])]

    arrays = [plane, opposite_plane, going[0], *late, *came]
    batch, *pair_and_going = pack(
        [cut(arrays, *[(value, 0, depth) for value in late]),
         cut(arrays, (going[0], 2 * depth, 2 * have)),
         cut(arrays, (came[0], 2 * depth, 2 * have))]
        + [
            cut(arrays, (plane, m * depth, depth), (opposite_plane, m * depth, depth))
            for m in outer
        ],
        *arrays, far_batch,
    )
    pair, going = pair_and_going[:2], pair_and_going[2:]
    last = [send(m, value) for m, value in zip(outer, going)] + [over(batch)]
    other_pair = [exchange(value, ("loop",), 1) for value in pair]

    first_rows = [(value, 2 * have) for value in pair]
    first_rows += [(plane, depth), (opposite_plane, depth)]
    first_rows += [(value, 2 * depth) for value in came]
    first_rows += [(value, value.shape[0]) for value in (near_batch, far_batch, batch)]
    last_rows = [(value, value.shape[0]) for value in (*other_pair, *last)]
    first_places = [(m, p) for m in (0, *inner) for p in range(2)]
    first_places += [(m, p) for p in range(2) for m in middle_masks]
    first_places += [(m, 0) for m in late_masks]
    last_places = [(m, p) for m in outer for p in range(2)] + [(m, 1) for m in late_masks]
    side = loop * block // 2
    columns = (
        (tuple(orders[:loop // 2]), tuple(first_places)),
        (tuple(orders[loop // 2:]), tuple(last_places)),
    )
    first_counts = tuple(n for _, n in first_rows)
    last_counts = tuple(n for _, n in last_rows)

    rows = loop * block
    rows_1 = jax.ShapeDtypeStruct((sum(first_counts), width), jnp.bfloat16)
    rows_2 = jax.ShapeDtypeStruct((sum(last_counts), width), jnp.bfloat16)
    payload = jax.ShapeDtypeStruct((side, width + 2 * LOSS), jnp.float32)
    scores, rows_1 = pl.pallas_call(
        functools.partial(early_kernel, first_counts),
        out_shape=[jax.ShapeDtypeStruct((count, rows_1.shape[0]), jnp.float32), rows_1],
        in_specs=[WHOLE] * (1 + len(first_rows)),
        out_specs=[WHOLE] * 2,
        compiler_params=budget(queries, rows_1, rows_1),
        cost_estimate=pl.CostEstimate(
            flops=2 * count * rows_1.size,
            bytes_accessed=2 * (queries.size + 2 * rows_1.size), transcendentals=0,
        ),
    )(queries, *[value for value, _ in first_rows])
    weights_1, weights_2, rows_2, send_part = pl.pallas_call(
        functools.partial(score_kernel, last_counts, len(other_pair), columns, slots),
        out_shape=[
            jax.ShapeDtypeStruct((count, rows_1.shape[0]), jnp.bfloat16),
            jax.ShapeDtypeStruct((count, rows_2.shape[0]), jnp.bfloat16),
            rows_2, payload,
        ],
        in_specs=[SCALARS] * 2 + [WHOLE] * (3 + len(last_rows)),
        out_specs=[WHOLE] * 4,
        compiler_params=budget(queries, rows_2, rows_2, payload, payload),
        cost_estimate=pl.CostEstimate(
            flops=2 * count * (rows_2.size + payload.size),
            bytes_accessed=2 * (queries.size + 2 * rows_2.size) + 4 * payload.size,
            transcendentals=2 * count * (rows_1.shape[0] + rows_2.shape[0]),
        ),
    )(
        meta, hard_counts, queries, positive.reshape(1, count), scores,
        *last, *other_pair,
    )

    sent = exchange(send_part, ("loop",), 1)
    kept = pl.pallas_call(
        keep_kernel,
        out_shape=jax.ShapeDtypeStruct((rows // 2, width + 2 * LOSS), jnp.float32),
        in_specs=[SCALARS] + [WHOLE] * 3,
        out_specs=WHOLE,
        compiler_params=budget(queries, payload, payload),
        cost_estimate=pl.CostEstimate(
            flops=count * rows * width,
            bytes_accessed=2 * count * width + 2 * rows * width, transcendentals=0,
        ),
    )(meta, weights_1, queries, send_part)
    query_grad, done = pl.pallas_call(
        grad_kernel,
        out_shape=[
            jax.ShapeDtypeStruct((count, width), jnp.float32),
            jax.ShapeDtypeStruct((8, 128), jnp.float32),
        ],
        in_specs=[WHOLE] * 4,
        out_specs=[WHOLE] * 2,
        compiler_params=budget(queries, queries, rows_1, rows_2),
        cost_estimate=pl.CostEstimate(
            flops=2 * count * (rows_1.size + rows_2.size),
            bytes_accessed=2 * (rows_1.size + rows_2.size) + 4 * count * width,
            transcendentals=0,
        ),
    )(weights_1, weights_2, rows_1, rows_2)
    part = half + LOSS
    quarter = rows // 4
    first = jax.ShapeDtypeStruct((quarter, part), jnp.float32)
    short = jax.ShapeDtypeStruct(first.shape, jnp.bfloat16)
    own, *going = pl.pallas_call(
        first_sum,
        out_shape=[first, short, first, short],
        in_specs=[WHOLE] * 2,
        out_specs=[WHOLE] * 4,
        compiler_params=budget(payload, payload, payload),
        cost_estimate=pl.CostEstimate(
            flops=payload.size, bytes_accessed=12 * payload.size, transcendentals=0
        ),
    )(kept, sent)
    came = [exchange(value, both, mask) for value, mask in zip(going, (4, 1, 5))]
    second = jax.ShapeDtypeStruct((block, part), jnp.float32)
    total, *going = pl.pallas_call(
        second_sum,
        out_shape=[second] * rest,
        in_specs=[WHOLE] * 5,
        out_specs=[WHOLE] * rest,
        compiler_params=budget(payload, payload),
        cost_estimate=pl.CostEstimate(
            flops=4 * first.size, bytes_accessed=20 * first.size, transcendentals=0
        ),
    )(own, *came, done)
    for value, order in zip(going, orders[1:rest]):
        total = total + exchange(value, ("loop",), order)
    mean_loss = (total[0, half] + total[0, half + LOSS // 2]) / (count * loop * reps)
    total = total[:, :half]
    opposite = exchange(total, ("rep",), 1)
    passage_grad = jnp.where(
        rep == 0,
        jnp.concatenate([total, opposite], axis=1),
        jnp.concatenate([opposite, total], axis=1),
    )

    return (query_grad, passage_grad, mean_loss)


def solution(mesh):
    placed = (
        P(("loop", "rep"), None),
        P("loop", None),
        P(("loop", "rep"), None),
        P(("loop", "rep")),
        P("loop", None, None),
        P("loop", None),
    )
    return jax.shard_map(
        shards,
        mesh=mesh,
        in_specs=placed,
        out_specs=(P(("loop", "rep"), None), P("loop", None), P()),
        check_vma=False,
    )
```

```python
import functools

import jax
import jax.numpy as jnp
from jax import lax
from jax.experimental import pallas as pl
from jax.experimental.pallas import tpu as pltpu
from jax.sharding import PartitionSpec as P


def budget(*arrays):
    total = sum(a.size * a.dtype.itemsize for a in arrays)
    return pltpu.CompilerParams(vmem_limit_bytes=total + total // 4 + 6 * 1024 * 1024)


WHOLE = pl.BlockSpec(memory_space=pltpu.VMEM)
SCALARS = pl.BlockSpec(memory_space=pltpu.SMEM)
LOSS = 128


def exchange(value, axes, mask):
    size = 1
    for axis in axes:
        size *= lax.axis_size(axis)
    return lax.ppermute(value, axes, [(i, i ^ mask) for i in range(size)])


def pick_rows(count, reach, meta, other, own, after, *refs):
    asked, (plane, *pieces) = refs[:reach], refs[reach:]
    me, rep = meta[0], meta[1]
    owners = asked[0].shape[1]
    slots = plane.shape[0] // (2 * count)
    lanes = lax.broadcasted_iota(jnp.int32, (slots, owners), 1)
    rows = lax.broadcasted_iota(jnp.int32, (slots, own.shape[0]), 1)

    def hot(owner):
        picked = []
        for m in range(count + len(pieces)):
            at = m % 2 * slots
            tile = asked[m // 2][at:at + slots, :]
            column = jnp.sum(jnp.where(lanes == owner, tile, 0), axis=1, keepdims=True)
            picked.append(jnp.where(column == rows, 1.0, 0.0))
        return jnp.concatenate(picked, axis=0).astype(jnp.bfloat16)

    hot_own = hot(me * 2 + rep)
    hot_other = hot((me ^ 1) * 2 + rep)
    got_other = jnp.dot(hot_other, other[...], preferred_element_type=jnp.float32)
    got_own = jnp.dot(hot_own, own[...], preferred_element_type=jnp.float32)
    for m in range(count + len(pieces)):
        part = slice(m * slots, (m + 1) * slots)
        value = jnp.concatenate([got_own[part], got_other[part]], axis=0).astype(jnp.bfloat16)
        if m < count:
            plane[m * 2 * slots:(m + 1) * 2 * slots, :] = value
        else:
            pieces[m - count][...] = value


def pack_kernel(layouts, *refs):
    ins, outs = refs[:-len(layouts)], refs[-len(layouts):]
    for layout, out in zip(layouts, outs):
        at = 0
        for which, first, rows in layout:
            out[at:at + rows, :] = ins[which][first:first + rows, :]
            at += rows


def pack(layouts, *arrays):
    shapes = [
        jax.ShapeDtypeStruct((sum(rows for _, _, rows in layout), arrays[0].shape[1]), arrays[0].dtype)
        for layout in layouts
    ]
    size = sum(shape.size for shape in shapes)
    return pl.pallas_call(
        functools.partial(pack_kernel, layouts),
        out_shape=shapes,
        in_specs=[WHOLE] * len(arrays),
        out_specs=[WHOLE] * len(layouts),
        compiler_params=budget(*shapes, *arrays),
        cost_estimate=pl.CostEstimate(flops=size, bytes_accessed=4 * size, transcendentals=0),
    )(*arrays)


def stack(counts, refs, out):
    at = 0
    for rows, ref in zip(counts, refs):
        out[at:at + rows, :] = ref[:rows, :]
        at += rows


def scored(queries, rows):
    return 50.0 * lax.dot_general(
        queries[...], rows[...], (((1,), (1,)), ((), ())), preferred_element_type=jnp.float32
    )


def early_kernel(counts, queries, *refs):
    *batches, scores_out, rows = refs
    stack(counts, batches, rows)
    scores_out[...] = scored(queries, rows)


def lookup(index, values):
    total = jnp.zeros_like(index)
    for i, value in enumerate(values):
        total = jnp.where(index == i, value, total)
    return total


def score_kernel(
    counts, passages, columns, slots, meta, hard_counts, queries, positive, scores_ref, *refs
):
    *batches, out_1, out_2, rows, send_out = refs
    batches = batches[-passages:] + batches[:-passages]
    me, rep = meta[0], meta[1]
    stack(counts, batches, rows)
    side = send_out.shape[0]
    block = side // len(columns[0][0])
    blocks = [scores_ref[...], scored(queries, rows)]
    wanted = jnp.broadcast_to(positive[...].astype(jnp.float32), (8, positive.shape[1]))
    wanted = jnp.transpose(wanted)[:, :1]
    onehots = []
    for i, (order, places) in enumerate(columns):
        lane = lax.broadcasted_iota(jnp.int32, (1, blocks[i].shape[1]), 1)
        passage = lane < side
        ids = (lookup(lane // block, order) * block + lane % block) ^ (me * block)
        spot = jnp.where(passage, 0, lane - side)
        owner = lookup(spot // (2 * slots), [4 * m + p for m, p in places])
        owner = (owner + spot // slots % 2 * 2) ^ (me * 2 + rep)
        taken = lookup(owner, [hard_counts[0, o] for o in range(hard_counts.shape[1])])
        live = passage | (spot % slots < taken)
        onehots.append(
            jnp.where((wanted == ids.astype(jnp.float32)) & passage, 1.0, 0.0)
        )
        blocks[i] = jnp.where(live, blocks[i], -jnp.inf)
    tops = [jnp.max(value, axis=1, keepdims=True) for value in blocks]
    row_top = jnp.maximum(tops[0], tops[1])
    sums = [jnp.sum(jnp.exp(value - row_top), axis=1, keepdims=True) for value in blocks]
    log_total = row_top + jnp.log(sums[0] + sums[1])
    weights = [
        (jnp.exp(value - log_total) - onehot).astype(jnp.bfloat16)
        for value, onehot in zip(blocks, onehots)
    ]
    hit = sum(
        jnp.sum(jnp.where(onehot > 0, value, 0.0), axis=1, keepdims=True)
        for value, onehot in zip(blocks, onehots)
    )
    project(send_out, weights[1][:, :side], queries, meta[1], jnp.sum(log_total - hit))
    out_1[...] = weights[0]
    out_2[...] = weights[1]


def project(out, weights, queries, rep, loss):
    half = queries.shape[1] // 2
    for i, side in enumerate((rep, 1 - rep)):
        product = lax.dot_general(
            weights, queries[:, pl.ds(pl.multiple_of(side * half, half), half)],
            (((0,), (0,)), ((), ())), preferred_element_type=jnp.float32,
        )
        at = i * (half + LOSS)
        out[:, at:at + half] = 50.0 * product
        out[:, at + half:at + half + LOSS] = jnp.full((out.shape[0], LOSS), loss, jnp.float32)


def keep_kernel(meta, weights, queries, send, out):
    half = queries.shape[1] // 2
    project(
        out, weights[:, :out.shape[0]], queries, meta[1], send[0:1, half:half + 1]
    )


def first_sum(kept, sent, own, to_x, to_y, to_xy):
    rows, columns = own.shape
    half = columns - LOSS
    lanes = lax.broadcasted_iota(jnp.int32, (rows, LOSS), 1)
    for out, down, across in ((own, 0, 0), (to_x, 1, 0), (to_y, 0, 1), (to_xy, 1, 1)):
        at = pl.ds(down * rows, rows)
        data = pl.ds(across * columns, half)
        out[:, :half] = (kept[at, data] + sent[at, data]).astype(out.dtype)
        tile = pl.ds(across * columns + half, LOSS)
        loss = kept[at, tile] + sent[at, tile]
        high = loss.astype(jnp.bfloat16).astype(jnp.float32)
        out[:, half:] = jnp.where(lanes < LOSS // 2, high, loss - high).astype(out.dtype)


def second_sum(own, from_x, from_y, from_xy, after, *outs):
    rows = outs[0].shape[0]
    for i, out in enumerate(outs):
        at = pl.ds(i * rows, rows)
        out[...] = (own[at] + from_x[at].astype(jnp.float32)) + (
            from_y[at].astype(jnp.float32) + from_xy[at].astype(jnp.float32)
        )


def grad_kernel(weights_1, weights_2, rows_1, rows_2, out, done):
    done[...] = jnp.zeros(done.shape, done.dtype)
    out[...] = 50.0 * (
        jnp.dot(weights_1[...], rows_1[...], preferred_element_type=jnp.float32)
        + jnp.dot(weights_2[...], rows_2[...], preferred_element_type=jnp.float32)
    )


def shards(queries, passages, index_rows, positive, hard_rows, hard_counts):
    loop = lax.axis_size("loop")
    reps = lax.axis_size("rep")
    me = lax.axis_index("loop").astype(jnp.int32)
    rep = lax.axis_index("rep").astype(jnp.int32)
    count, width = queries.shape
    block = passages.shape[0]
    owners, slots = hard_rows.shape[1:]
    half = width // 2
    chips = loop // 2
    meta = jnp.stack([me, rep])
    both = ("loop", "rep")

    other_rows = exchange(index_rows, ("loop",), 1)
    rest = loop // 4
    wanted = jnp.transpose(hard_rows, (0, 2, 1)).reshape(slots, owners)
    asked, = pack([[(0, 0, slots), (1, 0, slots)]], wanted, exchange(wanted, ("loop",), 2))
    asked = [asked] + [exchange(asked, ("loop",), 4 * k) for k in range(1, rest)]
    own_rows, = pack([[(0, 0, index_rows.shape[0])]], index_rows)

    bits = [loop // 2 >> i for i in range(loop.bit_length() - 4)] + [4, 2, 1]
    orders = [0]
    for bit in bits:
        orders = orders + [o | bit for o in orders]
    for bit in bits[:-4]:
        passages = jnp.concatenate([passages, exchange(passages, ("loop",), bit)], axis=0)
    passages_z = exchange(passages, ("loop",), bits[-4])

    depth = 2 * slots
    have = 2 * passages.shape[0]
    top = chips // 2
    outs = [jax.ShapeDtypeStruct((top * depth, width), jnp.bfloat16)]
    outs += [jax.ShapeDtypeStruct((depth, width), jnp.bfloat16)] * top
    known = [passages, passages_z]
    plane, *sends = pl.pallas_call(
        functools.partial(pick_rows, top, rest),
        out_shape=outs,
        in_specs=[SCALARS] + [WHOLE] * (3 + rest),
        out_specs=[WHOLE] * (1 + top),
        compiler_params=budget(index_rows, index_rows, *outs, *outs),
        cost_estimate=pl.CostEstimate(
            flops=4 * chips * slots * index_rows.shape[0] * width,
            bytes_accessed=3 * index_rows.size * 2, transcendentals=0,
        ),
    )(meta, other_rows, own_rows, passages_z, *asked)

    def send(m, value):
        return exchange(value, ("loop",), 2 * m)

    def over(value):
        return exchange(value, ("rep",), 1)

    def cut(arrays, *pieces):
        return [
            (next(i for i, a in enumerate(arrays) if a is array), first, rows)
            for array, first, rows in pieces
        ]

    half_top = top // 2
    inner, outer = range(1, half_top + 1), range(half_top + 1, top)
    opposite_plane = over(plane)
    middle_masks, late_masks = range(top + 1, chips, 2), range(top, chips, 2)
    sends = dict(zip(range(top, chips), sends))
    middle = [send(m, sends[m]) for m in middle_masks]
    held_back = [sends[m] for m in late_masks]
    known += [exchange(value, ("loop",), 4) for value in known]

    arrays = [plane, opposite_plane, *middle, *known, *held_back]
    quad = [(value, 0, value.shape[0]) for value in known]
    batch, *going = pack(
        [cut(arrays, *[(value, 0, depth) for value in middle])]
        + [
            cut(arrays, (plane, m * depth, depth), (opposite_plane, m * depth, depth),
                *(quad if m == 1 else []))
            for m in inner
        ]
        + [cut(arrays, (value, 0, depth)) for value in held_back],
        *arrays,
    )
    near_batch, far_batch = batch, over(batch)
    came = [send(m, value) for m, value in zip(inner, going)]
    late = [send(m, value) for m, value in zip(late_masks, going[len(inner):])]

    arrays = [plane, opposite_plane, going[0], *late, *came]
    batch, *pair_and_going = pack(
        [cut(arrays, *[(value, 0, depth) for value in late]),
         cut(arrays, (going[0], 2 * depth, 2 * have)),
         cut(arrays, (came[0], 2 * depth, 2 * have))]
        + [
            cut(arrays, (plane, m * depth, depth), (opposite_plane, m * depth, depth))
            for m in outer
        ],
        *arrays, far_batch,
    )
    pair, going = pair_and_going[:2], pair_and_going[2:]
    last = [send(m, value) for m, value in zip(outer, going)] + [over(batch)]
    other_pair = [exchange(value, ("loop",), 1) for value in pair]

    first_rows = [(value, 2 * have) for value in pair]
    first_rows += [(plane, depth), (opposite_plane, depth)]
    first_rows += [(value, 2 * depth) for value in came]
    first_rows += [(value, value.shape[0]) for value in (near_batch, far_batch, batch)]
    last_rows = [(value, value.shape[0]) for value in (*other_pair, *last)]
    first_places = [(m, p) for m in (0, *inner) for p in range(2)]
    first_places += [(m, p) for p in range(2) for m in middle_masks]
    first_places += [(m, 0) for m in late_masks]
    last_places = [(m, p) for m in outer for p in range(2)] + [(m, 1) for m in late_masks]
    side = loop * block // 2
    columns = (
        (tuple(orders[:loop // 2]), tuple(first_places)),
        (tuple(orders[loop // 2:]), tuple(last_places)),
    )
    first_counts = tuple(n for _, n in first_rows)
    last_counts = tuple(n for _, n in last_rows)

    rows = loop * block
    rows_1 = jax.ShapeDtypeStruct((sum(first_counts), width), jnp.bfloat16)
    rows_2 = jax.ShapeDtypeStruct((sum(last_counts), width), jnp.bfloat16)
    payload = jax.ShapeDtypeStruct((side, width + 2 * LOSS), jnp.float32)
    scores, rows_1 = pl.pallas_call(
        functools.partial(early_kernel, first_counts),
        out_shape=[jax.ShapeDtypeStruct((count, rows_1.shape[0]), jnp.float32), rows_1],
        in_specs=[WHOLE] * (1 + len(first_rows)),
        out_specs=[WHOLE] * 2,
        compiler_params=budget(queries, rows_1, rows_1),
        cost_estimate=pl.CostEstimate(
            flops=2 * count * rows_1.size,
            bytes_accessed=2 * (queries.size + 2 * rows_1.size), transcendentals=0,
        ),
    )(queries, *[value for value, _ in first_rows])
    weights_1, weights_2, rows_2, send_part = pl.pallas_call(
        functools.partial(score_kernel, last_counts, len(other_pair), columns, slots),
        out_shape=[
            jax.ShapeDtypeStruct((count, rows_1.shape[0]), jnp.bfloat16),
            jax.ShapeDtypeStruct((count, rows_2.shape[0]), jnp.bfloat16),
            rows_2, payload,
        ],
        in_specs=[SCALARS] * 2 + [WHOLE] * (3 + len(last_rows)),
        out_specs=[WHOLE] * 4,
        compiler_params=budget(queries, rows_2, rows_2, payload, payload),
        cost_estimate=pl.CostEstimate(
            flops=2 * count * (rows_2.size + payload.size),
            bytes_accessed=2 * (queries.size + 2 * rows_2.size) + 4 * payload.size,
            transcendentals=2 * count * (rows_1.shape[0] + rows_2.shape[0]),
        ),
    )(
        meta, hard_counts, queries, positive.reshape(1, count), scores,
        *last, *other_pair,
    )

    sent = exchange(send_part, ("loop",), 1)
    kept = pl.pallas_call(
        keep_kernel,
        out_shape=jax.ShapeDtypeStruct((rows // 2, width + 2 * LOSS), jnp.float32),
        in_specs=[SCALARS] + [WHOLE] * 3,
        out_specs=WHOLE,
        compiler_params=budget(queries, payload, payload),
        cost_estimate=pl.CostEstimate(
            flops=count * rows * width,
            bytes_accessed=2 * count * width + 2 * rows * width, transcendentals=0,
        ),
    )(meta, weights_1, queries, send_part)
    query_grad, done = pl.pallas_call(
        grad_kernel,
        out_shape=[
            jax.ShapeDtypeStruct((count, width), jnp.float32),
            jax.ShapeDtypeStruct((8, 128), jnp.float32),
        ],
        in_specs=[WHOLE] * 4,
        out_specs=[WHOLE] * 2,
        compiler_params=budget(queries, queries, rows_1, rows_2),
        cost_estimate=pl.CostEstimate(
            flops=2 * count * (rows_1.size + rows_2.size),
            bytes_accessed=2 * (rows_1.size + rows_2.size) + 4 * count * width,
            transcendentals=0,
        ),
    )(weights_1, weights_2, rows_1, rows_2)
    part = half + LOSS
    quarter = rows // 4
    first = jax.ShapeDtypeStruct((quarter, part), jnp.float32)
    short = jax.ShapeDtypeStruct(first.shape, jnp.bfloat16)
    own, *going = pl.pallas_call(
        first_sum,
        out_shape=[first, short, first, short],
        in_specs=[WHOLE] * 2,
        out_specs=[WHOLE] * 4,
        compiler_params=budget(payload, payload, payload),
        cost_estimate=pl.CostEstimate(
            flops=payload.size, bytes_accessed=12 * payload.size, transcendentals=0
        ),
    )(kept, sent)
    came = [exchange(value, both, mask) for value, mask in zip(going, (4, 1, 5))]
    second = jax.ShapeDtypeStruct((block, part), jnp.float32)
    total, *going = pl.pallas_call(
        second_sum,
        out_shape=[second] * rest,
        in_specs=[WHOLE] * 5,
        out_specs=[WHOLE] * rest,
        compiler_params=budget(payload, payload),
        cost_estimate=pl.CostEstimate(
            flops=4 * first.size, bytes_accessed=20 * first.size, transcendentals=0
        ),
    )(own, *came, done)
    for value, order in zip(going, orders[1:rest]):
        total = total + exchange(value, ("loop",), order)
    mean_loss = (total[0, half] + total[0, half + LOSS // 2]) / (count * loop * reps)
    total = total[:, :half]
    opposite = exchange(total, ("rep",), 1)
    passage_grad = jnp.where(
        rep == 0,
        jnp.concatenate([total, opposite], axis=1),
        jnp.concatenate([opposite, total], axis=1),
    )

    return (query_grad, passage_grad, mean_loss)


def solution(mesh):
    placed = (
        P(("loop", "rep"), None),
        P("loop", None),
        P(("loop", "rep"), None),
        P(("loop", "rep")),
        P("loop", None, None),
        P("loop", None),
    )
    return jax.shard_map(
        shards,
        mesh=mesh,
        in_specs=placed,
        out_specs=(P(("loop", "rep"), None), P("loop", None), P()),
        check_vma=False,
    )
```

```python
import functools

import jax
import jax.numpy as jnp
from jax import lax
from jax.experimental import pallas as pl
from jax.experimental.pallas import tpu as pltpu
from jax.sharding import PartitionSpec as P


def budget(*arrays):
    total = sum(a.size * a.dtype.itemsize for a in arrays)
    return pltpu.CompilerParams(vmem_limit_bytes=total + total // 4 + 6 * 1024 * 1024)


WHOLE = pl.BlockSpec(memory_space=pltpu.VMEM)
SCALARS = pl.BlockSpec(memory_space=pltpu.SMEM)
LOSS = 128


def exchange(value, axes, mask):
    size = 1
    for axis in axes:
        size *= lax.axis_size(axis)
    return lax.ppermute(value, axes, [(i, i ^ mask) for i in range(size)])


def pick_rows(count, reach, meta, other, own, after, *refs):
    asked, (plane, *pieces) = refs[:reach], refs[reach:]
    me, rep = meta[0], meta[1]
    owners = asked[0].shape[1]
    slots = plane.shape[0] // (2 * count)
    lanes = lax.broadcasted_iota(jnp.int32, (slots, owners), 1)
    rows = lax.broadcasted_iota(jnp.int32, (slots, own.shape[0]), 1)

    def hot(owner):
        picked = []
        for m in range(count + len(pieces)):
            at = m % 2 * slots
            tile = asked[m // 2][at:at + slots, :]
            column = jnp.sum(jnp.where(lanes == owner, tile, 0), axis=1, keepdims=True)
            picked.append(jnp.where(column == rows, 1.0, 0.0))
        return jnp.concatenate(picked, axis=0).astype(jnp.bfloat16)

    hot_own = hot(me * 2 + rep)
    hot_other = hot((me ^ 1) * 2 + rep)
    got_other = jnp.dot(hot_other, other[...], preferred_element_type=jnp.float32)
    got_own = jnp.dot(hot_own, own[...], preferred_element_type=jnp.float32)
    for m in range(count + len(pieces)):
        part = slice(m * slots, (m + 1) * slots)
        value = jnp.concatenate([got_own[part], got_other[part]], axis=0).astype(jnp.bfloat16)
        if m < count:
            plane[m * 2 * slots:(m + 1) * 2 * slots, :] = value
        else:
            pieces[m - count][...] = value


def pack_kernel(layouts, *refs):
    ins, outs = refs[:-len(layouts)], refs[-len(layouts):]
    for layout, out in zip(layouts, outs):
        at = 0
        for which, first, rows in layout:
            out[at:at + rows, :] = ins[which][first:first + rows, :]
            at += rows


def pack(layouts, *arrays):
    shapes = [
        jax.ShapeDtypeStruct((sum(rows for _, _, rows in layout), arrays[0].shape[1]), arrays[0].dtype)
        for layout in layouts
    ]
    size = sum(shape.size for shape in shapes)
    return pl.pallas_call(
        functools.partial(pack_kernel, layouts),
        out_shape=shapes,
        in_specs=[WHOLE] * len(arrays),
        out_specs=[WHOLE] * len(layouts),
        compiler_params=budget(*shapes, *arrays),
        cost_estimate=pl.CostEstimate(flops=size, bytes_accessed=4 * size, transcendentals=0),
    )(*arrays)


def stack(counts, refs, out):
    at = 0
    for rows, ref in zip(counts, refs):
        out[at:at + rows, :] = ref[:rows, :]
        at += rows


def scored(queries, rows):
    return 50.0 * lax.dot_general(
        queries[...], rows[...], (((1,), (1,)), ((), ())), preferred_element_type=jnp.float32
    )


def early_kernel(counts, queries, *refs):
    *batches, scores_out, rows = refs
    stack(counts, batches, rows)
    scores_out[...] = scored(queries, rows)


def lookup(index, values):
    total = jnp.zeros_like(index)
    for i, value in enumerate(values):
        total = jnp.where(index == i, value, total)
    return total


def score_kernel(
    counts, passages, columns, slots, meta, hard_counts, queries, positive, scores_ref, *refs
):
    *batches, out_1, out_2, rows, send_out = refs
    batches = batches[-passages:] + batches[:-passages]
    me, rep = meta[0], meta[1]
    stack(counts, batches, rows)
    side = send_out.shape[0]
    block = side // len(columns[0][0])
    blocks = [scores_ref[...], scored(queries, rows)]
    wanted = jnp.broadcast_to(positive[...].astype(jnp.float32), (8, positive.shape[1]))
    wanted = jnp.transpose(wanted)[:, :1]
    onehots = []
    for i, (order, places) in enumerate(columns):
        lane = lax.broadcasted_iota(jnp.int32, (1, blocks[i].shape[1]), 1)
        passage = lane < side
        ids = (lookup(lane // block, order) * block + lane % block) ^ (me * block)
        spot = jnp.where(passage, 0, lane - side)
        owner = lookup(spot // (2 * slots), [4 * m + p for m, p in places])
        owner = (owner + spot // slots % 2 * 2) ^ (me * 2 + rep)
        taken = lookup(owner, [hard_counts[0, o] for o in range(hard_counts.shape[1])])
        live = passage | (spot % slots < taken)
        onehots.append(
            jnp.where((wanted == ids.astype(jnp.float32)) & passage, 1.0, 0.0)
        )
        blocks[i] = jnp.where(live, blocks[i], -jnp.inf)
    tops = [jnp.max(value, axis=1, keepdims=True) for value in blocks]
    row_top = jnp.maximum(tops[0], tops[1])
    sums = [jnp.sum(jnp.exp(value - row_top), axis=1, keepdims=True) for value in blocks]
    log_total = row_top + jnp.log(sums[0] + sums[1])
    weights = [
        (jnp.exp(value - log_total) - onehot).astype(jnp.bfloat16)
        for value, onehot in zip(blocks, onehots)
    ]
    hit = sum(
        jnp.sum(jnp.where(onehot > 0, value, 0.0), axis=1, keepdims=True)
        for value, onehot in zip(blocks, onehots)
    )
    project(send_out, weights[1][:, :side], queries, meta[1], jnp.sum(log_total - hit))
    out_1[...] = weights[0]
    out_2[...] = weights[1]


def project(out, weights, queries, rep, loss):
    half = queries.shape[1] // 2
    for i, side in enumerate((rep, 1 - rep)):
        product = lax.dot_general(
            weights, queries[:, pl.ds(pl.multiple_of(side * half, half), half)],
            (((0,), (0,)), ((), ())), preferred_element_type=jnp.float32,
        )
        at = i * (half + LOSS)
        out[:, at:at + half] = 50.0 * product
        out[:, at + half:at + half + LOSS] = jnp.full((out.shape[0], LOSS), loss, jnp.float32)


def keep_kernel(meta, weights, queries, send, out):
    half = queries.shape[1] // 2
    project(
        out, weights[:, :out.shape[0]], queries, meta[1], send[0:1, half:half + 1]
    )


def first_sum(kept, sent, own, to_x, to_y, to_xy):
    rows, columns = own.shape
    half = columns - LOSS
    lanes = lax.broadcasted_iota(jnp.int32, (rows, LOSS), 1)
    for out, down, across in ((own, 0, 0), (to_x, 1, 0), (to_y, 0, 1), (to_xy, 1, 1)):
        at = pl.ds(down * rows, rows)
        data = pl.ds(across * columns, half)
        out[:, :half] = (kept[at, data] + sent[at, data]).astype(out.dtype)
        tile = pl.ds(across * columns + half, LOSS)
        loss = kept[at, tile] + sent[at, tile]
        high = loss.astype(jnp.bfloat16).astype(jnp.float32)
        out[:, half:] = jnp.where(lanes < LOSS // 2, high, loss - high).astype(out.dtype)


def second_sum(own, from_x, from_y, from_xy, after, *outs):
    rows, columns = outs[0].shape
    half = columns - LOSS
    lanes = lax.broadcasted_iota(jnp.int32, (rows, LOSS), 1)
    for i, out in enumerate(outs):
        at = pl.ds(i * rows, rows)
        total = (own[at] + from_x[at]) + (from_y[at] + from_xy[at].astype(jnp.float32))
        if out.dtype == jnp.float32:
            out[...] = total
        else:
            loss = total[:, half:half + 1] + total[:, half + LOSS // 2:half + LOSS // 2 + 1]
            high = loss.astype(jnp.bfloat16).astype(jnp.float32)
            out[:, :half] = total[:, :half].astype(out.dtype)
            out[:, half:] = jnp.where(lanes < LOSS // 2, high, loss - high).astype(out.dtype)


def grad_kernel(weights_1, weights_2, rows_1, rows_2, out, done):
    done[...] = jnp.zeros(done.shape, done.dtype)
    out[...] = 50.0 * (
        jnp.dot(weights_1[...], rows_1[...], preferred_element_type=jnp.float32)
        + jnp.dot(weights_2[...], rows_2[...], preferred_element_type=jnp.float32)
    )


def shards(queries, passages, index_rows, positive, hard_rows, hard_counts):
    loop = lax.axis_size("loop")
    reps = lax.axis_size("rep")
    me = lax.axis_index("loop").astype(jnp.int32)
    rep = lax.axis_index("rep").astype(jnp.int32)
    count, width = queries.shape
    block = passages.shape[0]
    owners, slots = hard_rows.shape[1:]
    half = width // 2
    chips = loop // 2
    meta = jnp.stack([me, rep])
    both = ("loop", "rep")

    other_rows = exchange(index_rows, ("loop",), 1)
    rest = loop // 4
    wanted = jnp.transpose(hard_rows, (0, 2, 1)).reshape(slots, owners)
    neighbour, (own_wanted,) = exchange(wanted, ("loop",), 2), pack([[(0, 0, slots)]], wanted)
    asked, = pack([[(0, 0, slots), (1, 0, slots)]], own_wanted, neighbour)
    asked = [asked] + [exchange(asked, ("loop",), 4 * k) for k in range(1, rest)]
    own_rows, = pack([[(0, 0, index_rows.shape[0])]], index_rows)

    bits = [loop // 2 >> i for i in range(loop.bit_length() - 4)] + [4, 2, 1]
    orders = [0]
    for bit in bits:
        orders = orders + [o | bit for o in orders]
    for bit in bits[:-4]:
        passages = jnp.concatenate([passages, exchange(passages, ("loop",), bit)], axis=0)
    passages_z = exchange(passages, ("loop",), bits[-4])

    depth = 2 * slots
    have = 2 * passages.shape[0]
    top = chips // 2
    outs = [jax.ShapeDtypeStruct((top * depth, width), jnp.bfloat16)]
    outs += [jax.ShapeDtypeStruct((depth, width), jnp.bfloat16)] * top
    known, = pack([[(i, 0, have // 2) for i in range(2)]], passages, passages_z)
    plane, *sends = pl.pallas_call(
        functools.partial(pick_rows, top, rest),
        out_shape=outs,
        in_specs=[SCALARS] + [WHOLE] * (3 + rest),
        out_specs=[WHOLE] * (1 + top),
        compiler_params=budget(index_rows, index_rows, *outs, *outs),
        cost_estimate=pl.CostEstimate(
            flops=4 * chips * slots * index_rows.shape[0] * width,
            bytes_accessed=3 * index_rows.size * 2, transcendentals=0,
        ),
    )(meta, other_rows, own_rows, passages_z, *asked)

    def send(m, value):
        return exchange(value, ("loop",), 2 * m)

    def over(value):
        return exchange(value, ("rep",), 1)

    def cut(arrays, *pieces):
        return [
            (next(i for i, a in enumerate(arrays) if a is array), first, rows)
            for array, first, rows in pieces
        ]

    half_top = top // 2
    inner, outer = range(1, half_top + 1), range(half_top + 1, top)
    opposite_plane = over(plane)
    middle_masks, late_masks = range(top + 1, chips, 2), range(top, chips, 2)
    sends = dict(zip(range(top, chips), sends))
    middle = [send(m, sends[m]) for m in middle_masks]
    held_back = [sends[m] for m in late_masks]
    known = [known, exchange(known, ("loop",), 4)]

    arrays = [plane, opposite_plane, *middle, *known, *held_back]
    quad = [(value, 0, value.shape[0]) for value in known]
    batch, *going = pack(
        [cut(arrays, *[(value, 0, depth) for value in middle])]
        + [
            cut(arrays, (plane, m * depth, depth), (opposite_plane, m * depth, depth),
                *(quad if m == 1 else []))
            for m in inner
        ]
        + [cut(arrays, (value, 0, depth)) for value in held_back],
        *arrays,
    )
    near_batch, far_batch = batch, over(batch)
    came = [send(m, value) for m, value in zip(inner, going)]
    late = [send(m, value) for m, value in zip(late_masks, going[len(inner):])]

    arrays = [plane, opposite_plane, going[0], *late, *came]
    batch, *pair_and_going = pack(
        [cut(arrays, *[(value, 0, depth) for value in late]),
         cut(arrays, (going[0], 2 * depth, 2 * have)),
         cut(arrays, (came[0], 2 * depth, 2 * have))]
        + [
            cut(arrays, (plane, m * depth, depth), (opposite_plane, m * depth, depth))
            for m in outer
        ],
        *arrays, far_batch,
    )
    pair, going = pair_and_going[:2], pair_and_going[2:]
    last = [send(m, value) for m, value in zip(outer, going)] + [over(batch)]
    other_pair = [exchange(value, ("loop",), 1) for value in pair]

    first_rows = [(value, 2 * have) for value in pair]
    first_rows += [(plane, depth), (opposite_plane, depth)]
    first_rows += [(value, 2 * depth) for value in came]
    first_rows += [(value, value.shape[0]) for value in (near_batch, far_batch, batch)]
    last_rows = [(value, value.shape[0]) for value in (*other_pair, *last)]
    first_places = [(m, p) for m in (0, *inner) for p in range(2)]
    first_places += [(m, p) for p in range(2) for m in middle_masks]
    first_places += [(m, 0) for m in late_masks]
    last_places = [(m, p) for m in outer for p in range(2)] + [(m, 1) for m in late_masks]
    side = loop * block // 2
    columns = (
        (tuple(orders[:loop // 2]), tuple(first_places)),
        (tuple(orders[loop // 2:]), tuple(last_places)),
    )
    first_counts = tuple(n for _, n in first_rows)
    last_counts = tuple(n for _, n in last_rows)

    rows = loop * block
    rows_1 = jax.ShapeDtypeStruct((sum(first_counts), width), jnp.bfloat16)
    rows_2 = jax.ShapeDtypeStruct((sum(last_counts), width), jnp.bfloat16)
    payload = jax.ShapeDtypeStruct((side, width + 2 * LOSS), jnp.float32)
    scores, rows_1 = pl.pallas_call(
        functools.partial(early_kernel, first_counts),
        out_shape=[jax.ShapeDtypeStruct((count, rows_1.shape[0]), jnp.float32), rows_1],
        in_specs=[WHOLE] * (1 + len(first_rows)),
        out_specs=[WHOLE] * 2,
        compiler_params=budget(queries, rows_1, rows_1),
        cost_estimate=pl.CostEstimate(
            flops=2 * count * rows_1.size,
            bytes_accessed=2 * (queries.size + 2 * rows_1.size), transcendentals=0,
        ),
    )(queries, *[value for value, _ in first_rows])
    weights_1, weights_2, rows_2, send_part = pl.pallas_call(
        functools.partial(score_kernel, last_counts, len(other_pair), columns, slots),
        out_shape=[
            jax.ShapeDtypeStruct((count, rows_1.shape[0]), jnp.bfloat16),
            jax.ShapeDtypeStruct((count, rows_2.shape[0]), jnp.bfloat16),
            rows_2, payload,
        ],
        in_specs=[SCALARS] * 2 + [WHOLE] * (3 + len(last_rows)),
        out_specs=[WHOLE] * 4,
        compiler_params=budget(queries, rows_2, rows_2, payload, payload),
        cost_estimate=pl.CostEstimate(
            flops=2 * count * (rows_2.size + payload.size),
            bytes_accessed=2 * (queries.size + 2 * rows_2.size) + 4 * payload.size,
            transcendentals=2 * count * (rows_1.shape[0] + rows_2.shape[0]),
        ),
    )(
        meta, hard_counts, queries, positive.reshape(1, count), scores,
        *last, *other_pair,
    )

    sent = exchange(send_part, ("loop",), 1)
    kept = pl.pallas_call(
        keep_kernel,
        out_shape=jax.ShapeDtypeStruct((rows // 2, width + 2 * LOSS), jnp.float32),
        in_specs=[SCALARS] + [WHOLE] * 3,
        out_specs=WHOLE,
        compiler_params=budget(queries, payload, payload),
        cost_estimate=pl.CostEstimate(
            flops=count * rows * width,
            bytes_accessed=2 * count * width + 2 * rows * width, transcendentals=0,
        ),
    )(meta, weights_1, queries, send_part)
    query_grad, done = pl.pallas_call(
        grad_kernel,
        out_shape=[
            jax.ShapeDtypeStruct((count, width), jnp.float32),
            jax.ShapeDtypeStruct((8, 128), jnp.float32),
        ],
        in_specs=[WHOLE] * 4,
        out_specs=[WHOLE] * 2,
        compiler_params=budget(queries, queries, rows_1, rows_2),
        cost_estimate=pl.CostEstimate(
            flops=2 * count * (rows_1.size + rows_2.size),
            bytes_accessed=2 * (rows_1.size + rows_2.size) + 4 * count * width,
            transcendentals=0,
        ),
    )(weights_1, weights_2, rows_1, rows_2)
    part = half + LOSS
    quarter = rows // 4
    first = jax.ShapeDtypeStruct((quarter, part), jnp.float32)
    short = jax.ShapeDtypeStruct(first.shape, jnp.bfloat16)
    own, *going = pl.pallas_call(
        first_sum,
        out_shape=[first, first, first, short],
        in_specs=[WHOLE] * 2,
        out_specs=[WHOLE] * 4,
        compiler_params=budget(payload, payload, payload),
        cost_estimate=pl.CostEstimate(
            flops=payload.size, bytes_accessed=12 * payload.size, transcendentals=0
        ),
    )(kept, sent)
    came = [exchange(value, both, mask) for value, mask in zip(going, (4, 1, 5))]
    second = jax.ShapeDtypeStruct((block, part), jnp.float32)
    total, *going = pl.pallas_call(
        second_sum,
        out_shape=[second] * (rest - 1) + [jax.ShapeDtypeStruct(second.shape, jnp.bfloat16)],
        in_specs=[WHOLE] * 5,
        out_specs=[WHOLE] * rest,
        compiler_params=budget(payload, payload),
        cost_estimate=pl.CostEstimate(
            flops=4 * first.size, bytes_accessed=20 * first.size, transcendentals=0
        ),
    )(own, *came, done)
    for value, order in zip(going, orders[1:rest]):
        total = total + exchange(value, ("loop",), order).astype(jnp.float32)
    mean_loss = (total[0, half] + total[0, half + LOSS // 2]) / (count * loop * reps)
    total = total[:, :half]
    opposite = exchange(total, ("rep",), 1)
    passage_grad = jnp.where(
        rep == 0,
        jnp.concatenate([total, opposite], axis=1),
        jnp.concatenate([opposite, total], axis=1),
    )

    return (query_grad, passage_grad, mean_loss)


def solution(mesh):
    placed = (
        P(("loop", "rep"), None),
        P("loop", None),
        P(("loop", "rep"), None),
        P(("loop", "rep")),
        P("loop", None, None),
        P("loop", None),
    )
    return jax.shard_map(
        shards,
        mesh=mesh,
        in_specs=placed,
        out_specs=(P(("loop", "rep"), None), P("loop", None), P()),
        check_vma=False,
    )
```

```python
import functools

import jax
import jax.numpy as jnp
from jax import lax
from jax.experimental import pallas as pl
from jax.experimental.pallas import tpu as pltpu
from jax.sharding import PartitionSpec as P


def budget(*arrays):
    total = sum(a.size * a.dtype.itemsize for a in arrays)
    return pltpu.CompilerParams(vmem_limit_bytes=total + total // 4 + 6 * 1024 * 1024)


WHOLE = pl.BlockSpec(memory_space=pltpu.VMEM)
SCALARS = pl.BlockSpec(memory_space=pltpu.SMEM)
LOSS = 128


def exchange(value, axes, mask):
    size = 1
    for axis in axes:
        size *= lax.axis_size(axis)
    return lax.ppermute(value, axes, [(i, i ^ mask) for i in range(size)])


def pick_rows(count, reach, meta, other, own, after, *refs):
    asked, (plane, *pieces) = refs[:reach], refs[reach:]
    me, rep = meta[0], meta[1]
    owners = asked[0].shape[1]
    slots = plane.shape[0] // (2 * count)
    lanes = lax.broadcasted_iota(jnp.int32, (slots, owners), 1)
    rows = lax.broadcasted_iota(jnp.int32, (slots, own.shape[0]), 1)

    def hot(owner):
        picked = []
        for m in range(count + len(pieces)):
            at = m % 2 * slots
            tile = asked[m // 2][at:at + slots, :]
            column = jnp.sum(jnp.where(lanes == owner, tile, 0), axis=1, keepdims=True)
            picked.append(jnp.where(column == rows, 1.0, 0.0))
        return jnp.concatenate(picked, axis=0).astype(jnp.bfloat16)

    hot_own = hot(me * 2 + rep)
    hot_other = hot((me ^ 1) * 2 + rep)
    got_other = jnp.dot(hot_other, other[...], preferred_element_type=jnp.float32)
    got_own = jnp.dot(hot_own, own[...], preferred_element_type=jnp.float32)
    for m in range(count + len(pieces)):
        part = slice(m * slots, (m + 1) * slots)
        value = jnp.concatenate([got_own[part], got_other[part]], axis=0).astype(jnp.bfloat16)
        if m < count:
            plane[m * 2 * slots:(m + 1) * 2 * slots, :] = value
        else:
            pieces[m - count][...] = value


def pack_kernel(layouts, *refs):
    ins, outs = refs[:-len(layouts)], refs[-len(layouts):]
    for layout, out in zip(layouts, outs):
        at = 0
        for which, first, rows in layout:
            out[at:at + rows, :] = ins[which][first:first + rows, :]
            at += rows


def pack(layouts, *arrays):
    shapes = [
        jax.ShapeDtypeStruct((sum(rows for _, _, rows in layout), arrays[0].shape[1]), arrays[0].dtype)
        for layout in layouts
    ]
    size = sum(shape.size for shape in shapes)
    return pl.pallas_call(
        functools.partial(pack_kernel, layouts),
        out_shape=shapes,
        in_specs=[WHOLE] * len(arrays),
        out_specs=[WHOLE] * len(layouts),
        compiler_params=budget(*shapes, *arrays),
        cost_estimate=pl.CostEstimate(flops=size, bytes_accessed=4 * size, transcendentals=0),
    )(*arrays)


def stack(counts, refs, out):
    at = 0
    for rows, ref in zip(counts, refs):
        out[at:at + rows, :] = ref[:rows, :]
        at += rows


def scored(queries, rows):
    return 50.0 * lax.dot_general(
        queries[...], rows[...], (((1,), (1,)), ((), ())), preferred_element_type=jnp.float32
    )


def early_kernel(counts, queries, *refs):
    *batches, scores_out, rows = refs
    stack(counts, batches, rows)
    scores_out[...] = scored(queries, rows)


def lookup(index, values):
    total = jnp.zeros_like(index)
    for i, value in enumerate(values):
        total = jnp.where(index == i, value, total)
    return total


def score_kernel(
    counts, passages, columns, slots, meta, hard_counts, queries, positive, scores_ref, *refs
):
    *batches, out_1, out_2, rows, send_out = refs
    batches = batches[-passages:] + batches[:-passages]
    me, rep = meta[0], meta[1]
    stack(counts, batches, rows)
    side = send_out.shape[0]
    block = side // len(columns[0][0])
    blocks = [scores_ref[...], scored(queries, rows)]
    wanted = jnp.broadcast_to(positive[...].astype(jnp.float32), (8, positive.shape[1]))
    wanted = jnp.transpose(wanted)[:, :1]
    onehots = []
    for i, (order, places) in enumerate(columns):
        lane = lax.broadcasted_iota(jnp.int32, (1, blocks[i].shape[1]), 1)
        passage = lane < side
        ids = (lookup(lane // block, order) * block + lane % block) ^ (me * block)
        spot = jnp.where(passage, 0, lane - side)
        owner = lookup(spot // (2 * slots), [4 * m + p for m, p in places])
        owner = (owner + spot // slots % 2 * 2) ^ (me * 2 + rep)
        taken = lookup(owner, [hard_counts[0, o] for o in range(hard_counts.shape[1])])
        live = passage | (spot % slots < taken)
        onehots.append(
            jnp.where((wanted == ids.astype(jnp.float32)) & passage, 1.0, 0.0)
        )
        blocks[i] = jnp.where(live, blocks[i], -jnp.inf)
    tops = [jnp.max(value, axis=1, keepdims=True) for value in blocks]
    row_top = jnp.maximum(tops[0], tops[1])
    sums = [jnp.sum(jnp.exp(value - row_top), axis=1, keepdims=True) for value in blocks]
    log_total = row_top + jnp.log(sums[0] + sums[1])
    weights = [
        (jnp.exp(value - log_total) - onehot).astype(jnp.bfloat16)
        for value, onehot in zip(blocks, onehots)
    ]
    hit = sum(
        jnp.sum(jnp.where(onehot > 0, value, 0.0), axis=1, keepdims=True)
        for value, onehot in zip(blocks, onehots)
    )
    project(send_out, weights[1][:, :side], queries, meta[1], jnp.sum(log_total - hit))
    out_1[...] = weights[0]
    out_2[...] = weights[1]


def project(out, weights, queries, rep, loss):
    half = queries.shape[1] // 2
    for i, side in enumerate((rep, 1 - rep)):
        product = lax.dot_general(
            weights, queries[:, pl.ds(pl.multiple_of(side * half, half), half)],
            (((0,), (0,)), ((), ())), preferred_element_type=jnp.float32,
        )
        at = i * (half + LOSS)
        out[:, at:at + half] = 50.0 * product
        out[:, at + half:at + half + LOSS] = jnp.full((out.shape[0], LOSS), loss, jnp.float32)


def keep_kernel(meta, weights, queries, send, out):
    half = queries.shape[1] // 2
    project(
        out, weights[:, :out.shape[0]], queries, meta[1], send[0:1, half:half + 1]
    )


def first_sum(kept, sent, own, to_x, to_y, to_xy):
    rows, columns = own.shape
    half = columns - LOSS
    lanes = lax.broadcasted_iota(jnp.int32, (rows, LOSS), 1)
    for out, down, across in ((own, 0, 0), (to_x, 1, 0), (to_y, 0, 1), (to_xy, 1, 1)):
        at = pl.ds(down * rows, rows)
        data = pl.ds(across * columns, half)
        out[:, :half] = (kept[at, data] + sent[at, data]).astype(out.dtype)
        tile = pl.ds(across * columns + half, LOSS)
        loss = kept[at, tile] + sent[at, tile]
        high = loss.astype(jnp.bfloat16).astype(jnp.float32)
        out[:, half:] = jnp.where(lanes < LOSS // 2, high, loss - high).astype(out.dtype)


def second_sum(own, from_x, from_y, from_xy, after, *outs):
    rows, columns = outs[0].shape
    half = columns - LOSS
    lanes = lax.broadcasted_iota(jnp.int32, (rows, LOSS), 1)
    for i, out in enumerate(outs):
        at = pl.ds(i * rows, rows)
        total = (own[at] + from_x[at]) + (from_y[at] + from_xy[at].astype(jnp.float32))
        if out.dtype == jnp.float32:
            out[...] = total
        else:
            loss = total[:, half:half + 1] + total[:, half + LOSS // 2:half + LOSS // 2 + 1]
            high = loss.astype(jnp.bfloat16).astype(jnp.float32)
            out[:, :half] = total[:, :half].astype(out.dtype)
            out[:, half:] = jnp.where(lanes < LOSS // 2, high, loss - high).astype(out.dtype)


def grad_kernel(weights_1, weights_2, rows_1, rows_2, out, done):
    done[...] = jnp.zeros(done.shape, done.dtype)
    out[...] = 50.0 * (
        jnp.dot(weights_1[...], rows_1[...], preferred_element_type=jnp.float32)
        + jnp.dot(weights_2[...], rows_2[...], preferred_element_type=jnp.float32)
    )


def shards(queries, passages, index_rows, positive, hard_rows, hard_counts):
    loop = lax.axis_size("loop")
    reps = lax.axis_size("rep")
    me = lax.axis_index("loop").astype(jnp.int32)
    rep = lax.axis_index("rep").astype(jnp.int32)
    count, width = queries.shape
    block = passages.shape[0]
    owners, slots = hard_rows.shape[1:]
    half = width // 2
    chips = loop // 2
    meta = jnp.stack([me, rep])
    both = ("loop", "rep")

    other_rows = exchange(index_rows, ("loop",), 1)
    rest = loop // 4
    wanted = jnp.transpose(hard_rows, (0, 2, 1)).reshape(slots, owners)
    neighbour, (own_wanted,) = exchange(wanted, ("loop",), 2), pack([[(0, 0, slots)]], wanted)
    asked, = pack([[(0, 0, slots), (1, 0, slots)]], own_wanted, neighbour)
    asked = [asked] + [exchange(asked, ("loop",), 4 * k) for k in range(1, rest)]
    own_rows, = pack([[(0, 0, index_rows.shape[0])]], index_rows)

    bits = [loop // 2 >> i for i in range(loop.bit_length() - 4)] + [4, 2, 1]
    orders = [0]
    for bit in bits:
        orders = orders + [o | bit for o in orders]
    for bit in bits[:-4]:
        passages = jnp.concatenate([passages, exchange(passages, ("loop",), bit)], axis=0)
    passages_z = exchange(passages, ("loop",), bits[-4])

    depth = 2 * slots
    have = 2 * passages.shape[0]
    top = chips // 2
    outs = [jax.ShapeDtypeStruct((top * depth, width), jnp.bfloat16)]
    outs += [jax.ShapeDtypeStruct((depth, width), jnp.bfloat16)] * top
    known, = pack([[(i, 0, have // 2) for i in range(2)]], passages, passages_z)
    plane, *sends = pl.pallas_call(
        functools.partial(pick_rows, top, rest),
        out_shape=outs,
        in_specs=[SCALARS] + [WHOLE] * (3 + rest),
        out_specs=[WHOLE] * (1 + top),
        compiler_params=budget(index_rows, index_rows, *outs, *outs),
        cost_estimate=pl.CostEstimate(
            flops=4 * chips * slots * index_rows.shape[0] * width,
            bytes_accessed=3 * index_rows.size * 2, transcendentals=0,
        ),
    )(meta, other_rows, own_rows, passages_z, *asked)

    def send(m, value):
        return exchange(value, ("loop",), 2 * m)

    def over(value):
        return exchange(value, ("rep",), 1)

    def cut(arrays, *pieces):
        return [
            (next(i for i, a in enumerate(arrays) if a is array), first, rows)
            for array, first, rows in pieces
        ]

    half_top = top // 2
    inner, outer = range(1, half_top + 1), range(half_top + 1, top)
    opposite_plane = over(plane)
    middle_masks, late_masks = range(top + 1, chips, 2), range(top, chips, 2)
    sends = dict(zip(range(top, chips), sends))
    middle = [send(m, sends[m]) for m in middle_masks]
    held_back = [sends[m] for m in late_masks]
    known = [known, exchange(known, ("loop",), 4)]

    arrays = [plane, opposite_plane, *middle, *known, *held_back]
    quad = [(value, 0, value.shape[0]) for value in known]
    batch, *going = pack(
        [cut(arrays, *[(value, 0, depth) for value in middle])]
        + [
            cut(arrays, (plane, m * depth, depth), (opposite_plane, m * depth, depth),
                *(quad if m == 1 else []))
            for m in inner
        ]
        + [cut(arrays, (value, 0, depth)) for value in held_back],
        *arrays,
    )
    near_batch, far_batch = batch, over(batch)
    came = [send(m, value) for m, value in zip(inner, going)]
    late = [send(m, value) for m, value in zip(late_masks, going[len(inner):])]

    arrays = [plane, opposite_plane, going[0], *late, *came]
    batch, *pair_and_going = pack(
        [cut(arrays, *[(value, 0, depth) for value in late]),
         cut(arrays, (going[0], 2 * depth, 2 * have)),
         cut(arrays, (came[0], 2 * depth, 2 * have))]
        + [
            cut(arrays, (plane, m * depth, depth), (opposite_plane, m * depth, depth))
            for m in outer
        ],
        *arrays, far_batch,
    )
    pair, going = pair_and_going[:2], pair_and_going[2:]
    last = [send(m, value) for m, value in zip(outer, going)] + [over(batch)]
    other_pair = [exchange(value, ("loop",), 1) for value in pair]

    first_rows = [(value, 2 * have) for value in pair]
    first_rows += [(plane, depth), (opposite_plane, depth)]
    first_rows += [(value, 2 * depth) for value in came]
    first_rows += [(value, value.shape[0]) for value in (near_batch, far_batch, batch)]
    last_rows = [(value, value.shape[0]) for value in (*other_pair, *last)]
    first_places = [(m, p) for m in (0, *inner) for p in range(2)]
    first_places += [(m, p) for p in range(2) for m in middle_masks]
    first_places += [(m, 0) for m in late_masks]
    last_places = [(m, p) for m in outer for p in range(2)] + [(m, 1) for m in late_masks]
    side = loop * block // 2
    columns = (
        (tuple(orders[:loop // 2]), tuple(first_places)),
        (tuple(orders[loop // 2:]), tuple(last_places)),
    )
    first_counts = tuple(n for _, n in first_rows)
    last_counts = tuple(n for _, n in last_rows)

    rows = loop * block
    rows_1 = jax.ShapeDtypeStruct((sum(first_counts), width), jnp.bfloat16)
    rows_2 = jax.ShapeDtypeStruct((sum(last_counts), width), jnp.bfloat16)
    payload = jax.ShapeDtypeStruct((side, width + 2 * LOSS), jnp.float32)
    scores, rows_1 = pl.pallas_call(
        functools.partial(early_kernel, first_counts),
        out_shape=[jax.ShapeDtypeStruct((count, rows_1.shape[0]), jnp.float32), rows_1],
        in_specs=[WHOLE] * (1 + len(first_rows)),
        out_specs=[WHOLE] * 2,
        compiler_params=budget(queries, rows_1, rows_1),
        cost_estimate=pl.CostEstimate(
            flops=2 * count * rows_1.size,
            bytes_accessed=2 * (queries.size + 2 * rows_1.size), transcendentals=0,
        ),
    )(queries, *[value for value, _ in first_rows])
    weights_1, weights_2, rows_2, send_part = pl.pallas_call(
        functools.partial(score_kernel, last_counts, len(other_pair), columns, slots),
        out_shape=[
            jax.ShapeDtypeStruct((count, rows_1.shape[0]), jnp.bfloat16),
            jax.ShapeDtypeStruct((count, rows_2.shape[0]), jnp.bfloat16),
            rows_2, payload,
        ],
        in_specs=[SCALARS] * 2 + [WHOLE] * (3 + len(last_rows)),
        out_specs=[WHOLE] * 4,
        compiler_params=budget(queries, rows_2, rows_2, payload, payload),
        cost_estimate=pl.CostEstimate(
            flops=2 * count * (rows_2.size + payload.size),
            bytes_accessed=2 * (queries.size + 2 * rows_2.size) + 4 * payload.size,
            transcendentals=2 * count * (rows_1.shape[0] + rows_2.shape[0]),
        ),
    )(
        meta, hard_counts, queries, positive.reshape(1, count), scores,
        *last, *other_pair,
    )

    sent = exchange(send_part, ("loop",), 1)
    kept = pl.pallas_call(
        keep_kernel,
        out_shape=jax.ShapeDtypeStruct((rows // 2, width + 2 * LOSS), jnp.float32),
        in_specs=[SCALARS] + [WHOLE] * 3,
        out_specs=WHOLE,
        compiler_params=budget(queries, payload, payload),
        cost_estimate=pl.CostEstimate(
            flops=count * rows * width,
            bytes_accessed=2 * count * width + 2 * rows * width, transcendentals=0,
        ),
    )(meta, weights_1, queries, send_part)
    query_grad, done = pl.pallas_call(
        grad_kernel,
        out_shape=[
            jax.ShapeDtypeStruct((count, width), jnp.float32),
            jax.ShapeDtypeStruct((8, 128), jnp.float32),
        ],
        in_specs=[WHOLE] * 4,
        out_specs=[WHOLE] * 2,
        compiler_params=budget(queries, queries, rows_1, rows_2),
        cost_estimate=pl.CostEstimate(
            flops=2 * count * (rows_1.size + rows_2.size),
            bytes_accessed=2 * (rows_1.size + rows_2.size) + 4 * count * width,
            transcendentals=0,
        ),
    )(weights_1, weights_2, rows_1, rows_2)
    part = half + LOSS
    quarter = rows // 4
    first = jax.ShapeDtypeStruct((quarter, part), jnp.float32)
    short = jax.ShapeDtypeStruct(first.shape, jnp.bfloat16)
    own, *going = pl.pallas_call(
        first_sum,
        out_shape=[first, first, first, short],
        in_specs=[WHOLE] * 2,
        out_specs=[WHOLE] * 4,
        compiler_params=budget(payload, payload, payload),
        cost_estimate=pl.CostEstimate(
            flops=payload.size, bytes_accessed=12 * payload.size, transcendentals=0
        ),
    )(kept, sent)
    came = [exchange(value, both, mask) for value, mask in zip(going, (4, 1, 5))]
    second = jax.ShapeDtypeStruct((block, part), jnp.float32)
    total, *going = pl.pallas_call(
        second_sum,
        out_shape=[
            jax.ShapeDtypeStruct(second.shape, jnp.bfloat16 if i == 1 else jnp.float32)
            for i in range(rest)
        ],
        in_specs=[WHOLE] * 5,
        out_specs=[WHOLE] * rest,
        compiler_params=budget(payload, payload),
        cost_estimate=pl.CostEstimate(
            flops=4 * first.size, bytes_accessed=20 * first.size, transcendentals=0
        ),
    )(own, *came, done)
    for value, order in reversed(list(zip(going, orders[1:rest]))):
        total = total + exchange(value, ("loop",), order).astype(jnp.float32)
    mean_loss = (total[0, half] + total[0, half + LOSS // 2]) / (count * loop * reps)
    total = total[:, :half]
    opposite = exchange(total, ("rep",), 1)
    passage_grad = jnp.where(
        rep == 0,
        jnp.concatenate([total, opposite], axis=1),
        jnp.concatenate([opposite, total], axis=1),
    )

    return (query_grad, passage_grad, mean_loss)


def solution(mesh):
    placed = (
        P(("loop", "rep"), None),
        P("loop", None),
        P(("loop", "rep"), None),
        P(("loop", "rep")),
        P("loop", None, None),
        P("loop", None),
    )
    return jax.shard_map(
        shards,
        mesh=mesh,
        in_specs=placed,
        out_specs=(P(("loop", "rep"), None), P("loop", None), P()),
        check_vma=False,
    )
```

```python
import functools

import jax
import jax.numpy as jnp
from jax import lax
from jax.experimental import pallas as pl
from jax.experimental.pallas import tpu as pltpu
from jax.sharding import PartitionSpec as P


def budget(*arrays):
    total = sum(a.size * a.dtype.itemsize for a in arrays)
    return pltpu.CompilerParams(vmem_limit_bytes=total + total // 4 + 6 * 1024 * 1024)


WHOLE = pl.BlockSpec(memory_space=pltpu.VMEM)
SCALARS = pl.BlockSpec(memory_space=pltpu.SMEM)
LOSS = 128


def exchange(value, axes, mask):
    size = 1
    for axis in axes:
        size *= lax.axis_size(axis)
    return lax.ppermute(value, axes, [(i, i ^ mask) for i in range(size)])


def pick_rows(count, reach, meta, other, own, after, *refs):
    asked, (plane, *pieces) = refs[:reach], refs[reach:]
    me, rep = meta[0], meta[1]
    owners = asked[0].shape[1]
    slots = plane.shape[0] // (2 * count)
    lanes = lax.broadcasted_iota(jnp.int32, (slots, owners), 1)
    rows = lax.broadcasted_iota(jnp.int32, (slots, own.shape[0]), 1)

    def hot(owner):
        picked = []
        for m in range(count + len(pieces)):
            at = m % 2 * slots
            tile = asked[-(m // 2)][at:at + slots, :]
            column = jnp.sum(jnp.where(lanes == owner, tile, 0), axis=1, keepdims=True)
            picked.append(jnp.where(column == rows, 1.0, 0.0))
        return jnp.concatenate(picked, axis=0).astype(jnp.bfloat16)

    hot_own = hot(me * 2 + rep)
    hot_other = hot((me ^ 1) * 2 + rep)
    got_other = jnp.dot(hot_other, other[...], preferred_element_type=jnp.float32)
    got_own = jnp.dot(hot_own, own[...], preferred_element_type=jnp.float32)
    for m in range(count + len(pieces)):
        part = slice(m * slots, (m + 1) * slots)
        value = jnp.concatenate([got_own[part], got_other[part]], axis=0).astype(jnp.bfloat16)
        if m < count:
            plane[m * 2 * slots:(m + 1) * 2 * slots, :] = value
        else:
            pieces[m - count][...] = value


def pack_kernel(layouts, *refs):
    ins, outs = refs[:-len(layouts)], refs[-len(layouts):]
    for layout, out in zip(layouts, outs):
        at = 0
        for which, first, rows in layout:
            out[at:at + rows, :] = ins[which][first:first + rows, :]
            at += rows


def pack(layouts, *arrays):
    shapes = [
        jax.ShapeDtypeStruct((sum(rows for _, _, rows in layout), arrays[0].shape[1]), arrays[0].dtype)
        for layout in layouts
    ]
    size = sum(shape.size for shape in shapes)
    return pl.pallas_call(
        functools.partial(pack_kernel, layouts),
        out_shape=shapes,
        in_specs=[WHOLE] * len(arrays),
        out_specs=[WHOLE] * len(layouts),
        compiler_params=budget(*shapes, *arrays),
        cost_estimate=pl.CostEstimate(flops=size, bytes_accessed=4 * size, transcendentals=0),
    )(*arrays)


def stack(counts, refs, out):
    at = 0
    for rows, ref in zip(counts, refs):
        out[at:at + rows, :] = ref[:rows, :]
        at += rows


def scored(queries, rows):
    return 50.0 * lax.dot_general(
        queries[...], rows[...], (((1,), (1,)), ((), ())), preferred_element_type=jnp.float32
    )


def early_kernel(counts, queries, *refs):
    *batches, scores_out, rows = refs
    stack(counts, batches, rows)
    scores_out[...] = scored(queries, rows)


def lookup(index, values):
    total = jnp.zeros_like(index)
    for i, value in enumerate(values):
        total = jnp.where(index == i, value, total)
    return total


def score_kernel(
    counts, passages, columns, slots, meta, hard_counts, queries, positive, scores_ref, *refs
):
    *batches, out_1, out_2, rows, send_out = refs
    batches = batches[-passages:] + batches[:-passages]
    me, rep = meta[0], meta[1]
    stack(counts, batches, rows)
    side = send_out.shape[0]
    block = side // len(columns[0][0])
    blocks = [scores_ref[...], scored(queries, rows)]
    wanted = jnp.broadcast_to(positive[...].astype(jnp.float32), (8, positive.shape[1]))
    wanted = jnp.transpose(wanted)[:, :1]
    onehots = []
    for i, (order, places) in enumerate(columns):
        lane = lax.broadcasted_iota(jnp.int32, (1, blocks[i].shape[1]), 1)
        passage = lane < side
        ids = (lookup(lane // block, order) * block + lane % block) ^ (me * block)
        spot = jnp.where(passage, 0, lane - side)
        owner = lookup(spot // (2 * slots), [4 * m + p for m, p in places])
        owner = (owner + spot // slots % 2 * 2) ^ (me * 2 + rep)
        taken = lookup(owner, [hard_counts[0, o] for o in range(hard_counts.shape[1])])
        live = passage | (spot % slots < taken)
        onehots.append(
            jnp.where((wanted == ids.astype(jnp.float32)) & passage, 1.0, 0.0)
        )
        blocks[i] = jnp.where(live, blocks[i], -jnp.inf)
    tops = [jnp.max(value, axis=1, keepdims=True) for value in blocks]
    row_top = jnp.maximum(tops[0], tops[1])
    sums = [jnp.sum(jnp.exp(value - row_top), axis=1, keepdims=True) for value in blocks]
    log_total = row_top + jnp.log(sums[0] + sums[1])
    weights = [
        (jnp.exp(value - log_total) - onehot).astype(jnp.bfloat16)
        for value, onehot in zip(blocks, onehots)
    ]
    hit = sum(
        jnp.sum(jnp.where(onehot > 0, value, 0.0), axis=1, keepdims=True)
        for value, onehot in zip(blocks, onehots)
    )
    project(send_out, weights[1][:, :side], queries, meta[1], jnp.sum(log_total - hit))
    out_1[...] = weights[0]
    out_2[...] = weights[1]


def project(out, weights, queries, rep, loss):
    half = queries.shape[1] // 2
    for i, side in enumerate((rep, 1 - rep)):
        product = lax.dot_general(
            weights, queries[:, pl.ds(pl.multiple_of(side * half, half), half)],
            (((0,), (0,)), ((), ())), preferred_element_type=jnp.float32,
        )
        at = i * (half + LOSS)
        out[:, at:at + half] = 50.0 * product
        out[:, at + half:at + half + LOSS] = jnp.full((out.shape[0], LOSS), loss, jnp.float32)


def keep_kernel(meta, weights, queries, send, out):
    half = queries.shape[1] // 2
    project(
        out, weights[:, :out.shape[0]], queries, meta[1], send[0:1, half:half + 1]
    )


def first_sum(kept, sent, own, to_x, to_y, to_xy):
    rows, columns = own.shape
    half = columns - LOSS
    lanes = lax.broadcasted_iota(jnp.int32, (rows, LOSS), 1)
    for out, down, across in ((own, 0, 0), (to_x, 1, 0), (to_y, 0, 1), (to_xy, 1, 1)):
        at = pl.ds(down * rows, rows)
        data = pl.ds(across * columns, half)
        out[:, :half] = (kept[at, data] + sent[at, data]).astype(out.dtype)
        tile = pl.ds(across * columns + half, LOSS)
        loss = kept[at, tile] + sent[at, tile]
        high = loss.astype(jnp.bfloat16).astype(jnp.float32)
        out[:, half:] = jnp.where(lanes < LOSS // 2, high, loss - high).astype(out.dtype)


def second_sum(own, from_x, from_y, from_xy, after, *outs):
    rows, columns = outs[0].shape
    half = columns - LOSS
    lanes = lax.broadcasted_iota(jnp.int32, (rows, LOSS), 1)
    for i, out in enumerate(outs):
        at = pl.ds(i * rows, rows)
        total = (own[at] + from_x[at]) + (from_y[at] + from_xy[at].astype(jnp.float32))
        if out.dtype == jnp.float32:
            out[...] = total
        else:
            loss = total[:, half:half + 1] + total[:, half + LOSS // 2:half + LOSS // 2 + 1]
            high = loss.astype(jnp.bfloat16).astype(jnp.float32)
            out[:, :half] = total[:, :half].astype(out.dtype)
            out[:, half:] = jnp.where(lanes < LOSS // 2, high, loss - high).astype(out.dtype)


def grad_kernel(weights_1, weights_2, rows_1, rows_2, out, done):
    done[...] = jnp.zeros(done.shape, done.dtype)
    out[...] = 50.0 * (
        jnp.dot(weights_1[...], rows_1[...], preferred_element_type=jnp.float32)
        + jnp.dot(weights_2[...], rows_2[...], preferred_element_type=jnp.float32)
    )


def shards(queries, passages, index_rows, positive, hard_rows, hard_counts):
    loop = lax.axis_size("loop")
    reps = lax.axis_size("rep")
    me = lax.axis_index("loop").astype(jnp.int32)
    rep = lax.axis_index("rep").astype(jnp.int32)
    count, width = queries.shape
    block = passages.shape[0]
    owners, slots = hard_rows.shape[1:]
    half = width // 2
    chips = loop // 2
    meta = jnp.stack([me, rep])
    both = ("loop", "rep")

    other_rows = exchange(index_rows, ("loop",), 1)
    rest = loop // 4
    wanted = jnp.transpose(hard_rows, (0, 2, 1)).reshape(slots, owners)
    neighbour, (own_wanted,) = exchange(wanted, ("loop",), 2), pack([[(0, 0, slots)]], wanted)
    asked, = pack([[(0, 0, slots), (1, 0, slots)]], own_wanted, neighbour)
    asked = [asked] + [exchange(asked, ("loop",), 4 * k) for k in reversed(range(1, rest))]
    own_rows, = pack([[(0, 0, index_rows.shape[0])]], index_rows)

    bits = [loop // 2 >> i for i in range(loop.bit_length() - 4)] + [4, 2, 1]
    orders = [0]
    for bit in bits:
        orders = orders + [o | bit for o in orders]
    for bit in bits[:-4]:
        passages = jnp.concatenate([passages, exchange(passages, ("loop",), bit)], axis=0)
    passages_z = exchange(passages, ("loop",), bits[-4])

    depth = 2 * slots
    have = 2 * passages.shape[0]
    top = chips // 2
    outs = [jax.ShapeDtypeStruct((top * depth, width), jnp.bfloat16)]
    outs += [jax.ShapeDtypeStruct((depth, width), jnp.bfloat16)] * top
    known, = pack([[(i, 0, have // 2) for i in range(2)]], passages, passages_z)
    plane, *sends = pl.pallas_call(
        functools.partial(pick_rows, top, rest),
        out_shape=outs,
        in_specs=[SCALARS] + [WHOLE] * (3 + rest),
        out_specs=[WHOLE] * (1 + top),
        compiler_params=budget(index_rows, index_rows, *outs, *outs),
        cost_estimate=pl.CostEstimate(
            flops=4 * chips * slots * index_rows.shape[0] * width,
            bytes_accessed=3 * index_rows.size * 2, transcendentals=0,
        ),
    )(meta, other_rows, own_rows, passages_z, *asked)

    def send(m, value):
        return exchange(value, ("loop",), 2 * m)

    def over(value):
        return exchange(value, ("rep",), 1)

    def cut(arrays, *pieces):
        return [
            (next(i for i, a in enumerate(arrays) if a is array), first, rows)
            for array, first, rows in pieces
        ]

    half_top = top // 2
    inner, outer = range(1, half_top + 1), range(half_top + 1, top)
    opposite_plane = over(plane)
    middle_masks, late_masks = range(chips - 1, top, -2), range(chips - 2, top - 1, -2)
    sends = dict(zip(range(top, chips), sends))
    middle = [send(m, sends[m]) for m in middle_masks]
    held_back = [sends[m] for m in late_masks]
    known = [known, exchange(known, ("loop",), 4)]

    arrays = [plane, opposite_plane, *middle, *known, *held_back]
    quad = [(value, 0, value.shape[0]) for value in known]
    batch, *going = pack(
        [cut(arrays, *[(value, 0, depth) for value in middle])]
        + [
            cut(arrays, (plane, m * depth, depth), (opposite_plane, m * depth, depth),
                *(quad if m == 1 else []))
            for m in inner
        ]
        + [cut(arrays, (value, 0, depth)) for value in held_back],
        *arrays,
    )
    near_batch, far_batch = batch, over(batch)
    came = [send(m, value) for m, value in zip(inner, going)]
    late = [send(m, value) for m, value in zip(late_masks, going[len(inner):])]

    arrays = [plane, opposite_plane, going[0], *late, *came]
    batch, *pair_and_going = pack(
        [cut(arrays, *[(value, 0, depth) for value in late]),
         cut(arrays, (going[0], 2 * depth, 2 * have)),
         cut(arrays, (came[0], 2 * depth, 2 * have))]
        + [
            cut(arrays, (plane, m * depth, depth), (opposite_plane, m * depth, depth))
            for m in outer
        ],
        *arrays, far_batch,
    )
    pair, going = pair_and_going[:2], pair_and_going[2:]
    last = [send(m, value) for m, value in zip(outer, going)] + [over(batch)]
    other_pair = [exchange(value, ("loop",), 1) for value in pair]

    first_rows = [(value, 2 * have) for value in pair]
    first_rows += [(plane, depth), (opposite_plane, depth)]
    first_rows += [(value, 2 * depth) for value in came]
    first_rows += [(value, value.shape[0]) for value in (near_batch, far_batch, batch)]
    last_rows = [(value, value.shape[0]) for value in (*other_pair, *last)]
    first_places = [(m, p) for m in (0, *inner) for p in range(2)]
    first_places += [(m, p) for p in range(2) for m in middle_masks]
    first_places += [(m, 0) for m in late_masks]
    last_places = [(m, p) for m in outer for p in range(2)] + [(m, 1) for m in late_masks]
    side = loop * block // 2
    columns = (
        (tuple(orders[:loop // 2]), tuple(first_places)),
        (tuple(orders[loop // 2:]), tuple(last_places)),
    )
    first_counts = tuple(n for _, n in first_rows)
    last_counts = tuple(n for _, n in last_rows)

    rows = loop * block
    rows_1 = jax.ShapeDtypeStruct((sum(first_counts), width), jnp.bfloat16)
    rows_2 = jax.ShapeDtypeStruct((sum(last_counts), width), jnp.bfloat16)
    payload = jax.ShapeDtypeStruct((side, width + 2 * LOSS), jnp.float32)
    scores, rows_1 = pl.pallas_call(
        functools.partial(early_kernel, first_counts),
        out_shape=[jax.ShapeDtypeStruct((count, rows_1.shape[0]), jnp.float32), rows_1],
        in_specs=[WHOLE] * (1 + len(first_rows)),
        out_specs=[WHOLE] * 2,
        compiler_params=budget(queries, rows_1, rows_1),
        cost_estimate=pl.CostEstimate(
            flops=2 * count * rows_1.size,
            bytes_accessed=2 * (queries.size + 2 * rows_1.size), transcendentals=0,
        ),
    )(queries, *[value for value, _ in first_rows])
    weights_1, weights_2, rows_2, send_part = pl.pallas_call(
        functools.partial(score_kernel, last_counts, len(other_pair), columns, slots),
        out_shape=[
            jax.ShapeDtypeStruct((count, rows_1.shape[0]), jnp.bfloat16),
            jax.ShapeDtypeStruct((count, rows_2.shape[0]), jnp.bfloat16),
            rows_2, payload,
        ],
        in_specs=[SCALARS] * 2 + [WHOLE] * (3 + len(last_rows)),
        out_specs=[WHOLE] * 4,
        compiler_params=budget(queries, rows_2, rows_2, payload, payload),
        cost_estimate=pl.CostEstimate(
            flops=2 * count * (rows_2.size + payload.size),
            bytes_accessed=2 * (queries.size + 2 * rows_2.size) + 4 * payload.size,
            transcendentals=2 * count * (rows_1.shape[0] + rows_2.shape[0]),
        ),
    )(
        meta, hard_counts, queries, positive.reshape(1, count), scores,
        *last, *other_pair,
    )

    sent = exchange(send_part, ("loop",), 1)
    kept = pl.pallas_call(
        keep_kernel,
        out_shape=jax.ShapeDtypeStruct((rows // 2, width + 2 * LOSS), jnp.float32),
        in_specs=[SCALARS] + [WHOLE] * 3,
        out_specs=WHOLE,
        compiler_params=budget(queries, payload, payload),
        cost_estimate=pl.CostEstimate(
            flops=count * rows * width,
            bytes_accessed=2 * count * width + 2 * rows * width, transcendentals=0,
        ),
    )(meta, weights_1, queries, send_part)
    query_grad, done = pl.pallas_call(
        grad_kernel,
        out_shape=[
            jax.ShapeDtypeStruct((count, width), jnp.float32),
            jax.ShapeDtypeStruct((8, 128), jnp.float32),
        ],
        in_specs=[WHOLE] * 4,
        out_specs=[WHOLE] * 2,
        compiler_params=budget(queries, queries, rows_1, rows_2),
        cost_estimate=pl.CostEstimate(
            flops=2 * count * (rows_1.size + rows_2.size),
            bytes_accessed=2 * (rows_1.size + rows_2.size) + 4 * count * width,
            transcendentals=0,
        ),
    )(weights_1, weights_2, rows_1, rows_2)
    part = half + LOSS
    quarter = rows // 4
    first = jax.ShapeDtypeStruct((quarter, part), jnp.float32)
    short = jax.ShapeDtypeStruct(first.shape, jnp.bfloat16)
    own, *going = pl.pallas_call(
        first_sum,
        out_shape=[first, first, first, short],
        in_specs=[WHOLE] * 2,
        out_specs=[WHOLE] * 4,
        compiler_params=budget(payload, payload, payload),
        cost_estimate=pl.CostEstimate(
            flops=payload.size, bytes_accessed=12 * payload.size, transcendentals=0
        ),
    )(kept, sent)
    came = [exchange(value, both, mask) for value, mask in zip(going, (4, 1, 5))]
    second = jax.ShapeDtypeStruct((block, part), jnp.float32)
    total, *going = pl.pallas_call(
        second_sum,
        out_shape=[
            jax.ShapeDtypeStruct(second.shape, jnp.bfloat16 if i == 1 else jnp.float32)
            for i in range(rest)
        ],
        in_specs=[WHOLE] * 5,
        out_specs=[WHOLE] * rest,
        compiler_params=budget(payload, payload),
        cost_estimate=pl.CostEstimate(
            flops=4 * first.size, bytes_accessed=20 * first.size, transcendentals=0
        ),
    )(own, *came, done)
    for value, order in reversed(list(zip(going, orders[1:rest]))):
        total = total + exchange(value, ("loop",), order).astype(jnp.float32)
    mean_loss = (total[0, half] + total[0, half + LOSS // 2]) / (count * loop * reps)
    total = total[:, :half]
    opposite = exchange(total, ("rep",), 1)
    passage_grad = jnp.where(
        rep == 0,
        jnp.concatenate([total, opposite], axis=1),
        jnp.concatenate([opposite, total], axis=1),
    )

    return (query_grad, passage_grad, mean_loss)


def solution(mesh):
    placed = (
        P(("loop", "rep"), None),
        P("loop", None),
        P(("loop", "rep"), None),
        P(("loop", "rep")),
        P("loop", None, None),
        P("loop", None),
    )
    return jax.shard_map(
        shards,
        mesh=mesh,
        in_specs=placed,
        out_specs=(P(("loop", "rep"), None), P("loop", None), P()),
        check_vma=False,
    )
```

```python
import functools

import jax
import jax.numpy as jnp
from jax import lax
from jax.experimental import pallas as pl
from jax.experimental.pallas import tpu as pltpu
from jax.sharding import PartitionSpec as P


def budget(*arrays):
    total = sum(a.size * a.dtype.itemsize for a in arrays)
    return pltpu.CompilerParams(vmem_limit_bytes=total + total // 4 + 6 * 1024 * 1024)


WHOLE = pl.BlockSpec(memory_space=pltpu.VMEM)
SCALARS = pl.BlockSpec(memory_space=pltpu.SMEM)
LOSS = 128


def exchange(value, axes, mask):
    size = 1
    for axis in axes:
        size *= lax.axis_size(axis)
    return lax.ppermute(value, axes, [(i, i ^ mask) for i in range(size)])


def pick_rows(count, reach, meta, other, own, after, *refs):
    asked, (plane, *pieces) = refs[:reach], refs[reach:]
    me, rep = meta[0], meta[1]
    owners = asked[0].shape[1]
    slots = plane.shape[0] // (2 * count)
    lanes = lax.broadcasted_iota(jnp.int32, (slots, owners), 1)
    rows = lax.broadcasted_iota(jnp.int32, (slots, own.shape[0]), 1)

    def hot(owner):
        picked = []
        for m in range(count + len(pieces)):
            at = m % 2 * slots
            tile = asked[m // 2][at:at + slots, :]
            column = jnp.sum(jnp.where(lanes == owner, tile, 0), axis=1, keepdims=True)
            picked.append(jnp.where(column == rows, 1.0, 0.0))
        return jnp.concatenate(picked, axis=0).astype(jnp.bfloat16)

    hot_own = hot(me * 2 + rep)
    hot_other = hot((me ^ 1) * 2 + rep)
    got_other = jnp.dot(hot_other, other[...], preferred_element_type=jnp.float32)
    got_own = jnp.dot(hot_own, own[...], preferred_element_type=jnp.float32)
    for m in range(count + len(pieces)):
        part = slice(m * slots, (m + 1) * slots)
        value = jnp.concatenate([got_own[part], got_other[part]], axis=0).astype(jnp.bfloat16)
        if m < count:
            plane[m * 2 * slots:(m + 1) * 2 * slots, :] = value
        else:
            pieces[m - count][...] = value


def pack_kernel(layouts, *refs):
    ins, outs = refs[:-len(layouts)], refs[-len(layouts):]
    for layout, out in zip(layouts, outs):
        at = 0
        for which, first, rows in layout:
            out[at:at + rows, :] = ins[which][first:first + rows, :]
            at += rows


def pack(layouts, *arrays):
    shapes = [
        jax.ShapeDtypeStruct((sum(rows for _, _, rows in layout), arrays[0].shape[1]), arrays[0].dtype)
        for layout in layouts
    ]
    size = sum(shape.size for shape in shapes)
    return pl.pallas_call(
        functools.partial(pack_kernel, layouts),
        out_shape=shapes,
        in_specs=[WHOLE] * len(arrays),
        out_specs=[WHOLE] * len(layouts),
        compiler_params=budget(*shapes, *arrays),
        cost_estimate=pl.CostEstimate(flops=size, bytes_accessed=4 * size, transcendentals=0),
    )(*arrays)


def stack(counts, refs, out):
    at = 0
    for rows, ref in zip(counts, refs):
        out[at:at + rows, :] = ref[:rows, :]
        at += rows


def scored(queries, rows):
    return 50.0 * lax.dot_general(
        queries[...], rows[...], (((1,), (1,)), ((), ())), preferred_element_type=jnp.float32
    )


def early_kernel(counts, queries, *refs):
    *batches, scores_out, rows = refs
    stack(counts, batches, rows)
    scores_out[...] = scored(queries, rows)


def lookup(index, values):
    total = jnp.zeros_like(index)
    for i, value in enumerate(values):
        total = jnp.where(index == i, value, total)
    return total


def score_kernel(
    counts, passages, columns, slots, meta, hard_counts, queries, positive, scores_ref, *refs
):
    *batches, out_1, out_2, rows, send_out = refs
    batches = batches[-passages:] + batches[:-passages]
    me, rep = meta[0], meta[1]
    stack(counts, batches, rows)
    side = send_out.shape[0]
    block = side // len(columns[0][0])
    blocks = [scores_ref[...], scored(queries, rows)]
    wanted = jnp.broadcast_to(positive[...].astype(jnp.float32), (8, positive.shape[1]))
    wanted = jnp.transpose(wanted)[:, :1]
    onehots = []
    for i, (order, places) in enumerate(columns):
        lane = lax.broadcasted_iota(jnp.int32, (1, blocks[i].shape[1]), 1)
        passage = lane < side
        ids = (lookup(lane // block, order) * block + lane % block) ^ (me * block)
        spot = jnp.where(passage, 0, lane - side)
        owner = lookup(spot // (2 * slots), [4 * m + p for m, p in places])
        owner = (owner + spot // slots % 2 * 2) ^ (me * 2 + rep)
        taken = lookup(owner, [hard_counts[0, o] for o in range(hard_counts.shape[1])])
        live = passage | (spot % slots < taken)
        onehots.append(
            jnp.where((wanted == ids.astype(jnp.float32)) & passage, 1.0, 0.0)
        )
        blocks[i] = jnp.where(live, blocks[i], -jnp.inf)
    tops = [jnp.max(value, axis=1, keepdims=True) for value in blocks]
    row_top = jnp.maximum(tops[0], tops[1])
    sums = [jnp.sum(jnp.exp(value - row_top), axis=1, keepdims=True) for value in blocks]
    log_total = row_top + jnp.log(sums[0] + sums[1])
    weights = [
        (jnp.exp(value - log_total) - onehot).astype(jnp.bfloat16)
        for value, onehot in zip(blocks, onehots)
    ]
    hit = sum(
        jnp.sum(jnp.where(onehot > 0, value, 0.0), axis=1, keepdims=True)
        for value, onehot in zip(blocks, onehots)
    )
    project(send_out, weights[1][:, :side], queries, meta[1], jnp.sum(log_total - hit))
    out_1[...] = weights[0]
    out_2[...] = weights[1]


def project(out, weights, queries, rep, loss):
    half = queries.shape[1] // 2
    for i, side in enumerate((rep, 1 - rep)):
        product = lax.dot_general(
            weights, queries[:, pl.ds(pl.multiple_of(side * half, half), half)],
            (((0,), (0,)), ((), ())), preferred_element_type=jnp.float32,
        )
        at = i * (half + LOSS)
        out[:, at:at + half] = 50.0 * product
        out[:, at + half:at + half + LOSS] = jnp.full((out.shape[0], LOSS), loss, jnp.float32)


def keep_kernel(meta, weights, queries, send, out):
    half = queries.shape[1] // 2
    project(
        out, weights[:, :out.shape[0]], queries, meta[1], send[0:1, half:half + 1]
    )


def first_sum(kept, sent, own, to_xy, *halves):
    rows, columns = own.shape
    half = columns - LOSS
    cuts = [(own, 0, 0, 0), (to_xy, 1, 0, 1)]
    for i, out in enumerate(halves):
        cuts.append((out, (i + 1) % 2, i // 2 * out.shape[0], i % 2))
    for out, down, first, across in cuts:
        at = pl.ds(down * rows + first, out.shape[0])
        data = pl.ds(across * columns, half)
        out[:, :half] = (kept[at, data] + sent[at, data]).astype(out.dtype)
        tile = pl.ds(across * columns + half, LOSS)
        loss = kept[at, tile] + sent[at, tile]
        high = loss.astype(jnp.bfloat16).astype(jnp.float32)
        lanes = lax.broadcasted_iota(jnp.int32, loss.shape, 1)
        out[:, half:] = jnp.where(lanes < LOSS // 2, high, loss - high).astype(out.dtype)


def second_sum(own, from_xy, x_0, y_0, x_1, y_1, after, *outs):
    rows, columns = outs[0].shape
    half = columns - LOSS
    lanes = lax.broadcasted_iota(jnp.int32, (rows, LOSS), 1)
    for i, out in enumerate(outs):
        at = pl.ds(i * rows, rows)
        from_x, from_y, start = (x_0, y_0, 0) if i * rows < x_0.shape[0] else (x_1, y_1, x_0.shape[0])
        near = pl.ds(i * rows - start, rows)
        total = (own[at] + from_x[near]) + (from_y[near] + from_xy[at].astype(jnp.float32))
        if out.dtype == jnp.float32:
            out[...] = total
        else:
            loss = total[:, half:half + 1] + total[:, half + LOSS // 2:half + LOSS // 2 + 1]
            high = loss.astype(jnp.bfloat16).astype(jnp.float32)
            out[:, :half] = total[:, :half].astype(out.dtype)
            out[:, half:] = jnp.where(lanes < LOSS // 2, high, loss - high).astype(out.dtype)


def grad_kernel(weights_1, weights_2, rows_1, rows_2, out, done):
    done[...] = jnp.zeros(done.shape, done.dtype)
    out[...] = 50.0 * (
        jnp.dot(weights_1[...], rows_1[...], preferred_element_type=jnp.float32)
        + jnp.dot(weights_2[...], rows_2[...], preferred_element_type=jnp.float32)
    )


def shards(queries, passages, index_rows, positive, hard_rows, hard_counts):
    loop = lax.axis_size("loop")
    reps = lax.axis_size("rep")
    me = lax.axis_index("loop").astype(jnp.int32)
    rep = lax.axis_index("rep").astype(jnp.int32)
    count, width = queries.shape
    block = passages.shape[0]
    owners, slots = hard_rows.shape[1:]
    half = width // 2
    chips = loop // 2
    meta = jnp.stack([me, rep])
    both = ("loop", "rep")

    other_rows = exchange(index_rows, ("loop",), 1)
    rest = loop // 4
    wanted = jnp.transpose(hard_rows, (0, 2, 1)).reshape(slots, owners)
    neighbour, (own_wanted,) = exchange(wanted, ("loop",), 2), pack([[(0, 0, slots)]], wanted)
    asked, = pack([[(0, 0, slots), (1, 0, slots)]], own_wanted, neighbour)
    asked = [asked] + [exchange(asked, ("loop",), 4 * k) for k in range(1, rest)]
    own_rows, = pack([[(0, 0, index_rows.shape[0])]], index_rows)

    bits = [loop // 2 >> i for i in range(loop.bit_length() - 4)] + [4, 2, 1]
    orders = [0]
    for bit in bits:
        orders = orders + [o | bit for o in orders]
    for bit in bits[:-4]:
        passages = jnp.concatenate([passages, exchange(passages, ("loop",), bit)], axis=0)
    passages_z = exchange(passages, ("loop",), bits[-4])

    depth = 2 * slots
    have = 2 * passages.shape[0]
    top = chips // 2
    outs = [jax.ShapeDtypeStruct((top * depth, width), jnp.bfloat16)]
    outs += [jax.ShapeDtypeStruct((depth, width), jnp.bfloat16)] * top
    known, = pack([[(i, 0, have // 2) for i in range(2)]], passages, passages_z)
    plane, *sends = pl.pallas_call(
        functools.partial(pick_rows, top, rest),
        out_shape=outs,
        in_specs=[SCALARS] + [WHOLE] * (3 + rest),
        out_specs=[WHOLE] * (1 + top),
        compiler_params=budget(index_rows, index_rows, *outs, *outs),
        cost_estimate=pl.CostEstimate(
            flops=4 * chips * slots * index_rows.shape[0] * width,
            bytes_accessed=3 * index_rows.size * 2, transcendentals=0,
        ),
    )(meta, other_rows, own_rows, passages_z, *asked)

    def send(m, value):
        return exchange(value, ("loop",), 2 * m)

    def over(value):
        return exchange(value, ("rep",), 1)

    def cut(arrays, *pieces):
        return [
            (next(i for i, a in enumerate(arrays) if a is array), first, rows)
            for array, first, rows in pieces
        ]

    half_top = top // 2
    inner, outer = range(1, half_top + 1), range(half_top + 1, top)
    opposite_plane = over(plane)
    middle_masks, late_masks = range(top + 1, chips, 2), range(top, chips, 2)
    sends = dict(zip(range(top, chips), sends))
    middle = [send(m, sends[m]) for m in middle_masks]
    held_back = [sends[m] for m in late_masks]
    known = [known, exchange(known, ("loop",), 4)]

    arrays = [plane, opposite_plane, *middle, *known, *held_back]
    quad = [(value, 0, value.shape[0]) for value in known]
    batch, *going = pack(
        [cut(arrays, *[(value, 0, depth) for value in middle])]
        + [
            cut(arrays, (plane, m * depth, depth), (opposite_plane, m * depth, depth),
                *(quad if m == 1 else []))
            for m in inner
        ]
        + [cut(arrays, (value, 0, depth)) for value in held_back],
        *arrays,
    )
    near_batch, far_batch = batch, over(batch)
    came = [send(m, value) for m, value in zip(inner, going)]
    late = [send(m, value) for m, value in zip(late_masks, going[len(inner):])]

    arrays = [plane, opposite_plane, going[0], *late, *came]
    batch, *pair_and_going = pack(
        [cut(arrays, *[(value, 0, depth) for value in late]),
         cut(arrays, (going[0], 2 * depth, 2 * have)),
         cut(arrays, (came[0], 2 * depth, 2 * have))]
        + [
            cut(arrays, (plane, m * depth, depth), (opposite_plane, m * depth, depth))
            for m in outer
        ],
        *arrays, far_batch,
    )
    pair, going = pair_and_going[:2], pair_and_going[2:]
    last = [send(m, value) for m, value in zip(outer, going)] + [over(batch)]
    other_pair = [exchange(value, ("loop",), 1) for value in pair]

    first_rows = [(value, 2 * have) for value in pair]
    first_rows += [(plane, depth), (opposite_plane, depth)]
    first_rows += [(value, 2 * depth) for value in came]
    first_rows += [(value, value.shape[0]) for value in (near_batch, far_batch, batch)]
    last_rows = [(value, value.shape[0]) for value in (*other_pair, *last)]
    first_places = [(m, p) for m in (0, *inner) for p in range(2)]
    first_places += [(m, p) for p in range(2) for m in middle_masks]
    first_places += [(m, 0) for m in late_masks]
    last_places = [(m, p) for m in outer for p in range(2)] + [(m, 1) for m in late_masks]
    side = loop * block // 2
    columns = (
        (tuple(orders[:loop // 2]), tuple(first_places)),
        (tuple(orders[loop // 2:]), tuple(last_places)),
    )
    first_counts = tuple(n for _, n in first_rows)
    last_counts = tuple(n for _, n in last_rows)

    rows = loop * block
    rows_1 = jax.ShapeDtypeStruct((sum(first_counts), width), jnp.bfloat16)
    rows_2 = jax.ShapeDtypeStruct((sum(last_counts), width), jnp.bfloat16)
    payload = jax.ShapeDtypeStruct((side, width + 2 * LOSS), jnp.float32)
    scores, rows_1 = pl.pallas_call(
        functools.partial(early_kernel, first_counts),
        out_shape=[jax.ShapeDtypeStruct((count, rows_1.shape[0]), jnp.float32), rows_1],
        in_specs=[WHOLE] * (1 + len(first_rows)),
        out_specs=[WHOLE] * 2,
        compiler_params=budget(queries, rows_1, rows_1),
        cost_estimate=pl.CostEstimate(
            flops=2 * count * rows_1.size,
            bytes_accessed=2 * (queries.size + 2 * rows_1.size), transcendentals=0,
        ),
    )(queries, *[value for value, _ in first_rows])
    weights_1, weights_2, rows_2, send_part = pl.pallas_call(
        functools.partial(score_kernel, last_counts, len(other_pair), columns, slots),
        out_shape=[
            jax.ShapeDtypeStruct((count, rows_1.shape[0]), jnp.bfloat16),
            jax.ShapeDtypeStruct((count, rows_2.shape[0]), jnp.bfloat16),
            rows_2, payload,
        ],
        in_specs=[SCALARS] * 2 + [WHOLE] * (3 + len(last_rows)),
        out_specs=[WHOLE] * 4,
        compiler_params=budget(queries, rows_2, rows_2, payload, payload),
        cost_estimate=pl.CostEstimate(
            flops=2 * count * (rows_2.size + payload.size),
            bytes_accessed=2 * (queries.size + 2 * rows_2.size) + 4 * payload.size,
            transcendentals=2 * count * (rows_1.shape[0] + rows_2.shape[0]),
        ),
    )(
        meta, hard_counts, queries, positive.reshape(1, count), scores,
        *last, *other_pair,
    )

    sent = exchange(send_part, ("loop",), 1)
    kept = pl.pallas_call(
        keep_kernel,
        out_shape=jax.ShapeDtypeStruct((rows // 2, width + 2 * LOSS), jnp.float32),
        in_specs=[SCALARS] + [WHOLE] * 3,
        out_specs=WHOLE,
        compiler_params=budget(queries, payload, payload),
        cost_estimate=pl.CostEstimate(
            flops=count * rows * width,
            bytes_accessed=2 * count * width + 2 * rows * width, transcendentals=0,
        ),
    )(meta, weights_1, queries, send_part)
    query_grad, done = pl.pallas_call(
        grad_kernel,
        out_shape=[
            jax.ShapeDtypeStruct((count, width), jnp.float32),
            jax.ShapeDtypeStruct((8, 128), jnp.float32),
        ],
        in_specs=[WHOLE] * 4,
        out_specs=[WHOLE] * 2,
        compiler_params=budget(queries, queries, rows_1, rows_2),
        cost_estimate=pl.CostEstimate(
            flops=2 * count * (rows_1.size + rows_2.size),
            bytes_accessed=2 * (rows_1.size + rows_2.size) + 4 * count * width,
            transcendentals=0,
        ),
    )(weights_1, weights_2, rows_1, rows_2)
    part = half + LOSS
    quarter = rows // 4
    first = jax.ShapeDtypeStruct((quarter, part), jnp.float32)
    short = jax.ShapeDtypeStruct(first.shape, jnp.bfloat16)
    own, *going = pl.pallas_call(
        first_sum,
        out_shape=[first, short] + [jax.ShapeDtypeStruct((quarter // 2, part), jnp.float32)] * 4,
        in_specs=[WHOLE] * 2,
        out_specs=[WHOLE] * 6,
        compiler_params=budget(payload, payload, payload),
        cost_estimate=pl.CostEstimate(
            flops=payload.size, bytes_accessed=12 * payload.size, transcendentals=0
        ),
    )(kept, sent)
    came = [exchange(value, both, mask) for value, mask in zip(going, (5, 4, 1, 4, 1))]
    second = jax.ShapeDtypeStruct((block, part), jnp.float32)
    total, *going = pl.pallas_call(
        second_sum,
        out_shape=[
            jax.ShapeDtypeStruct(second.shape, jnp.bfloat16 if i == 1 else jnp.float32)
            for i in range(rest)
        ],
        in_specs=[WHOLE] * 7,
        out_specs=[WHOLE] * rest,
        compiler_params=budget(payload, payload),
        cost_estimate=pl.CostEstimate(
            flops=4 * first.size, bytes_accessed=20 * first.size, transcendentals=0
        ),
    )(own, *came, done)
    for value, order in reversed(list(zip(going, orders[1:rest]))):
        total = total + exchange(value, ("loop",), order).astype(jnp.float32)
    mean_loss = (total[0, half] + total[0, half + LOSS // 2]) / (count * loop * reps)
    total = total[:, :half]
    opposite = exchange(total, ("rep",), 1)
    passage_grad = jnp.where(
        rep == 0,
        jnp.concatenate([total, opposite], axis=1),
        jnp.concatenate([opposite, total], axis=1),
    )

    return (query_grad, passage_grad, mean_loss)


def solution(mesh):
    placed = (
        P(("loop", "rep"), None),
        P("loop", None),
        P(("loop", "rep"), None),
        P(("loop", "rep")),
        P("loop", None, None),
        P("loop", None),
    )
    return jax.shard_map(
        shards,
        mesh=mesh,
        in_specs=placed,
        out_specs=(P(("loop", "rep"), None), P("loop", None), P()),
        check_vma=False,
    )
```

```python
import functools

import jax
import jax.numpy as jnp
from jax import lax
from jax.experimental import pallas as pl
from jax.experimental.pallas import tpu as pltpu
from jax.sharding import PartitionSpec as P


def budget(*arrays):
    total = sum(a.size * a.dtype.itemsize for a in arrays)
    return pltpu.CompilerParams(vmem_limit_bytes=total + total // 4 + 6 * 1024 * 1024)


WHOLE = pl.BlockSpec(memory_space=pltpu.VMEM)
SCALARS = pl.BlockSpec(memory_space=pltpu.SMEM)
LOSS = 128


def exchange(value, axes, mask):
    size = 1
    for axis in axes:
        size *= lax.axis_size(axis)
    return lax.ppermute(value, axes, [(i, i ^ mask) for i in range(size)])


def pick_rows(count, reach, meta, other, own, after, *refs):
    asked, (plane, *pieces) = refs[:reach], refs[reach:]
    me, rep = meta[0], meta[1]
    owners = asked[0].shape[1]
    slots = plane.shape[0] // (2 * count)
    lanes = lax.broadcasted_iota(jnp.int32, (slots, owners), 1)
    rows = lax.broadcasted_iota(jnp.int32, (slots, own.shape[0]), 1)

    def hot(owner):
        picked = []
        for m in range(count + len(pieces)):
            at = m % 2 * slots
            tile = asked[m // 2][at:at + slots, :]
            column = jnp.sum(jnp.where(lanes == owner, tile, 0), axis=1, keepdims=True)
            picked.append(jnp.where(column == rows, 1.0, 0.0))
        return jnp.concatenate(picked, axis=0).astype(jnp.bfloat16)

    hot_own = hot(me * 2 + rep)
    hot_other = hot((me ^ 1) * 2 + rep)
    got_other = jnp.dot(hot_other, other[...], preferred_element_type=jnp.float32)
    got_own = jnp.dot(hot_own, own[...], preferred_element_type=jnp.float32)
    for m in range(count + len(pieces)):
        part = slice(m * slots, (m + 1) * slots)
        value = jnp.concatenate([got_own[part], got_other[part]], axis=0).astype(jnp.bfloat16)
        if m < count:
            plane[m * 2 * slots:(m + 1) * 2 * slots, :] = value
        else:
            pieces[m - count][...] = value


def pack_kernel(layouts, *refs):
    ins, outs = refs[:-len(layouts)], refs[-len(layouts):]
    for layout, out in zip(layouts, outs):
        at = 0
        for which, first, rows in layout:
            out[at:at + rows, :] = ins[which][first:first + rows, :]
            at += rows


def pack(layouts, *arrays):
    shapes = [
        jax.ShapeDtypeStruct((sum(rows for _, _, rows in layout), arrays[0].shape[1]), arrays[0].dtype)
        for layout in layouts
    ]
    size = sum(shape.size for shape in shapes)
    return pl.pallas_call(
        functools.partial(pack_kernel, layouts),
        out_shape=shapes,
        in_specs=[WHOLE] * len(arrays),
        out_specs=[WHOLE] * len(layouts),
        compiler_params=budget(*shapes, *arrays),
        cost_estimate=pl.CostEstimate(flops=size, bytes_accessed=4 * size, transcendentals=0),
    )(*arrays)


def stack(counts, refs, out):
    at = 0
    for rows, ref in zip(counts, refs):
        out[at:at + rows, :] = ref[:rows, :]
        at += rows


def scored(queries, rows):
    return 50.0 * lax.dot_general(
        queries[...], rows[...], (((1,), (1,)), ((), ())), preferred_element_type=jnp.float32
    )


def early_kernel(counts, queries, *refs):
    *batches, scores_out, rows = refs
    stack(counts, batches, rows)
    scores_out[...] = scored(queries, rows)


def lookup(index, values):
    total = jnp.zeros_like(index)
    for i, value in enumerate(values):
        total = jnp.where(index == i, value, total)
    return total


def score_kernel(
    counts, passages, columns, slots, meta, hard_counts, queries, positive, scores_ref, *refs
):
    *batches, out_1, out_2, rows, send_out = refs
    batches = batches[-passages:] + batches[:-passages]
    me, rep = meta[0], meta[1]
    stack(counts, batches, rows)
    side = send_out.shape[0]
    block = side // len(columns[0][0])
    blocks = [scores_ref[...], scored(queries, rows)]
    wanted = jnp.broadcast_to(positive[...].astype(jnp.float32), (8, positive.shape[1]))
    wanted = jnp.transpose(wanted)[:, :1]
    onehots = []
    for i, (order, places) in enumerate(columns):
        lane = lax.broadcasted_iota(jnp.int32, (1, blocks[i].shape[1]), 1)
        passage = lane < side
        ids = (lookup(lane // block, order) * block + lane % block) ^ (me * block)
        spot = jnp.where(passage, 0, lane - side)
        owner = lookup(spot // (2 * slots), [4 * m + p for m, p in places])
        owner = (owner + spot // slots % 2 * 2) ^ (me * 2 + rep)
        taken = lookup(owner, [hard_counts[0, o] for o in range(hard_counts.shape[1])])
        live = passage | (spot % slots < taken)
        onehots.append(
            jnp.where((wanted == ids.astype(jnp.float32)) & passage, 1.0, 0.0)
        )
        blocks[i] = jnp.where(live, blocks[i], -jnp.inf)
    tops = [jnp.max(value, axis=1, keepdims=True) for value in blocks]
    row_top = jnp.maximum(tops[0], tops[1])
    sums = [jnp.sum(jnp.exp(value - row_top), axis=1, keepdims=True) for value in blocks]
    log_total = row_top + jnp.log(sums[0] + sums[1])
    weights = [
        (jnp.exp(value - log_total) - onehot).astype(jnp.bfloat16)
        for value, onehot in zip(blocks, onehots)
    ]
    hit = sum(
        jnp.sum(jnp.where(onehot > 0, value, 0.0), axis=1, keepdims=True)
        for value, onehot in zip(blocks, onehots)
    )
    project(send_out, weights[1][:, :side], queries, meta[1], jnp.sum(log_total - hit))
    out_1[...] = weights[0]
    out_2[...] = weights[1]


def project(out, weights, queries, rep, loss):
    half = queries.shape[1] // 2
    for i, side in enumerate((rep, 1 - rep)):
        product = lax.dot_general(
            weights, queries[:, pl.ds(pl.multiple_of(side * half, half), half)],
            (((0,), (0,)), ((), ())), preferred_element_type=jnp.float32,
        )
        at = i * (half + LOSS)
        out[:, at:at + half] = 50.0 * product
        out[:, at + half:at + half + LOSS] = jnp.full((out.shape[0], LOSS), loss, jnp.float32)


def keep_kernel(meta, weights, queries, send, out):
    half = queries.shape[1] // 2
    project(
        out, weights[:, :out.shape[0]], queries, meta[1], send[0:1, half:half + 1]
    )


def first_sum(block, kept, sent, own, to_xy, *halves):
    rows, columns = own.shape
    half = columns - LOSS
    lanes = lax.broadcasted_iota(jnp.int32, (block, LOSS), 1)
    cuts = []
    for i in range(rows // block):
        x_out, y_out = halves[:2] if i % 2 else halves[2:]
        for out, at, down, across in (
            (own, i, 0, 0), (to_xy, i, 1, 1), (x_out, i // 2, 1, 0), (y_out, i // 2, 0, 1)
        ):
            cuts.append((out, at * block, down * rows + i * block, across * columns))
    for out, to, row, column in cuts:
        at, to = pl.ds(row, block), pl.ds(to, block)
        data, tile = pl.ds(column, half), pl.ds(column + half, LOSS)
        out[to, :half] = (kept[at, data] + sent[at, data]).astype(out.dtype)
        loss = kept[at, tile] + sent[at, tile]
        high = loss.astype(jnp.bfloat16).astype(jnp.float32)
        out[to, half:] = jnp.where(lanes < LOSS // 2, high, loss - high).astype(out.dtype)


def second_sum(odd, own, from_xy, from_x, from_y, after, *outs):
    rows, columns = outs[0].shape
    half = columns - LOSS
    lanes = lax.broadcasted_iota(jnp.int32, (rows, LOSS), 1)
    for i, out in enumerate(outs):
        at, near = pl.ds((2 * i + odd) * rows, rows), pl.ds(i * rows, rows)
        total = (own[at] + from_x[near]) + (from_y[near] + from_xy[at].astype(jnp.float32))
        if out.dtype == jnp.float32:
            out[...] = total
        else:
            loss = total[:, half:half + 1] + total[:, half + LOSS // 2:half + LOSS // 2 + 1]
            high = loss.astype(jnp.bfloat16).astype(jnp.float32)
            out[:, :half] = total[:, :half].astype(out.dtype)
            out[:, half:] = jnp.where(lanes < LOSS // 2, high, loss - high).astype(out.dtype)


def grad_kernel(weights_1, weights_2, rows_1, rows_2, out, done):
    done[...] = jnp.zeros(done.shape, done.dtype)
    out[...] = 50.0 * (
        jnp.dot(weights_1[...], rows_1[...], preferred_element_type=jnp.float32)
        + jnp.dot(weights_2[...], rows_2[...], preferred_element_type=jnp.float32)
    )


def shards(queries, passages, index_rows, positive, hard_rows, hard_counts):
    loop = lax.axis_size("loop")
    reps = lax.axis_size("rep")
    me = lax.axis_index("loop").astype(jnp.int32)
    rep = lax.axis_index("rep").astype(jnp.int32)
    count, width = queries.shape
    block = passages.shape[0]
    owners, slots = hard_rows.shape[1:]
    half = width // 2
    chips = loop // 2
    meta = jnp.stack([me, rep])
    both = ("loop", "rep")

    other_rows = exchange(index_rows, ("loop",), 1)
    rest = loop // 4
    wanted = jnp.transpose(hard_rows, (0, 2, 1)).reshape(slots, owners)
    neighbour, (own_wanted,) = exchange(wanted, ("loop",), 2), pack([[(0, 0, slots)]], wanted)
    asked, = pack([[(0, 0, slots), (1, 0, slots)]], own_wanted, neighbour)
    asked = [asked] + [exchange(asked, ("loop",), 4 * k) for k in range(1, rest)]
    own_rows, = pack([[(0, 0, index_rows.shape[0])]], index_rows)

    bits = [loop // 2 >> i for i in range(loop.bit_length() - 4)] + [4, 2, 1]
    orders = [0]
    for bit in bits:
        orders = orders + [o | bit for o in orders]
    for bit in bits[:-4]:
        passages = jnp.concatenate([passages, exchange(passages, ("loop",), bit)], axis=0)
    passages_z = exchange(passages, ("loop",), bits[-4])

    depth = 2 * slots
    have = 2 * passages.shape[0]
    top = chips // 2
    outs = [jax.ShapeDtypeStruct((top * depth, width), jnp.bfloat16)]
    outs += [jax.ShapeDtypeStruct((depth, width), jnp.bfloat16)] * top
    known, = pack([[(i, 0, have // 2) for i in range(2)]], passages, passages_z)
    plane, *sends = pl.pallas_call(
        functools.partial(pick_rows, top, rest),
        out_shape=outs,
        in_specs=[SCALARS] + [WHOLE] * (3 + rest),
        out_specs=[WHOLE] * (1 + top),
        compiler_params=budget(index_rows, index_rows, *outs, *outs),
        cost_estimate=pl.CostEstimate(
            flops=4 * chips * slots * index_rows.shape[0] * width,
            bytes_accessed=3 * index_rows.size * 2, transcendentals=0,
        ),
    )(meta, other_rows, own_rows, passages_z, *asked)

    def send(m, value):
        return exchange(value, ("loop",), 2 * m)

    def over(value):
        return exchange(value, ("rep",), 1)

    def cut(arrays, *pieces):
        return [
            (next(i for i, a in enumerate(arrays) if a is array), first, rows)
            for array, first, rows in pieces
        ]

    half_top = top // 2
    inner, outer = range(1, half_top + 1), range(half_top + 1, top)
    opposite_plane = over(plane)
    middle_masks, late_masks = range(top + 1, chips, 2), range(top, chips, 2)
    sends = dict(zip(range(top, chips), sends))
    middle = [send(m, sends[m]) for m in middle_masks]
    held_back = [sends[m] for m in late_masks]
    known = [known, exchange(known, ("loop",), 4)]

    arrays = [plane, opposite_plane, *middle, *known, *held_back]
    quad = [(value, 0, value.shape[0]) for value in known]
    batch, *going = pack(
        [cut(arrays, *[(value, 0, depth) for value in middle])]
        + [
            cut(arrays, (plane, m * depth, depth), (opposite_plane, m * depth, depth),
                *(quad if m == 1 else []))
            for m in inner
        ]
        + [cut(arrays, (value, 0, depth)) for value in held_back],
        *arrays,
    )
    near_batch, far_batch = batch, over(batch)
    came = [send(m, value) for m, value in zip(inner, going)]
    late = [send(m, value) for m, value in zip(late_masks, going[len(inner):])]

    arrays = [plane, opposite_plane, going[0], *late, *came]
    batch, *pair_and_going = pack(
        [cut(arrays, *[(value, 0, depth) for value in late]),
         cut(arrays, (going[0], 2 * depth, 2 * have)),
         cut(arrays, (came[0], 2 * depth, 2 * have))]
        + [
            cut(arrays, (plane, m * depth, depth), (opposite_plane, m * depth, depth))
            for m in outer
        ],
        *arrays, far_batch,
    )
    pair, going = pair_and_going[:2], pair_and_going[2:]
    last = [send(m, value) for m, value in zip(outer, going)] + [over(batch)]
    other_pair = [exchange(value, ("loop",), 1) for value in pair]

    first_rows = [(value, 2 * have) for value in pair]
    first_rows += [(plane, depth), (opposite_plane, depth)]
    first_rows += [(value, 2 * depth) for value in came]
    first_rows += [(value, value.shape[0]) for value in (near_batch, far_batch, batch)]
    last_rows = [(value, value.shape[0]) for value in (*other_pair, *last)]
    first_places = [(m, p) for m in (0, *inner) for p in range(2)]
    first_places += [(m, p) for p in range(2) for m in middle_masks]
    first_places += [(m, 0) for m in late_masks]
    last_places = [(m, p) for m in outer for p in range(2)] + [(m, 1) for m in late_masks]
    side = loop * block // 2
    columns = (
        (tuple(orders[:loop // 2]), tuple(first_places)),
        (tuple(orders[loop // 2:]), tuple(last_places)),
    )
    first_counts = tuple(n for _, n in first_rows)
    last_counts = tuple(n for _, n in last_rows)

    rows = loop * block
    rows_1 = jax.ShapeDtypeStruct((sum(first_counts), width), jnp.bfloat16)
    rows_2 = jax.ShapeDtypeStruct((sum(last_counts), width), jnp.bfloat16)
    payload = jax.ShapeDtypeStruct((side, width + 2 * LOSS), jnp.float32)
    scores, rows_1 = pl.pallas_call(
        functools.partial(early_kernel, first_counts),
        out_shape=[jax.ShapeDtypeStruct((count, rows_1.shape[0]), jnp.float32), rows_1],
        in_specs=[WHOLE] * (1 + len(first_rows)),
        out_specs=[WHOLE] * 2,
        compiler_params=budget(queries, rows_1, rows_1),
        cost_estimate=pl.CostEstimate(
            flops=2 * count * rows_1.size,
            bytes_accessed=2 * (queries.size + 2 * rows_1.size), transcendentals=0,
        ),
    )(queries, *[value for value, _ in first_rows])
    weights_1, weights_2, rows_2, send_part = pl.pallas_call(
        functools.partial(score_kernel, last_counts, len(other_pair), columns, slots),
        out_shape=[
            jax.ShapeDtypeStruct((count, rows_1.shape[0]), jnp.bfloat16),
            jax.ShapeDtypeStruct((count, rows_2.shape[0]), jnp.bfloat16),
            rows_2, payload,
        ],
        in_specs=[SCALARS] * 2 + [WHOLE] * (3 + len(last_rows)),
        out_specs=[WHOLE] * 4,
        compiler_params=budget(queries, rows_2, rows_2, payload, payload),
        cost_estimate=pl.CostEstimate(
            flops=2 * count * (rows_2.size + payload.size),
            bytes_accessed=2 * (queries.size + 2 * rows_2.size) + 4 * payload.size,
            transcendentals=2 * count * (rows_1.shape[0] + rows_2.shape[0]),
        ),
    )(
        meta, hard_counts, queries, positive.reshape(1, count), scores,
        *last, *other_pair,
    )

    sent = exchange(send_part, ("loop",), 1)
    kept = pl.pallas_call(
        keep_kernel,
        out_shape=jax.ShapeDtypeStruct((rows // 2, width + 2 * LOSS), jnp.float32),
        in_specs=[SCALARS] + [WHOLE] * 3,
        out_specs=WHOLE,
        compiler_params=budget(queries, payload, payload),
        cost_estimate=pl.CostEstimate(
            flops=count * rows * width,
            bytes_accessed=2 * count * width + 2 * rows * width, transcendentals=0,
        ),
    )(meta, weights_1, queries, send_part)
    query_grad, done = pl.pallas_call(
        grad_kernel,
        out_shape=[
            jax.ShapeDtypeStruct((count, width), jnp.float32),
            jax.ShapeDtypeStruct((8, 128), jnp.float32),
        ],
        in_specs=[WHOLE] * 4,
        out_specs=[WHOLE] * 2,
        compiler_params=budget(queries, queries, rows_1, rows_2),
        cost_estimate=pl.CostEstimate(
            flops=2 * count * (rows_1.size + rows_2.size),
            bytes_accessed=2 * (rows_1.size + rows_2.size) + 4 * count * width,
            transcendentals=0,
        ),
    )(weights_1, weights_2, rows_1, rows_2)
    part = half + LOSS
    quarter = rows // 4
    first = jax.ShapeDtypeStruct((quarter, part), jnp.float32)
    short = jax.ShapeDtypeStruct(first.shape, jnp.bfloat16)
    own, *going = pl.pallas_call(
        functools.partial(first_sum, block),
        out_shape=[first, short] + [jax.ShapeDtypeStruct((quarter // 2, part), jnp.float32)] * 4,
        in_specs=[WHOLE] * 2,
        out_specs=[WHOLE] * 6,
        compiler_params=budget(payload, payload, payload),
        cost_estimate=pl.CostEstimate(
            flops=payload.size, bytes_accessed=12 * payload.size, transcendentals=0
        ),
    )(kept, sent)
    came = [exchange(value, both, mask) for value, mask in zip(going, (5, 4, 1, 4, 1))]
    second = jax.ShapeDtypeStruct((block, part), jnp.float32)

    def summed(odd, from_x, from_y, after):
        shapes = [second] * (rest // 2)
        if not odd:
            shapes[1] = jax.ShapeDtypeStruct(second.shape, jnp.bfloat16)
        return pl.pallas_call(
            functools.partial(second_sum, odd),
            out_shape=shapes,
            in_specs=[WHOLE] * 5,
            out_specs=[WHOLE] * (rest // 2),
            compiler_params=budget(payload, payload),
            cost_estimate=pl.CostEstimate(
                flops=2 * first.size, bytes_accessed=10 * first.size, transcendentals=0
            ),
        )(own, came[0], from_x, from_y, after)

    far_sums = summed(1, came[1], came[2], done)
    total, *near_sums = summed(0, came[3], came[4], done)
    going = list(zip(far_sums, orders[1:rest:2])) + list(zip(near_sums, orders[2:rest:2]))
    for value, order in sorted(going, key=lambda pair: -pair[1]):
        total = total + exchange(value, ("loop",), order).astype(jnp.float32)
    mean_loss = (total[0, half] + total[0, half + LOSS // 2]) / (count * loop * reps)
    total = total[:, :half]
    opposite = exchange(total, ("rep",), 1)
    passage_grad = jnp.where(
        rep == 0,
        jnp.concatenate([total, opposite], axis=1),
        jnp.concatenate([opposite, total], axis=1),
    )

    return (query_grad, passage_grad, mean_loss)


def solution(mesh):
    placed = (
        P(("loop", "rep"), None),
        P("loop", None),
        P(("loop", "rep"), None),
        P(("loop", "rep")),
        P("loop", None, None),
        P("loop", None),
    )
    return jax.shard_map(
        shards,
        mesh=mesh,
        in_specs=placed,
        out_specs=(P(("loop", "rep"), None), P("loop", None), P()),
        check_vma=False,
    )
```

```python
import functools

import jax
import jax.numpy as jnp
from jax import lax
from jax.experimental import pallas as pl
from jax.experimental.pallas import tpu as pltpu
from jax.sharding import PartitionSpec as P


def budget(*arrays):
    total = sum(a.size * a.dtype.itemsize for a in arrays)
    return pltpu.CompilerParams(vmem_limit_bytes=total + total // 4 + 6 * 1024 * 1024)


WHOLE = pl.BlockSpec(memory_space=pltpu.VMEM)
SCALARS = pl.BlockSpec(memory_space=pltpu.SMEM)
LOSS = 128


def exchange(value, axes, mask):
    size = 1
    for axis in axes:
        size *= lax.axis_size(axis)
    return lax.ppermute(value, axes, [(i, i ^ mask) for i in range(size)])


def pick_rows(count, reach, meta, other, own, after, *refs):
    asked, (plane, *pieces) = refs[:reach], refs[reach:]
    me, rep = meta[0], meta[1]
    owners = asked[0].shape[1]
    slots = plane.shape[0] // (2 * count)
    lanes = lax.broadcasted_iota(jnp.int32, (slots, owners), 1)
    rows = lax.broadcasted_iota(jnp.int32, (slots, own.shape[0]), 1)

    def hot(owner):
        picked = []
        for m in range(count + len(pieces)):
            at = m % 2 * slots
            tile = asked[m // 2][at:at + slots, :]
            column = jnp.sum(jnp.where(lanes == owner, tile, 0), axis=1, keepdims=True)
            picked.append(jnp.where(column == rows, 1.0, 0.0))
        return jnp.concatenate(picked, axis=0).astype(jnp.bfloat16)

    hot_own = hot(me * 2 + rep)
    hot_other = hot((me ^ 1) * 2 + rep)
    got_other = jnp.dot(hot_other, other[...], preferred_element_type=jnp.float32)
    got_own = jnp.dot(hot_own, own[...], preferred_element_type=jnp.float32)
    for m in range(count + len(pieces)):
        part = slice(m * slots, (m + 1) * slots)
        value = jnp.concatenate([got_own[part], got_other[part]], axis=0).astype(jnp.bfloat16)
        if m < count:
            plane[m * 2 * slots:(m + 1) * 2 * slots, :] = value
        else:
            pieces[m - count][...] = value


def pack_kernel(layouts, *refs):
    ins, outs = refs[:-len(layouts)], refs[-len(layouts):]
    for layout, out in zip(layouts, outs):
        at = 0
        for which, first, rows in layout:
            out[at:at + rows, :] = ins[which][first:first + rows, :]
            at += rows


def pack(layouts, *arrays):
    shapes = [
        jax.ShapeDtypeStruct((sum(rows for _, _, rows in layout), arrays[0].shape[1]), arrays[0].dtype)
        for layout in layouts
    ]
    size = sum(shape.size for shape in shapes)
    return pl.pallas_call(
        functools.partial(pack_kernel, layouts),
        out_shape=shapes,
        in_specs=[WHOLE] * len(arrays),
        out_specs=[WHOLE] * len(layouts),
        compiler_params=budget(*shapes, *arrays),
        cost_estimate=pl.CostEstimate(flops=size, bytes_accessed=4 * size, transcendentals=0),
    )(*arrays)


def stack(counts, refs, out):
    at = 0
    for rows, ref in zip(counts, refs):
        out[at:at + rows, :] = ref[:rows, :]
        at += rows


def scored(queries, rows):
    return 50.0 * lax.dot_general(
        queries[...], rows[...], (((1,), (1,)), ((), ())), preferred_element_type=jnp.float32
    )


def early_kernel(counts, queries, *refs):
    *batches, scores_out, rows = refs
    stack(counts, batches, rows)
    scores_out[...] = scored(queries, rows)


def lookup(index, values):
    total = jnp.zeros_like(index)
    for i, value in enumerate(values):
        total = jnp.where(index == i, value, total)
    return total


def score_kernel(
    counts, passages, columns, slots, meta, hard_counts, queries, positive, scores_ref, *refs
):
    *batches, out_1, out_2, rows, send_out = refs
    batches = batches[-passages:] + batches[:-passages]
    me, rep = meta[0], meta[1]
    stack(counts, batches, rows)
    side = send_out.shape[0]
    block = side // len(columns[0][0])
    blocks = [scores_ref[...], scored(queries, rows)]
    wanted = jnp.broadcast_to(positive[...].astype(jnp.float32), (8, positive.shape[1]))
    wanted = jnp.transpose(wanted)[:, :1]
    onehots = []
    for i, (order, places) in enumerate(columns):
        lane = lax.broadcasted_iota(jnp.int32, (1, blocks[i].shape[1]), 1)
        passage = lane < side
        ids = (lookup(lane // block, order) * block + lane % block) ^ (me * block)
        spot = jnp.where(passage, 0, lane - side)
        owner = lookup(spot // (2 * slots), [4 * m + p for m, p in places])
        owner = (owner + spot // slots % 2 * 2) ^ (me * 2 + rep)
        taken = lookup(owner, [hard_counts[0, o] for o in range(hard_counts.shape[1])])
        live = passage | (spot % slots < taken)
        onehots.append(
            jnp.where((wanted == ids.astype(jnp.float32)) & passage, 1.0, 0.0)
        )
        blocks[i] = jnp.where(live, blocks[i], -jnp.inf)
    tops = [jnp.max(value, axis=1, keepdims=True) for value in blocks]
    row_top = jnp.maximum(tops[0], tops[1])
    sums = [jnp.sum(jnp.exp(value - row_top), axis=1, keepdims=True) for value in blocks]
    log_total = row_top + jnp.log(sums[0] + sums[1])
    weights = [
        (jnp.exp(value - log_total) - onehot).astype(jnp.bfloat16)
        for value, onehot in zip(blocks, onehots)
    ]
    hit = sum(
        jnp.sum(jnp.where(onehot > 0, value, 0.0), axis=1, keepdims=True)
        for value, onehot in zip(blocks, onehots)
    )
    project(send_out, weights[1][:, :side], queries, meta[1], jnp.sum(log_total - hit))
    out_1[...] = weights[0]
    out_2[...] = weights[1]


def project(out, weights, queries, rep, loss):
    half = queries.shape[1] // 2
    for i, side in enumerate((rep, 1 - rep)):
        product = lax.dot_general(
            weights, queries[:, pl.ds(pl.multiple_of(side * half, half), half)],
            (((0,), (0,)), ((), ())), preferred_element_type=jnp.float32,
        )
        at = i * (half + LOSS)
        out[:, at:at + half] = 50.0 * product
        out[:, at + half:at + half + LOSS] = jnp.full((out.shape[0], LOSS), loss, jnp.float32)


def keep_kernel(meta, weights, queries, send, out):
    half = queries.shape[1] // 2
    project(
        out, weights[:, :out.shape[0]], queries, meta[1], send[0:1, half:half + 1]
    )


def first_sum(block, kept, sent, own, to_xy, *halves):
    rows, columns = own.shape
    half = columns - LOSS
    lanes = lax.broadcasted_iota(jnp.int32, (block, LOSS), 1)
    cuts = []
    for i in range(rows // block):
        x_out, y_out = halves[:2] if i % 2 else halves[2:]
        for out, at, down, across in (
            (own, i, 0, 0), (to_xy, i, 1, 1), (x_out, i // 2, 1, 0), (y_out, i // 2, 0, 1)
        ):
            cuts.append((out, at * block, down * rows + i * block, across * columns))
    for out, to, row, column in cuts:
        at, to = pl.ds(row, block), pl.ds(to, block)
        data, tile = pl.ds(column, half), pl.ds(column + half, LOSS)
        out[to, :half] = (kept[at, data] + sent[at, data]).astype(out.dtype)
        loss = kept[at, tile] + sent[at, tile]
        high = loss.astype(jnp.bfloat16).astype(jnp.float32)
        out[to, half:] = jnp.where(lanes < LOSS // 2, high, loss - high).astype(out.dtype)


def second_sum(odd, own, from_xy, from_x, from_y, after, *outs):
    rows, columns = outs[0].shape
    half = columns - LOSS
    lanes = lax.broadcasted_iota(jnp.int32, (rows, LOSS), 1)
    for i, out in enumerate(outs):
        at, near = pl.ds((2 * i + odd) * rows, rows), pl.ds(i * rows, rows)
        total = (own[at] + from_x[near].astype(jnp.float32)) + (
            from_y[near].astype(jnp.float32) + from_xy[at].astype(jnp.float32)
        )
        if out.dtype == jnp.float32:
            out[...] = total
        else:
            loss = total[:, half:half + 1] + total[:, half + LOSS // 2:half + LOSS // 2 + 1]
            high = loss.astype(jnp.bfloat16).astype(jnp.float32)
            out[:, :half] = total[:, :half].astype(out.dtype)
            out[:, half:] = jnp.where(lanes < LOSS // 2, high, loss - high).astype(out.dtype)


def grad_kernel(weights_1, weights_2, rows_1, rows_2, out, done):
    done[...] = jnp.zeros(done.shape, done.dtype)
    out[...] = 50.0 * (
        jnp.dot(weights_1[...], rows_1[...], preferred_element_type=jnp.float32)
        + jnp.dot(weights_2[...], rows_2[...], preferred_element_type=jnp.float32)
    )


def shards(queries, passages, index_rows, positive, hard_rows, hard_counts):
    loop = lax.axis_size("loop")
    reps = lax.axis_size("rep")
    me = lax.axis_index("loop").astype(jnp.int32)
    rep = lax.axis_index("rep").astype(jnp.int32)
    count, width = queries.shape
    block = passages.shape[0]
    owners, slots = hard_rows.shape[1:]
    half = width // 2
    chips = loop // 2
    meta = jnp.stack([me, rep])
    both = ("loop", "rep")

    other_rows = exchange(index_rows, ("loop",), 1)
    rest = loop // 4
    wanted = jnp.transpose(hard_rows, (0, 2, 1)).reshape(slots, owners)
    neighbour, (own_wanted,) = exchange(wanted, ("loop",), 2), pack([[(0, 0, slots)]], wanted)
    asked, = pack([[(0, 0, slots), (1, 0, slots)]], own_wanted, neighbour)
    asked = [asked] + [exchange(asked, ("loop",), 4 * k) for k in range(1, rest)]
    own_rows, = pack([[(0, 0, index_rows.shape[0])]], index_rows)

    bits = [loop // 2 >> i for i in range(loop.bit_length() - 4)] + [4, 2, 1]
    orders = [0]
    for bit in bits:
        orders = orders + [o | bit for o in orders]
    for bit in bits[:-4]:
        passages = jnp.concatenate([passages, exchange(passages, ("loop",), bit)], axis=0)
    passages_z = exchange(passages, ("loop",), bits[-4])

    depth = 2 * slots
    have = 2 * passages.shape[0]
    top = chips // 2
    outs = [jax.ShapeDtypeStruct((top * depth, width), jnp.bfloat16)]
    outs += [jax.ShapeDtypeStruct((depth, width), jnp.bfloat16)] * top
    known, = pack([[(i, 0, have // 2) for i in range(2)]], passages, passages_z)
    plane, *sends = pl.pallas_call(
        functools.partial(pick_rows, top, rest),
        out_shape=outs,
        in_specs=[SCALARS] + [WHOLE] * (3 + rest),
        out_specs=[WHOLE] * (1 + top),
        compiler_params=budget(index_rows, index_rows, *outs, *outs),
        cost_estimate=pl.CostEstimate(
            flops=4 * chips * slots * index_rows.shape[0] * width,
            bytes_accessed=3 * index_rows.size * 2, transcendentals=0,
        ),
    )(meta, other_rows, own_rows, passages_z, *asked)

    def send(m, value):
        return exchange(value, ("loop",), 2 * m)

    def over(value):
        return exchange(value, ("rep",), 1)

    def cut(arrays, *pieces):
        return [
            (next(i for i, a in enumerate(arrays) if a is array), first, rows)
            for array, first, rows in pieces
        ]

    half_top = top // 2
    inner, outer = range(1, half_top + 1), range(half_top + 1, top)
    opposite_plane = over(plane)
    middle_masks, late_masks = range(top + 1, chips, 2), range(top, chips, 2)
    sends = dict(zip(range(top, chips), sends))
    middle = [send(m, sends[m]) for m in middle_masks]
    held_back = [sends[m] for m in late_masks]
    known = [known, exchange(known, ("loop",), 4)]

    arrays = [plane, opposite_plane, *middle, *known, *held_back]
    quad = [(value, 0, value.shape[0]) for value in known]
    batch, *going = pack(
        [cut(arrays, *[(value, 0, depth) for value in middle])]
        + [
            cut(arrays, (plane, m * depth, depth), (opposite_plane, m * depth, depth),
                *(quad if m == 1 else []))
            for m in inner
        ]
        + [cut(arrays, (value, 0, depth)) for value in held_back],
        *arrays,
    )
    near_batch, far_batch = batch, over(batch)
    came = [send(m, value) for m, value in zip(inner, going)]
    late = [send(m, value) for m, value in zip(late_masks, going[len(inner):])]

    arrays = [plane, opposite_plane, going[0], *late, *came]
    batch, *pair_and_going = pack(
        [cut(arrays, *[(value, 0, depth) for value in late]),
         cut(arrays, (going[0], 2 * depth, 2 * have)),
         cut(arrays, (came[0], 2 * depth, 2 * have))]
        + [
            cut(arrays, (plane, m * depth, depth), (opposite_plane, m * depth, depth))
            for m in outer
        ],
        *arrays, far_batch,
    )
    pair, going = pair_and_going[:2], pair_and_going[2:]
    last = [send(m, value) for m, value in zip(outer, going)] + [over(batch)]
    other_pair = [exchange(value, ("loop",), 1) for value in pair]

    first_rows = [(value, 2 * have) for value in pair]
    first_rows += [(plane, depth), (opposite_plane, depth)]
    first_rows += [(value, 2 * depth) for value in came]
    first_rows += [(value, value.shape[0]) for value in (near_batch, far_batch, batch)]
    last_rows = [(value, value.shape[0]) for value in (*other_pair, *last)]
    first_places = [(m, p) for m in (0, *inner) for p in range(2)]
    first_places += [(m, p) for p in range(2) for m in middle_masks]
    first_places += [(m, 0) for m in late_masks]
    last_places = [(m, p) for m in outer for p in range(2)] + [(m, 1) for m in late_masks]
    side = loop * block // 2
    columns = (
        (tuple(orders[:loop // 2]), tuple(first_places)),
        (tuple(orders[loop // 2:]), tuple(last_places)),
    )
    first_counts = tuple(n for _, n in first_rows)
    last_counts = tuple(n for _, n in last_rows)

    rows = loop * block
    rows_1 = jax.ShapeDtypeStruct((sum(first_counts), width), jnp.bfloat16)
    rows_2 = jax.ShapeDtypeStruct((sum(last_counts), width), jnp.bfloat16)
    payload = jax.ShapeDtypeStruct((side, width + 2 * LOSS), jnp.float32)
    scores, rows_1 = pl.pallas_call(
        functools.partial(early_kernel, first_counts),
        out_shape=[jax.ShapeDtypeStruct((count, rows_1.shape[0]), jnp.float32), rows_1],
        in_specs=[WHOLE] * (1 + len(first_rows)),
        out_specs=[WHOLE] * 2,
        compiler_params=budget(queries, rows_1, rows_1),
        cost_estimate=pl.CostEstimate(
            flops=2 * count * rows_1.size,
            bytes_accessed=2 * (queries.size + 2 * rows_1.size), transcendentals=0,
        ),
    )(queries, *[value for value, _ in first_rows])
    weights_1, weights_2, rows_2, send_part = pl.pallas_call(
        functools.partial(score_kernel, last_counts, len(other_pair), columns, slots),
        out_shape=[
            jax.ShapeDtypeStruct((count, rows_1.shape[0]), jnp.bfloat16),
            jax.ShapeDtypeStruct((count, rows_2.shape[0]), jnp.bfloat16),
            rows_2, payload,
        ],
        in_specs=[SCALARS] * 2 + [WHOLE] * (3 + len(last_rows)),
        out_specs=[WHOLE] * 4,
        compiler_params=budget(queries, rows_2, rows_2, payload, payload),
        cost_estimate=pl.CostEstimate(
            flops=2 * count * (rows_2.size + payload.size),
            bytes_accessed=2 * (queries.size + 2 * rows_2.size) + 4 * payload.size,
            transcendentals=2 * count * (rows_1.shape[0] + rows_2.shape[0]),
        ),
    )(
        meta, hard_counts, queries, positive.reshape(1, count), scores,
        *last, *other_pair,
    )

    sent = exchange(send_part, ("loop",), 1)
    kept = pl.pallas_call(
        keep_kernel,
        out_shape=jax.ShapeDtypeStruct((rows // 2, width + 2 * LOSS), jnp.float32),
        in_specs=[SCALARS] + [WHOLE] * 3,
        out_specs=WHOLE,
        compiler_params=budget(queries, payload, payload),
        cost_estimate=pl.CostEstimate(
            flops=count * rows * width,
            bytes_accessed=2 * count * width + 2 * rows * width, transcendentals=0,
        ),
    )(meta, weights_1, queries, send_part)
    query_grad, done = pl.pallas_call(
        grad_kernel,
        out_shape=[
            jax.ShapeDtypeStruct((count, width), jnp.float32),
            jax.ShapeDtypeStruct((8, 128), jnp.float32),
        ],
        in_specs=[WHOLE] * 4,
        out_specs=[WHOLE] * 2,
        compiler_params=budget(queries, queries, rows_1, rows_2),
        cost_estimate=pl.CostEstimate(
            flops=2 * count * (rows_1.size + rows_2.size),
            bytes_accessed=2 * (rows_1.size + rows_2.size) + 4 * count * width,
            transcendentals=0,
        ),
    )(weights_1, weights_2, rows_1, rows_2)
    part = half + LOSS
    quarter = rows // 4
    first = jax.ShapeDtypeStruct((quarter, part), jnp.float32)
    short = jax.ShapeDtypeStruct(first.shape, jnp.bfloat16)
    own, *going = pl.pallas_call(
        functools.partial(first_sum, block),
        out_shape=[first, short] + [
            jax.ShapeDtypeStruct((quarter // 2, part), dtype)
            for dtype in (jnp.float32, jnp.float32, jnp.bfloat16, jnp.bfloat16)
        ],
        in_specs=[WHOLE] * 2,
        out_specs=[WHOLE] * 6,
        compiler_params=budget(payload, payload, payload),
        cost_estimate=pl.CostEstimate(
            flops=payload.size, bytes_accessed=12 * payload.size, transcendentals=0
        ),
    )(kept, sent)
    came = [exchange(value, both, mask) for value, mask in zip(going, (5, 4, 1, 4, 1))]
    second = jax.ShapeDtypeStruct((block, part), jnp.float32)

    def summed(odd, from_x, from_y, after):
        shapes = [second] * (rest // 2)
        return pl.pallas_call(
            functools.partial(second_sum, odd),
            out_shape=shapes,
            in_specs=[WHOLE] * 5,
            out_specs=[WHOLE] * (rest // 2),
            compiler_params=budget(payload, payload),
            cost_estimate=pl.CostEstimate(
                flops=2 * first.size, bytes_accessed=10 * first.size, transcendentals=0
            ),
        )(own, came[0], from_x, from_y, after)

    far_sums = summed(1, came[1], came[2], done)
    total, *near_sums = summed(0, came[3], came[4], done)
    going = list(zip(far_sums, orders[1:rest:2])) + list(zip(near_sums, orders[2:rest:2]))
    for value, order in sorted(going, key=lambda pair: -pair[1]):
        total = total + exchange(value, ("loop",), order).astype(jnp.float32)
    mean_loss = (total[0, half] + total[0, half + LOSS // 2]) / (count * loop * reps)
    total = total[:, :half]
    opposite = exchange(total, ("rep",), 1)
    passage_grad = jnp.where(
        rep == 0,
        jnp.concatenate([total, opposite], axis=1),
        jnp.concatenate([opposite, total], axis=1),
    )

    return (query_grad, passage_grad, mean_loss)


def solution(mesh):
    placed = (
        P(("loop", "rep"), None),
        P("loop", None),
        P(("loop", "rep"), None),
        P(("loop", "rep")),
        P("loop", None, None),
        P("loop", None),
    )
    return jax.shard_map(
        shards,
        mesh=mesh,
        in_specs=placed,
        out_specs=(P(("loop", "rep"), None), P("loop", None), P()),
        check_vma=False,
    )
```

```python
import functools

import jax
import jax.numpy as jnp
from jax import lax
from jax.experimental import pallas as pl
from jax.experimental.pallas import tpu as pltpu
from jax.sharding import PartitionSpec as P


def budget(*arrays):
    total = sum(a.size * a.dtype.itemsize for a in arrays)
    return pltpu.CompilerParams(vmem_limit_bytes=total + total // 4 + 6 * 1024 * 1024)


WHOLE = pl.BlockSpec(memory_space=pltpu.VMEM)
SCALARS = pl.BlockSpec(memory_space=pltpu.SMEM)
LOSS = 128


def exchange(value, axes, mask):
    size = 1
    for axis in axes:
        size *= lax.axis_size(axis)
    return lax.ppermute(value, axes, [(i, i ^ mask) for i in range(size)])


def pick_rows(count, reach, meta, other, own, after, *refs):
    asked, (plane, *pieces) = refs[:reach], refs[reach:]
    me, rep = meta[0], meta[1]
    owners = asked[0].shape[1]
    slots = plane.shape[0] // (2 * count)
    lanes = lax.broadcasted_iota(jnp.int32, (slots, owners), 1)
    rows = lax.broadcasted_iota(jnp.int32, (slots, own.shape[0]), 1)

    def hot(owner):
        picked = []
        for m in range(count + len(pieces)):
            at = m % 2 * slots
            tile = asked[m // 2][at:at + slots, :]
            column = jnp.sum(jnp.where(lanes == owner, tile, 0), axis=1, keepdims=True)
            picked.append(jnp.where(column == rows, 1.0, 0.0))
        return jnp.concatenate(picked, axis=0).astype(jnp.bfloat16)

    hot_own = hot(me * 2 + rep)
    hot_other = hot((me ^ 1) * 2 + rep)
    got_other = jnp.dot(hot_other, other[...], preferred_element_type=jnp.float32)
    got_own = jnp.dot(hot_own, own[...], preferred_element_type=jnp.float32)
    for m in range(count + len(pieces)):
        part = slice(m * slots, (m + 1) * slots)
        value = jnp.concatenate([got_own[part], got_other[part]], axis=0).astype(jnp.bfloat16)
        if m < count:
            plane[m * 2 * slots:(m + 1) * 2 * slots, :] = value
        else:
            pieces[m - count][...] = value


def pack_kernel(layouts, *refs):
    ins, outs = refs[:-len(layouts)], refs[-len(layouts):]
    for layout, out in zip(layouts, outs):
        at = 0
        for which, first, rows in layout:
            out[at:at + rows, :] = ins[which][first:first + rows, :]
            at += rows


def pack(layouts, *arrays):
    shapes = [
        jax.ShapeDtypeStruct((sum(rows for _, _, rows in layout), arrays[0].shape[1]), arrays[0].dtype)
        for layout in layouts
    ]
    size = sum(shape.size for shape in shapes)
    return pl.pallas_call(
        functools.partial(pack_kernel, layouts),
        out_shape=shapes,
        in_specs=[WHOLE] * len(arrays),
        out_specs=[WHOLE] * len(layouts),
        compiler_params=budget(*shapes, *arrays),
        cost_estimate=pl.CostEstimate(flops=size, bytes_accessed=4 * size, transcendentals=0),
    )(*arrays)


def stack(counts, refs, out):
    at = 0
    for rows, ref in zip(counts, refs):
        out[at:at + rows, :] = ref[:rows, :]
        at += rows


def scored(queries, rows):
    return 50.0 * lax.dot_general(
        queries[...], rows[...], (((1,), (1,)), ((), ())), preferred_element_type=jnp.float32
    )


def early_kernel(counts, queries, *refs):
    *batches, scores_out, rows = refs
    stack(counts, batches, rows)
    scores_out[...] = scored(queries, rows)


def lookup(index, values):
    total = jnp.zeros_like(index)
    for i, value in enumerate(values):
        total = jnp.where(index == i, value, total)
    return total


def score_kernel(
    counts, passages, columns, slots, meta, hard_counts, queries, positive, scores_ref, *refs
):
    *batches, out_1, out_2, rows, send_out = refs
    batches = batches[-passages:] + batches[:-passages]
    me, rep = meta[0], meta[1]
    stack(counts, batches, rows)
    side = send_out.shape[0]
    block = side // len(columns[0][0])
    blocks = [scores_ref[...], scored(queries, rows)]
    wanted = jnp.broadcast_to(positive[...].astype(jnp.float32), (8, positive.shape[1]))
    wanted = jnp.transpose(wanted)[:, :1]
    onehots = []
    for i, (order, places) in enumerate(columns):
        lane = lax.broadcasted_iota(jnp.int32, (1, blocks[i].shape[1]), 1)
        passage = lane < side
        ids = (lookup(lane // block, order) * block + lane % block) ^ (me * block)
        spot = jnp.where(passage, 0, lane - side)
        owner = lookup(spot // (2 * slots), [4 * m + p for m, p in places])
        owner = (owner + spot // slots % 2 * 2) ^ (me * 2 + rep)
        taken = lookup(owner, [hard_counts[0, o] for o in range(hard_counts.shape[1])])
        live = passage | (spot % slots < taken)
        onehots.append(
            jnp.where((wanted == ids.astype(jnp.float32)) & passage, 1.0, 0.0)
        )
        blocks[i] = jnp.where(live, blocks[i], -jnp.inf)
    tops = [jnp.max(value, axis=1, keepdims=True) for value in blocks]
    row_top = jnp.maximum(tops[0], tops[1])
    sums = [jnp.sum(jnp.exp(value - row_top), axis=1, keepdims=True) for value in blocks]
    log_total = row_top + jnp.log(sums[0] + sums[1])
    weights = [
        (jnp.exp(value - log_total) - onehot).astype(jnp.bfloat16)
        for value, onehot in zip(blocks, onehots)
    ]
    hit = sum(
        jnp.sum(jnp.where(onehot > 0, value, 0.0), axis=1, keepdims=True)
        for value, onehot in zip(blocks, onehots)
    )
    project(send_out, weights[1][:, :side], queries, meta[1], jnp.sum(log_total - hit))
    out_1[...] = weights[0]
    out_2[...] = weights[1]


def project(out, weights, queries, rep, loss):
    half = queries.shape[1] // 2
    for i, side in enumerate((rep, 1 - rep)):
        product = lax.dot_general(
            weights, queries[:, pl.ds(pl.multiple_of(side * half, half), half)],
            (((0,), (0,)), ((), ())), preferred_element_type=jnp.float32,
        )
        at = i * (half + LOSS)
        out[:, at:at + half] = 50.0 * product
        out[:, at + half:at + half + LOSS] = jnp.full((out.shape[0], LOSS), loss, jnp.float32)


def keep_kernel(meta, weights, queries, send, out):
    half = queries.shape[1] // 2
    project(
        out, weights[:, :out.shape[0]], queries, meta[1], send[0:1, half:half + 1]
    )


def first_sum(block, kept, sent, own, to_xy, *halves):
    rows, columns = own.shape
    half = columns - LOSS
    lanes = lax.broadcasted_iota(jnp.int32, (block, LOSS), 1)
    cuts = []
    for i in range(rows // block):
        x_out, y_out = halves[:2] if i % 2 else halves[2:]
        for out, at, down, across in (
            (own, i, 0, 0), (to_xy, i, 1, 1), (x_out, i // 2, 1, 0), (y_out, i // 2, 0, 1)
        ):
            cuts.append((out, at * block, down * rows + i * block, across * columns))
    for out, to, row, column in cuts:
        at, to = pl.ds(row, block), pl.ds(to, block)
        data, tile = pl.ds(column, half), pl.ds(column + half, LOSS)
        out[to, :half] = (kept[at, data] + sent[at, data]).astype(out.dtype)
        loss = kept[at, tile] + sent[at, tile]
        high = loss.astype(jnp.bfloat16).astype(jnp.float32)
        out[to, half:] = jnp.where(lanes < LOSS // 2, high, loss - high).astype(out.dtype)


def second_sum(odd, own, from_xy, from_x, from_y, *outs):
    rows, columns = outs[0].shape
    half = columns - LOSS
    lanes = lax.broadcasted_iota(jnp.int32, (rows, LOSS), 1)
    for i, out in enumerate(outs):
        at, near = pl.ds((2 * i + odd) * rows, rows), pl.ds(i * rows, rows)
        total = (own[at] + from_x[near].astype(jnp.float32)) + (
            from_y[near].astype(jnp.float32) + from_xy[at].astype(jnp.float32)
        )
        if out.dtype == jnp.float32:
            out[...] = total
        else:
            loss = total[:, half:half + 1] + total[:, half + LOSS // 2:half + LOSS // 2 + 1]
            high = loss.astype(jnp.bfloat16).astype(jnp.float32)
            out[:, :half] = total[:, :half].astype(out.dtype)
            out[:, half:] = jnp.where(lanes < LOSS // 2, high, loss - high).astype(out.dtype)


def last_sum(after, *refs):
    *parts, out = refs
    total = parts[0][...]
    for part in parts[1:]:
        total = total + part[...]
    out[...] = total


def grad_kernel(weights_1, weights_2, rows_1, rows_2, out, done):
    done[...] = jnp.zeros(done.shape, done.dtype)
    out[...] = 50.0 * (
        jnp.dot(weights_1[...], rows_1[...], preferred_element_type=jnp.float32)
        + jnp.dot(weights_2[...], rows_2[...], preferred_element_type=jnp.float32)
    )


def shards(queries, passages, index_rows, positive, hard_rows, hard_counts):
    loop = lax.axis_size("loop")
    reps = lax.axis_size("rep")
    me = lax.axis_index("loop").astype(jnp.int32)
    rep = lax.axis_index("rep").astype(jnp.int32)
    count, width = queries.shape
    block = passages.shape[0]
    owners, slots = hard_rows.shape[1:]
    half = width // 2
    chips = loop // 2
    meta = jnp.stack([me, rep])
    both = ("loop", "rep")

    other_rows = exchange(index_rows, ("loop",), 1)
    rest = loop // 4
    wanted = jnp.transpose(hard_rows, (0, 2, 1)).reshape(slots, owners)
    neighbour, (own_wanted,) = exchange(wanted, ("loop",), 2), pack([[(0, 0, slots)]], wanted)
    asked, = pack([[(0, 0, slots), (1, 0, slots)]], own_wanted, neighbour)
    asked = [asked] + [exchange(asked, ("loop",), 4 * k) for k in range(1, rest)]
    own_rows, = pack([[(0, 0, index_rows.shape[0])]], index_rows)

    bits = [loop // 2 >> i for i in range(loop.bit_length() - 4)] + [4, 2, 1]
    orders = [0]
    for bit in bits:
        orders = orders + [o | bit for o in orders]
    for bit in bits[:-4]:
        passages = jnp.concatenate([passages, exchange(passages, ("loop",), bit)], axis=0)
    passages_z = exchange(passages, ("loop",), bits[-4])

    depth = 2 * slots
    have = 2 * passages.shape[0]
    top = chips // 2
    outs = [jax.ShapeDtypeStruct((top * depth, width), jnp.bfloat16)]
    outs += [jax.ShapeDtypeStruct((depth, width), jnp.bfloat16)] * top
    known, = pack([[(i, 0, have // 2) for i in range(2)]], passages, passages_z)
    plane, *sends = pl.pallas_call(
        functools.partial(pick_rows, top, rest),
        out_shape=outs,
        in_specs=[SCALARS] + [WHOLE] * (3 + rest),
        out_specs=[WHOLE] * (1 + top),
        compiler_params=budget(index_rows, index_rows, *outs, *outs),
        cost_estimate=pl.CostEstimate(
            flops=4 * chips * slots * index_rows.shape[0] * width,
            bytes_accessed=3 * index_rows.size * 2, transcendentals=0,
        ),
    )(meta, other_rows, own_rows, passages_z, *asked)

    def send(m, value):
        return exchange(value, ("loop",), 2 * m)

    def over(value):
        return exchange(value, ("rep",), 1)

    def cut(arrays, *pieces):
        return [
            (next(i for i, a in enumerate(arrays) if a is array), first, rows)
            for array, first, rows in pieces
        ]

    half_top = top // 2
    inner, outer = range(1, half_top + 1), range(half_top + 1, top)
    opposite_plane = over(plane)
    middle_masks, late_masks = range(top + 1, chips, 2), range(top, chips, 2)
    sends = dict(zip(range(top, chips), sends))
    middle = [send(m, sends[m]) for m in middle_masks]
    held_back = [sends[m] for m in late_masks]
    known = [known, exchange(known, ("loop",), 4)]

    arrays = [plane, opposite_plane, *middle, *known, *held_back]
    quad = [(value, 0, value.shape[0]) for value in known]
    batch, *going = pack(
        [cut(arrays, *[(value, 0, depth) for value in middle])]
        + [
            cut(arrays, (plane, m * depth, depth), (opposite_plane, m * depth, depth),
                *(quad if m == 1 else []))
            for m in inner
        ]
        + [cut(arrays, (value, 0, depth)) for value in held_back],
        *arrays,
    )
    near_batch, far_batch = batch, over(batch)
    came = [send(m, value) for m, value in zip(inner, going)]
    late = [send(m, value) for m, value in zip(late_masks, going[len(inner):])]

    arrays = [plane, opposite_plane, going[0], *late, *came]
    batch, *pair_and_going = pack(
        [cut(arrays, *[(value, 0, depth) for value in late]),
         cut(arrays, (going[0], 2 * depth, 2 * have)),
         cut(arrays, (came[0], 2 * depth, 2 * have))]
        + [
            cut(arrays, (plane, m * depth, depth), (opposite_plane, m * depth, depth))
            for m in outer
        ],
        *arrays, far_batch,
    )
    pair, going = pair_and_going[:2], pair_and_going[2:]
    last = [send(m, value) for m, value in zip(outer, going)] + [over(batch)]
    other_pair = [exchange(value, ("loop",), 1) for value in pair]

    first_rows = [(value, 2 * have) for value in pair]
    first_rows += [(plane, depth), (opposite_plane, depth)]
    first_rows += [(value, 2 * depth) for value in came]
    first_rows += [(value, value.shape[0]) for value in (near_batch, far_batch, batch)]
    last_rows = [(value, value.shape[0]) for value in (*other_pair, *last)]
    first_places = [(m, p) for m in (0, *inner) for p in range(2)]
    first_places += [(m, p) for p in range(2) for m in middle_masks]
    first_places += [(m, 0) for m in late_masks]
    last_places = [(m, p) for m in outer for p in range(2)] + [(m, 1) for m in late_masks]
    side = loop * block // 2
    columns = (
        (tuple(orders[:loop // 2]), tuple(first_places)),
        (tuple(orders[loop // 2:]), tuple(last_places)),
    )
    first_counts = tuple(n for _, n in first_rows)
    last_counts = tuple(n for _, n in last_rows)

    rows = loop * block
    rows_1 = jax.ShapeDtypeStruct((sum(first_counts), width), jnp.bfloat16)
    rows_2 = jax.ShapeDtypeStruct((sum(last_counts), width), jnp.bfloat16)
    payload = jax.ShapeDtypeStruct((side, width + 2 * LOSS), jnp.float32)
    scores, rows_1 = pl.pallas_call(
        functools.partial(early_kernel, first_counts),
        out_shape=[jax.ShapeDtypeStruct((count, rows_1.shape[0]), jnp.float32), rows_1],
        in_specs=[WHOLE] * (1 + len(first_rows)),
        out_specs=[WHOLE] * 2,
        compiler_params=budget(queries, rows_1, rows_1),
        cost_estimate=pl.CostEstimate(
            flops=2 * count * rows_1.size,
            bytes_accessed=2 * (queries.size + 2 * rows_1.size), transcendentals=0,
        ),
    )(queries, *[value for value, _ in first_rows])
    weights_1, weights_2, rows_2, send_part = pl.pallas_call(
        functools.partial(score_kernel, last_counts, len(other_pair), columns, slots),
        out_shape=[
            jax.ShapeDtypeStruct((count, rows_1.shape[0]), jnp.bfloat16),
            jax.ShapeDtypeStruct((count, rows_2.shape[0]), jnp.bfloat16),
            rows_2, payload,
        ],
        in_specs=[SCALARS] * 2 + [WHOLE] * (3 + len(last_rows)),
        out_specs=[WHOLE] * 4,
        compiler_params=budget(queries, rows_2, rows_2, payload, payload),
        cost_estimate=pl.CostEstimate(
            flops=2 * count * (rows_2.size + payload.size),
            bytes_accessed=2 * (queries.size + 2 * rows_2.size) + 4 * payload.size,
            transcendentals=2 * count * (rows_1.shape[0] + rows_2.shape[0]),
        ),
    )(
        meta, hard_counts, queries, positive.reshape(1, count), scores,
        *last, *other_pair,
    )

    sent = exchange(send_part, ("loop",), 1)
    kept = pl.pallas_call(
        keep_kernel,
        out_shape=jax.ShapeDtypeStruct((rows // 2, width + 2 * LOSS), jnp.float32),
        in_specs=[SCALARS] + [WHOLE] * 3,
        out_specs=WHOLE,
        compiler_params=budget(queries, payload, payload),
        cost_estimate=pl.CostEstimate(
            flops=count * rows * width,
            bytes_accessed=2 * count * width + 2 * rows * width, transcendentals=0,
        ),
    )(meta, weights_1, queries, send_part)
    query_grad, done = pl.pallas_call(
        grad_kernel,
        out_shape=[
            jax.ShapeDtypeStruct((count, width), jnp.float32),
            jax.ShapeDtypeStruct((8, 128), jnp.float32),
        ],
        in_specs=[WHOLE] * 4,
        out_specs=[WHOLE] * 2,
        compiler_params=budget(queries, queries, rows_1, rows_2),
        cost_estimate=pl.CostEstimate(
            flops=2 * count * (rows_1.size + rows_2.size),
            bytes_accessed=2 * (rows_1.size + rows_2.size) + 4 * count * width,
            transcendentals=0,
        ),
    )(weights_1, weights_2, rows_1, rows_2)
    part = half + LOSS
    quarter = rows // 4
    first = jax.ShapeDtypeStruct((quarter, part), jnp.float32)
    short = jax.ShapeDtypeStruct(first.shape, jnp.bfloat16)
    own, *going = pl.pallas_call(
        functools.partial(first_sum, block),
        out_shape=[first, short] + [
            jax.ShapeDtypeStruct((quarter // 2, part), dtype)
            for dtype in (jnp.float32, jnp.float32, jnp.bfloat16, jnp.bfloat16)
        ],
        in_specs=[WHOLE] * 2,
        out_specs=[WHOLE] * 6,
        compiler_params=budget(payload, payload, payload),
        cost_estimate=pl.CostEstimate(
            flops=payload.size, bytes_accessed=12 * payload.size, transcendentals=0
        ),
    )(kept, sent)
    came = [exchange(value, both, mask) for value, mask in zip(going, (5, 4, 1, 4, 1))]
    second = jax.ShapeDtypeStruct((block, part), jnp.float32)

    def summed(odd, from_x, from_y):
        shapes = [second] * (rest // 2)
        return pl.pallas_call(
            functools.partial(second_sum, odd),
            out_shape=shapes,
            in_specs=[WHOLE] * 4,
            out_specs=[WHOLE] * (rest // 2),
            compiler_params=budget(payload, payload),
            cost_estimate=pl.CostEstimate(
                flops=2 * first.size, bytes_accessed=10 * first.size, transcendentals=0
            ),
        )(own, came[0], from_x, from_y)

    far_sums = summed(1, came[1], came[2])
    total, *near_sums = summed(0, came[3], came[4])
    going = list(zip(far_sums, orders[1:rest:2])) + list(zip(near_sums, orders[2:rest:2]))
    ends = [
        exchange(value, ("loop",), order)
        for value, order in sorted(going, key=lambda pair: -pair[1])
    ]
    total = pl.pallas_call(
        last_sum,
        out_shape=second,
        in_specs=[WHOLE] * (2 + len(ends)),
        out_specs=WHOLE,
        compiler_params=budget(*[second] * (2 + len(ends))),
        cost_estimate=pl.CostEstimate(
            flops=rest * second.size, bytes_accessed=4 * rest * second.size, transcendentals=0
        ),
    )(done, total, *ends)
    mean_loss = (total[0, half] + total[0, half + LOSS // 2]) / (count * loop * reps)
    total = total[:, :half]
    opposite = exchange(total, ("rep",), 1)
    passage_grad = jnp.where(
        rep == 0,
        jnp.concatenate([total, opposite], axis=1),
        jnp.concatenate([opposite, total], axis=1),
    )

    return (query_grad, passage_grad, mean_loss)


def solution(mesh):
    placed = (
        P(("loop", "rep"), None),
        P("loop", None),
        P(("loop", "rep"), None),
        P(("loop", "rep")),
        P("loop", None, None),
        P("loop", None),
    )
    return jax.shard_map(
        shards,
        mesh=mesh,
        in_specs=placed,
        out_specs=(P(("loop", "rep"), None), P("loop", None), P()),
        check_vma=False,
    )
```

```python
import functools

import jax
import jax.numpy as jnp
from jax import lax
from jax.experimental import pallas as pl
from jax.experimental.pallas import tpu as pltpu
from jax.sharding import PartitionSpec as P


def budget(*arrays):
    total = sum(a.size * a.dtype.itemsize for a in arrays)
    return pltpu.CompilerParams(vmem_limit_bytes=total + total // 4 + 6 * 1024 * 1024)


WHOLE = pl.BlockSpec(memory_space=pltpu.VMEM)
SCALARS = pl.BlockSpec(memory_space=pltpu.SMEM)
LOSS = 128


def exchange(value, axes, mask):
    size = 1
    for axis in axes:
        size *= lax.axis_size(axis)
    return lax.ppermute(value, axes, [(i, i ^ mask) for i in range(size)])


def pick_rows(count, reach, meta, other, own, after, *refs):
    asked, (plane, *pieces) = refs[:reach], refs[reach:]
    me, rep = meta[0], meta[1]
    owners = asked[0].shape[1]
    slots = plane.shape[0] // (2 * count)
    lanes = lax.broadcasted_iota(jnp.int32, (slots, owners), 1)
    rows = lax.broadcasted_iota(jnp.int32, (slots, own.shape[0]), 1)

    def hot(owner):
        picked = []
        for m in range(count + len(pieces)):
            at = m % 2 * slots
            tile = asked[-(m // 2)][at:at + slots, :]
            column = jnp.sum(jnp.where(lanes == owner, tile, 0), axis=1, keepdims=True)
            picked.append(jnp.where(column == rows, 1.0, 0.0))
        return jnp.concatenate(picked, axis=0).astype(jnp.bfloat16)

    hot_own = hot(me * 2 + rep)
    hot_other = hot((me ^ 1) * 2 + rep)
    got_other = jnp.dot(hot_other, other[...], preferred_element_type=jnp.float32)
    got_own = jnp.dot(hot_own, own[...], preferred_element_type=jnp.float32)
    for m in range(count + len(pieces)):
        part = slice(m * slots, (m + 1) * slots)
        value = jnp.concatenate([got_own[part], got_other[part]], axis=0).astype(jnp.bfloat16)
        if m < count:
            plane[m * 2 * slots:(m + 1) * 2 * slots, :] = value
        else:
            pieces[m - count][...] = value


def pack_kernel(layouts, *refs):
    ins, outs = refs[:-len(layouts)], refs[-len(layouts):]
    for layout, out in zip(layouts, outs):
        at = 0
        for which, first, rows in layout:
            out[at:at + rows, :] = ins[which][first:first + rows, :]
            at += rows


def pack(layouts, *arrays):
    shapes = [
        jax.ShapeDtypeStruct((sum(rows for _, _, rows in layout), arrays[0].shape[1]), arrays[0].dtype)
        for layout in layouts
    ]
    size = sum(shape.size for shape in shapes)
    return pl.pallas_call(
        functools.partial(pack_kernel, layouts),
        out_shape=shapes,
        in_specs=[WHOLE] * len(arrays),
        out_specs=[WHOLE] * len(layouts),
        compiler_params=budget(*shapes, *arrays),
        cost_estimate=pl.CostEstimate(flops=size, bytes_accessed=4 * size, transcendentals=0),
    )(*arrays)


def stack(counts, refs, out):
    at = 0
    for rows, ref in zip(counts, refs):
        out[at:at + rows, :] = ref[:rows, :]
        at += rows


def scored(queries, rows):
    return 50.0 * lax.dot_general(
        queries[...], rows[...], (((1,), (1,)), ((), ())), preferred_element_type=jnp.float32
    )


def early_kernel(counts, queries, *refs):
    *batches, scores_out, rows = refs
    stack(counts, batches, rows)
    scores_out[...] = scored(queries, rows)


def lookup(index, values):
    total = jnp.zeros_like(index)
    for i, value in enumerate(values):
        total = jnp.where(index == i, value, total)
    return total


def score_kernel(
    counts, passages, columns, slots, meta, hard_counts, queries, positive, scores_ref, *refs
):
    *batches, out_1, out_2, rows, send_out = refs
    batches = batches[-passages:] + batches[:-passages]
    me, rep = meta[0], meta[1]
    stack(counts, batches, rows)
    side = send_out.shape[0]
    block = side // len(columns[0][0])
    blocks = [scores_ref[...], scored(queries, rows)]
    wanted = jnp.broadcast_to(positive[...].astype(jnp.float32), (8, positive.shape[1]))
    wanted = jnp.transpose(wanted)[:, :1]
    onehots = []
    for i, (order, places) in enumerate(columns):
        lane = lax.broadcasted_iota(jnp.int32, (1, blocks[i].shape[1]), 1)
        passage = lane < side
        ids = (lookup(lane // block, order) * block + lane % block) ^ (me * block)
        spot = jnp.where(passage, 0, lane - side)
        owner = lookup(spot // (2 * slots), [4 * m + p for m, p in places])
        owner = (owner + spot // slots % 2 * 2) ^ (me * 2 + rep)
        taken = lookup(owner, [hard_counts[0, o] for o in range(hard_counts.shape[1])])
        live = passage | (spot % slots < taken)
        onehots.append(
            jnp.where((wanted == ids.astype(jnp.float32)) & passage, 1.0, 0.0)
        )
        blocks[i] = jnp.where(live, blocks[i], -jnp.inf)
    tops = [jnp.max(value, axis=1, keepdims=True) for value in blocks]
    row_top = jnp.maximum(tops[0], tops[1])
    sums = [jnp.sum(jnp.exp(value - row_top), axis=1, keepdims=True) for value in blocks]
    log_total = row_top + jnp.log(sums[0] + sums[1])
    weights = [
        (jnp.exp(value - log_total) - onehot).astype(jnp.bfloat16)
        for value, onehot in zip(blocks, onehots)
    ]
    hit = sum(
        jnp.sum(jnp.where(onehot > 0, value, 0.0), axis=1, keepdims=True)
        for value, onehot in zip(blocks, onehots)
    )
    project(send_out, weights[1][:, :side], queries, meta[1], jnp.sum(log_total - hit))
    out_1[...] = weights[0]
    out_2[...] = weights[1]


def project(out, weights, queries, rep, loss):
    half = queries.shape[1] // 2
    for i, side in enumerate((rep, 1 - rep)):
        product = lax.dot_general(
            weights, queries[:, pl.ds(pl.multiple_of(side * half, half), half)],
            (((0,), (0,)), ((), ())), preferred_element_type=jnp.float32,
        )
        at = i * (half + LOSS)
        out[:, at:at + half] = 50.0 * product
        out[:, at + half:at + half + LOSS] = jnp.full((out.shape[0], LOSS), loss, jnp.float32)


def keep_kernel(meta, weights, queries, send, out):
    half = queries.shape[1] // 2
    project(
        out, weights[:, :out.shape[0]], queries, meta[1], send[0:1, half:half + 1]
    )


def first_sum(block, kept, sent, own, to_xy, *halves):
    rows, columns = own.shape
    half = columns - LOSS
    lanes = lax.broadcasted_iota(jnp.int32, (block, LOSS), 1)
    cuts = []
    for i in range(rows // block):
        x_out, y_out = halves[:2] if i % 2 else halves[2:]
        for out, at, down, across in (
            (own, i, 0, 0), (to_xy, i, 1, 1), (x_out, i // 2, 1, 0), (y_out, i // 2, 0, 1)
        ):
            cuts.append((out, at * block, down * rows + i * block, across * columns))
    for out, to, row, column in cuts:
        at, to = pl.ds(row, block), pl.ds(to, block)
        data, tile = pl.ds(column, half), pl.ds(column + half, LOSS)
        out[to, :half] = (kept[at, data] + sent[at, data]).astype(out.dtype)
        loss = kept[at, tile] + sent[at, tile]
        high = loss.astype(jnp.bfloat16).astype(jnp.float32)
        out[to, half:] = jnp.where(lanes < LOSS // 2, high, loss - high).astype(out.dtype)


def second_sum(odd, own, from_xy, from_x, from_y, after, *outs):
    rows, columns = outs[0].shape
    half = columns - LOSS
    lanes = lax.broadcasted_iota(jnp.int32, (rows, LOSS), 1)
    for i, out in enumerate(outs):
        at, near = pl.ds((2 * i + odd) * rows, rows), pl.ds(i * rows, rows)
        total = (own[at] + from_x[near].astype(jnp.float32)) + (
            from_y[near].astype(jnp.float32) + from_xy[at].astype(jnp.float32)
        )
        if out.dtype == jnp.float32:
            out[...] = total
        else:
            loss = total[:, half:half + 1] + total[:, half + LOSS // 2:half + LOSS // 2 + 1]
            high = loss.astype(jnp.bfloat16).astype(jnp.float32)
            out[:, :half] = total[:, :half].astype(out.dtype)
            out[:, half:] = jnp.where(lanes < LOSS // 2, high, loss - high).astype(out.dtype)


def grad_kernel(weights_1, weights_2, rows_1, rows_2, out, done):
    done[...] = jnp.zeros(done.shape, done.dtype)
    out[...] = 50.0 * (
        jnp.dot(weights_1[...], rows_1[...], preferred_element_type=jnp.float32)
        + jnp.dot(weights_2[...], rows_2[...], preferred_element_type=jnp.float32)
    )


def shards(queries, passages, index_rows, positive, hard_rows, hard_counts):
    loop = lax.axis_size("loop")
    reps = lax.axis_size("rep")
    me = lax.axis_index("loop").astype(jnp.int32)
    rep = lax.axis_index("rep").astype(jnp.int32)
    count, width = queries.shape
    block = passages.shape[0]
    owners, slots = hard_rows.shape[1:]
    half = width // 2
    chips = loop // 2
    meta = jnp.stack([me, rep])
    both = ("loop", "rep")

    other_rows = exchange(index_rows, ("loop",), 1)
    rest = loop // 4
    wanted = jnp.transpose(hard_rows, (0, 2, 1)).reshape(slots, owners)
    neighbour, (own_wanted,) = exchange(wanted, ("loop",), 2), pack([[(0, 0, slots)]], wanted)
    asked, = pack([[(0, 0, slots), (1, 0, slots)]], own_wanted, neighbour)
    asked = [asked] + [exchange(asked, ("loop",), 4 * k) for k in reversed(range(1, rest))]
    own_rows, = pack([[(0, 0, index_rows.shape[0])]], index_rows)

    bits = [loop // 2 >> i for i in range(loop.bit_length() - 4)] + [4, 2, 1]
    orders = [0]
    for bit in bits:
        orders = orders + [o | bit for o in orders]
    for bit in bits[:-4]:
        passages = jnp.concatenate([passages, exchange(passages, ("loop",), bit)], axis=0)
    passages_z = exchange(passages, ("loop",), bits[-4])

    depth = 2 * slots
    have = 2 * passages.shape[0]
    top = chips // 2
    outs = [jax.ShapeDtypeStruct((top * depth, width), jnp.bfloat16)]
    outs += [jax.ShapeDtypeStruct((depth, width), jnp.bfloat16)] * top
    known, = pack([[(i, 0, have // 2) for i in range(2)]], passages, passages_z)
    plane, *sends = pl.pallas_call(
        functools.partial(pick_rows, top, rest),
        out_shape=outs,
        in_specs=[SCALARS] + [WHOLE] * (3 + rest),
        out_specs=[WHOLE] * (1 + top),
        compiler_params=budget(index_rows, index_rows, *outs, *outs),
        cost_estimate=pl.CostEstimate(
            flops=4 * chips * slots * index_rows.shape[0] * width,
            bytes_accessed=3 * index_rows.size * 2, transcendentals=0,
        ),
    )(meta, other_rows, own_rows, passages_z, *asked)

    def send(m, value):
        return exchange(value, ("loop",), 2 * m)

    def over(value):
        return exchange(value, ("rep",), 1)

    def cut(arrays, *pieces):
        return [
            (next(i for i, a in enumerate(arrays) if a is array), first, rows)
            for array, first, rows in pieces
        ]

    half_top = top // 2
    inner, outer = range(1, half_top + 1), range(half_top + 1, top)
    opposite_plane = over(plane)
    middle_masks, late_masks = range(top + 1, chips, 2), range(top, chips, 2)
    sends = dict(zip(range(top, chips), sends))
    middle = [send(m, sends[m]) for m in middle_masks]
    held_back = [sends[m] for m in late_masks]
    known = [known, exchange(known, ("loop",), 4)]

    arrays = [plane, opposite_plane, *middle, *known, *held_back]
    quad = [(value, 0, value.shape[0]) for value in known]
    batch, *going = pack(
        [cut(arrays, *[(value, 0, depth) for value in middle])]
        + [
            cut(arrays, (plane, m * depth, depth), (opposite_plane, m * depth, depth),
                *(quad if m == 1 else []))
            for m in inner
        ]
        + [cut(arrays, (value, 0, depth)) for value in held_back],
        *arrays,
    )
    near_batch, far_batch = batch, over(batch)
    came = [send(m, value) for m, value in zip(inner, going)]
    late = [send(m, value) for m, value in zip(late_masks, going[len(inner):])]

    arrays = [plane, opposite_plane, going[0], *late, *came]
    batch, *pair_and_going = pack(
        [cut(arrays, *[(value, 0, depth) for value in late]),
         cut(arrays, (going[0], 2 * depth, 2 * have)),
         cut(arrays, (came[0], 2 * depth, 2 * have))]
        + [
            cut(arrays, (plane, m * depth, depth), (opposite_plane, m * depth, depth))
            for m in outer
        ],
        *arrays, far_batch,
    )
    pair, going = pair_and_going[:2], pair_and_going[2:]
    last = [send(m, value) for m, value in zip(outer, going)] + [over(batch)]
    other_pair = [exchange(value, ("loop",), 1) for value in pair]

    first_rows = [(value, 2 * have) for value in pair]
    first_rows += [(plane, depth), (opposite_plane, depth)]
    first_rows += [(value, 2 * depth) for value in came]
    first_rows += [(value, value.shape[0]) for value in (near_batch, far_batch, batch)]
    last_rows = [(value, value.shape[0]) for value in (*other_pair, *last)]
    first_places = [(m, p) for m in (0, *inner) for p in range(2)]
    first_places += [(m, p) for p in range(2) for m in middle_masks]
    first_places += [(m, 0) for m in late_masks]
    last_places = [(m, p) for m in outer for p in range(2)] + [(m, 1) for m in late_masks]
    side = loop * block // 2
    columns = (
        (tuple(orders[:loop // 2]), tuple(first_places)),
        (tuple(orders[loop // 2:]), tuple(last_places)),
    )
    first_counts = tuple(n for _, n in first_rows)
    last_counts = tuple(n for _, n in last_rows)

    rows = loop * block
    rows_1 = jax.ShapeDtypeStruct((sum(first_counts), width), jnp.bfloat16)
    rows_2 = jax.ShapeDtypeStruct((sum(last_counts), width), jnp.bfloat16)
    payload = jax.ShapeDtypeStruct((side, width + 2 * LOSS), jnp.float32)
    scores, rows_1 = pl.pallas_call(
        functools.partial(early_kernel, first_counts),
        out_shape=[jax.ShapeDtypeStruct((count, rows_1.shape[0]), jnp.float32), rows_1],
        in_specs=[WHOLE] * (1 + len(first_rows)),
        out_specs=[WHOLE] * 2,
        compiler_params=budget(queries, rows_1, rows_1),
        cost_estimate=pl.CostEstimate(
            flops=2 * count * rows_1.size,
            bytes_accessed=2 * (queries.size + 2 * rows_1.size), transcendentals=0,
        ),
    )(queries, *[value for value, _ in first_rows])
    weights_1, weights_2, rows_2, send_part = pl.pallas_call(
        functools.partial(score_kernel, last_counts, len(other_pair), columns, slots),
        out_shape=[
            jax.ShapeDtypeStruct((count, rows_1.shape[0]), jnp.bfloat16),
            jax.ShapeDtypeStruct((count, rows_2.shape[0]), jnp.bfloat16),
            rows_2, payload,
        ],
        in_specs=[SCALARS] * 2 + [WHOLE] * (3 + len(last_rows)),
        out_specs=[WHOLE] * 4,
        compiler_params=budget(queries, rows_2, rows_2, payload, payload),
        cost_estimate=pl.CostEstimate(
            flops=2 * count * (rows_2.size + payload.size),
            bytes_accessed=2 * (queries.size + 2 * rows_2.size) + 4 * payload.size,
            transcendentals=2 * count * (rows_1.shape[0] + rows_2.shape[0]),
        ),
    )(
        meta, hard_counts, queries, positive.reshape(1, count), scores,
        *last, *other_pair,
    )

    sent = exchange(send_part, ("loop",), 1)
    kept = pl.pallas_call(
        keep_kernel,
        out_shape=jax.ShapeDtypeStruct((rows // 2, width + 2 * LOSS), jnp.float32),
        in_specs=[SCALARS] + [WHOLE] * 3,
        out_specs=WHOLE,
        compiler_params=budget(queries, payload, payload),
        cost_estimate=pl.CostEstimate(
            flops=count * rows * width,
            bytes_accessed=2 * count * width + 2 * rows * width, transcendentals=0,
        ),
    )(meta, weights_1, queries, send_part)
    query_grad, done = pl.pallas_call(
        grad_kernel,
        out_shape=[
            jax.ShapeDtypeStruct((count, width), jnp.float32),
            jax.ShapeDtypeStruct((8, 128), jnp.float32),
        ],
        in_specs=[WHOLE] * 4,
        out_specs=[WHOLE] * 2,
        compiler_params=budget(queries, queries, rows_1, rows_2),
        cost_estimate=pl.CostEstimate(
            flops=2 * count * (rows_1.size + rows_2.size),
            bytes_accessed=2 * (rows_1.size + rows_2.size) + 4 * count * width,
            transcendentals=0,
        ),
    )(weights_1, weights_2, rows_1, rows_2)
    part = half + LOSS
    quarter = rows // 4
    first = jax.ShapeDtypeStruct((quarter, part), jnp.float32)
    short = jax.ShapeDtypeStruct(first.shape, jnp.bfloat16)
    own, *going = pl.pallas_call(
        functools.partial(first_sum, block),
        out_shape=[first, short] + [
            jax.ShapeDtypeStruct((quarter // 2, part), dtype)
            for dtype in (jnp.float32, jnp.float32, jnp.bfloat16, jnp.bfloat16)
        ],
        in_specs=[WHOLE] * 2,
        out_specs=[WHOLE] * 6,
        compiler_params=budget(payload, payload, payload),
        cost_estimate=pl.CostEstimate(
            flops=payload.size, bytes_accessed=12 * payload.size, transcendentals=0
        ),
    )(kept, sent)
    came = [exchange(value, both, mask) for value, mask in zip(going, (5, 4, 1, 4, 1))]
    second = jax.ShapeDtypeStruct((block, part), jnp.float32)

    def summed(odd, from_x, from_y, after):
        shapes = [second] * (rest // 2)
        return pl.pallas_call(
            functools.partial(second_sum, odd),
            out_shape=shapes,
            in_specs=[WHOLE] * 5,
            out_specs=[WHOLE] * (rest // 2),
            compiler_params=budget(payload, payload),
            cost_estimate=pl.CostEstimate(
                flops=2 * first.size, bytes_accessed=10 * first.size, transcendentals=0
            ),
        )(own, came[0], from_x, from_y, after)

    far_sums = summed(1, came[1], came[2], done)
    total, *near_sums = summed(0, came[3], came[4], done)
    going = list(zip(far_sums, orders[1:rest:2])) + list(zip(near_sums, orders[2:rest:2]))
    for value, order in sorted(going, key=lambda pair: -pair[1]):
        total = total + exchange(value, ("loop",), order).astype(jnp.float32)
    mean_loss = (total[0, half] + total[0, half + LOSS // 2]) / (count * loop * reps)
    total = total[:, :half]
    opposite = exchange(total, ("rep",), 1)
    passage_grad = jnp.where(
        rep == 0,
        jnp.concatenate([total, opposite], axis=1),
        jnp.concatenate([opposite, total], axis=1),
    )

    return (query_grad, passage_grad, mean_loss)


def solution(mesh):
    placed = (
        P(("loop", "rep"), None),
        P("loop", None),
        P(("loop", "rep"), None),
        P(("loop", "rep")),
        P("loop", None, None),
        P("loop", None),
    )
    return jax.shard_map(
        shards,
        mesh=mesh,
        in_specs=placed,
        out_specs=(P(("loop", "rep"), None), P("loop", None), P()),
        check_vma=False,
    )
```

```python
import functools

import jax
import jax.numpy as jnp
from jax import lax
from jax.experimental import pallas as pl
from jax.experimental.pallas import tpu as pltpu
from jax.sharding import PartitionSpec as P


def budget(*arrays):
    total = sum(a.size * a.dtype.itemsize for a in arrays)
    return pltpu.CompilerParams(vmem_limit_bytes=total + total // 4 + 6 * 1024 * 1024)


WHOLE = pl.BlockSpec(memory_space=pltpu.VMEM)
SCALARS = pl.BlockSpec(memory_space=pltpu.SMEM)
LOSS = 128


def exchange(value, axes, mask):
    size = 1
    for axis in axes:
        size *= lax.axis_size(axis)
    return lax.ppermute(value, axes, [(i, i ^ mask) for i in range(size)])


def pick_rows(count, reach, meta, other, own, after, *refs):
    asked, (plane, *pieces) = refs[:reach], refs[reach:]
    me, rep = meta[0], meta[1]
    owners = asked[0].shape[1]
    slots = plane.shape[0] // (2 * count)
    lanes = lax.broadcasted_iota(jnp.int32, (slots, owners), 1)
    rows = lax.broadcasted_iota(jnp.int32, (slots, own.shape[0]), 1)

    def hot(owner):
        picked = []
        for m in range(count + len(pieces)):
            at = m % 2 * slots
            tile = asked[m // 2][at:at + slots, :]
            column = jnp.sum(jnp.where(lanes == owner, tile, 0), axis=1, keepdims=True)
            picked.append(jnp.where(column == rows, 1.0, 0.0))
        return jnp.concatenate(picked, axis=0).astype(jnp.bfloat16)

    hot_own = hot(me * 2 + rep)
    hot_other = hot((me ^ 1) * 2 + rep)
    got_other = jnp.dot(hot_other, other[...], preferred_element_type=jnp.float32)
    got_own = jnp.dot(hot_own, own[...], preferred_element_type=jnp.float32)
    for m in range(count + len(pieces)):
        part = slice(m * slots, (m + 1) * slots)
        value = jnp.concatenate([got_own[part], got_other[part]], axis=0).astype(jnp.bfloat16)
        if m < count:
            plane[m * 2 * slots:(m + 1) * 2 * slots, :] = value
        else:
            pieces[m - count][...] = value


def pack_kernel(layouts, *refs):
    ins, outs = refs[:-len(layouts)], refs[-len(layouts):]
    for layout, out in zip(layouts, outs):
        at = 0
        for which, first, rows in layout:
            out[at:at + rows, :] = ins[which][first:first + rows, :]
            at += rows


def pack(layouts, *arrays):
    shapes = [
        jax.ShapeDtypeStruct((sum(rows for _, _, rows in layout), arrays[0].shape[1]), arrays[0].dtype)
        for layout in layouts
    ]
    size = sum(shape.size for shape in shapes)
    return pl.pallas_call(
        functools.partial(pack_kernel, layouts),
        out_shape=shapes,
        in_specs=[WHOLE] * len(arrays),
        out_specs=[WHOLE] * len(layouts),
        compiler_params=budget(*shapes, *arrays),
        cost_estimate=pl.CostEstimate(flops=size, bytes_accessed=4 * size, transcendentals=0),
    )(*arrays)


def stack(counts, refs, out):
    at = 0
    for rows, ref in zip(counts, refs):
        out[at:at + rows, :] = ref[:rows, :]
        at += rows


def scored(queries, rows):
    return 50.0 * lax.dot_general(
        queries[...], rows[...], (((1,), (1,)), ((), ())), preferred_element_type=jnp.float32
    )


def early_kernel(counts, queries, *refs):
    *batches, scores_out, rows = refs
    stack(counts, batches, rows)
    scores_out[...] = scored(queries, rows)


def lookup(index, values):
    total = jnp.zeros_like(index)
    for i, value in enumerate(values):
        total = jnp.where(index == i, value, total)
    return total


def score_kernel(
    counts, passages, columns, slots, meta, hard_counts, queries, positive, scores_ref, *refs
):
    *batches, out_1, out_2, rows, send_out = refs
    batches = batches[-passages:] + batches[:-passages]
    me, rep = meta[0], meta[1]
    stack(counts, batches, rows)
    side = send_out.shape[0]
    block = side // len(columns[0][0])
    blocks = [scores_ref[...], scored(queries, rows)]
    wanted = jnp.broadcast_to(positive[...].astype(jnp.float32), (8, positive.shape[1]))
    wanted = jnp.transpose(wanted)[:, :1]
    onehots = []
    for i, (order, places) in enumerate(columns):
        lane = lax.broadcasted_iota(jnp.int32, (1, blocks[i].shape[1]), 1)
        passage = lane < side
        ids = (lookup(lane // block, order) * block + lane % block) ^ (me * block)
        spot = jnp.where(passage, 0, lane - side)
        owner = lookup(spot // (2 * slots), [4 * m + p for m, p in places])
        owner = (owner + spot // slots % 2 * 2) ^ (me * 2 + rep)
        taken = lookup(owner, [hard_counts[0, o] for o in range(hard_counts.shape[1])])
        live = passage | (spot % slots < taken)
        onehots.append(
            jnp.where((wanted == ids.astype(jnp.float32)) & passage, 1.0, 0.0)
        )
        blocks[i] = jnp.where(live, blocks[i], -jnp.inf)
    tops = [jnp.max(value, axis=1, keepdims=True) for value in blocks]
    row_top = jnp.maximum(tops[0], tops[1])
    sums = [jnp.sum(jnp.exp(value - row_top), axis=1, keepdims=True) for value in blocks]
    log_total = row_top + jnp.log(sums[0] + sums[1])
    weights = [
        (jnp.exp(value - log_total) - onehot).astype(jnp.bfloat16)
        for value, onehot in zip(blocks, onehots)
    ]
    hit = sum(
        jnp.sum(jnp.where(onehot > 0, value, 0.0), axis=1, keepdims=True)
        for value, onehot in zip(blocks, onehots)
    )
    project(send_out, weights[1][:, :side], queries, meta[1], jnp.sum(log_total - hit))
    out_1[...] = weights[0]
    out_2[...] = weights[1]


def project(out, weights, queries, rep, loss):
    half = queries.shape[1] // 2
    for i, side in enumerate((rep, 1 - rep)):
        product = lax.dot_general(
            weights, queries[:, pl.ds(pl.multiple_of(side * half, half), half)],
            (((0,), (0,)), ((), ())), preferred_element_type=jnp.float32,
        )
        at = i * (half + LOSS)
        out[:, at:at + half] = 50.0 * product
        out[:, at + half:at + half + LOSS] = jnp.full((out.shape[0], LOSS), loss, jnp.float32)


def keep_kernel(meta, weights, queries, send, out):
    half = queries.shape[1] // 2
    project(
        out, weights[:, :out.shape[0]], queries, meta[1], send[0:1, half:half + 1]
    )


def first_sum(block, kept, sent, own, to_xy, *halves):
    rows, columns = own.shape
    half = columns - LOSS
    lanes = lax.broadcasted_iota(jnp.int32, (block, LOSS), 1)
    cuts = []
    for i in range(rows // block):
        x_out, y_out = halves[:2] if i % 2 else halves[2:]
        for out, at, down, across in (
            (own, i, 0, 0), (to_xy, i, 1, 1), (x_out, i // 2, 1, 0), (y_out, i // 2, 0, 1)
        ):
            cuts.append((out, at * block, down * rows + i * block, across * columns))
    for out, to, row, column in cuts:
        at, to = pl.ds(row, block), pl.ds(to, block)
        data, tile = pl.ds(column, half), pl.ds(column + half, LOSS)
        out[to, :half] = (kept[at, data] + sent[at, data]).astype(out.dtype)
        loss = kept[at, tile] + sent[at, tile]
        high = loss.astype(jnp.bfloat16).astype(jnp.float32)
        out[to, half:] = jnp.where(lanes < LOSS // 2, high, loss - high).astype(out.dtype)


def second_sum(odd, own, from_xy, from_x, from_y, after, *outs):
    rows, columns = outs[0].shape
    half = columns - LOSS
    lanes = lax.broadcasted_iota(jnp.int32, (rows, LOSS), 1)
    for i, out in enumerate(outs):
        at, near = pl.ds((2 * i + odd) * rows, rows), pl.ds(i * rows, rows)
        total = (own[at] + from_x[near].astype(jnp.float32)) + (
            from_y[near].astype(jnp.float32) + from_xy[at].astype(jnp.float32)
        )
        if out.dtype == jnp.float32:
            out[...] = total
        else:
            loss = total[:, half:half + 1] + total[:, half + LOSS // 2:half + LOSS // 2 + 1]
            high = loss.astype(jnp.bfloat16).astype(jnp.float32)
            out[:, :half] = total[:, :half].astype(out.dtype)
            out[:, half:] = jnp.where(lanes < LOSS // 2, high, loss - high).astype(out.dtype)


def grad_kernel(weights_1, weights_2, rows_1, rows_2, out, done):
    done[...] = jnp.zeros(done.shape, done.dtype)
    out[...] = 50.0 * (
        jnp.dot(weights_1[...], rows_1[...], preferred_element_type=jnp.float32)
        + jnp.dot(weights_2[...], rows_2[...], preferred_element_type=jnp.float32)
    )


def shards(queries, passages, index_rows, positive, hard_rows, hard_counts):
    loop = lax.axis_size("loop")
    reps = lax.axis_size("rep")
    me = lax.axis_index("loop").astype(jnp.int32)
    rep = lax.axis_index("rep").astype(jnp.int32)
    count, width = queries.shape
    block = passages.shape[0]
    owners, slots = hard_rows.shape[1:]
    half = width // 2
    chips = loop // 2
    meta = jnp.stack([me, rep])
    both = ("loop", "rep")

    other_rows = exchange(index_rows, ("loop",), 1)
    rest = loop // 4
    wanted = jnp.transpose(hard_rows, (0, 2, 1)).reshape(slots, owners)
    neighbour, (own_wanted,) = exchange(wanted, ("loop",), 2), pack([[(0, 0, slots)]], wanted)
    asked, = pack([[(0, 0, slots), (1, 0, slots)]], own_wanted, neighbour)
    asked = [asked] + [exchange(asked, ("loop",), 4 * k) for k in range(1, rest)]
    own_rows, = pack([[(0, 0, index_rows.shape[0])]], index_rows)

    bits = [loop // 2 >> i for i in range(loop.bit_length() - 4)] + [4, 2, 1]
    orders = [0]
    for bit in bits:
        orders = orders + [o | bit for o in orders]
    for bit in bits[:-4]:
        passages = jnp.concatenate([passages, exchange(passages, ("loop",), bit)], axis=0)
    passages_z = exchange(passages, ("loop",), bits[-4])

    depth = 2 * slots
    have = 2 * passages.shape[0]
    top = chips // 2
    outs = [jax.ShapeDtypeStruct((top * depth, width), jnp.bfloat16)]
    outs += [jax.ShapeDtypeStruct((depth, width), jnp.bfloat16)] * top
    known, = pack([[(i, 0, have // 2) for i in range(2)]], passages, passages_z)
    plane, *sends = pl.pallas_call(
        functools.partial(pick_rows, top, rest),
        out_shape=outs,
        in_specs=[SCALARS] + [WHOLE] * (3 + rest),
        out_specs=[WHOLE] * (1 + top),
        compiler_params=budget(index_rows, index_rows, *outs, *outs),
        cost_estimate=pl.CostEstimate(
            flops=4 * chips * slots * index_rows.shape[0] * width,
            bytes_accessed=3 * index_rows.size * 2, transcendentals=0,
        ),
    )(meta, other_rows, own_rows, passages_z, *asked)

    def send(m, value):
        return exchange(value, ("loop",), 2 * m)

    def over(value):
        return exchange(value, ("rep",), 1)

    def cut(arrays, *pieces):
        return [
            (next(i for i, a in enumerate(arrays) if a is array), first, rows)
            for array, first, rows in pieces
        ]

    half_top = top // 2
    inner, outer = range(1, half_top + 1), range(half_top + 1, top)
    opposite_plane = over(plane)
    middle_masks, late_masks = range(top + 1, chips, 2), range(top, chips, 2)
    sends = dict(zip(range(top, chips), sends))
    middle = [send(m, sends[m]) for m in middle_masks]
    held_back = [sends[m] for m in late_masks]
    known = [known, exchange(known, ("loop",), 4)]

    arrays = [plane, opposite_plane, *middle, *known, *held_back]
    quad = [(value, 0, value.shape[0]) for value in known]
    batch, *going = pack(
        [cut(arrays, *[(value, 0, depth) for value in middle])]
        + [
            cut(arrays, (plane, m * depth, depth), (opposite_plane, m * depth, depth),
                *(quad if m == 1 else []))
            for m in inner
        ]
        + [cut(arrays, (value, 0, depth)) for value in held_back],
        *arrays,
    )
    near_batch, far_batch = batch, over(batch)
    came = [send(m, value) for m, value in zip(inner, going)]
    late = [send(m, value) for m, value in zip(late_masks, going[len(inner):])]

    arrays = [plane, opposite_plane, going[0], *late, *came]
    batch, *pair_and_going = pack(
        [cut(arrays, *[(value, 0, depth) for value in late]),
         cut(arrays, (going[0], 2 * depth, 2 * have)),
         cut(arrays, (came[0], 2 * depth, 2 * have))]
        + [
            cut(arrays, (plane, m * depth, depth), (opposite_plane, m * depth, depth))
            for m in outer
        ],
        *arrays, far_batch,
    )
    pair, going = pair_and_going[:2], pair_and_going[2:]
    last = [over(batch)] + [send(m, value) for m, value in zip(outer, going)]
    other_pair = [exchange(value, ("loop",), 1) for value in pair]

    first_rows = [(value, 2 * have) for value in pair]
    first_rows += [(plane, depth), (opposite_plane, depth)]
    first_rows += [(value, 2 * depth) for value in came]
    first_rows += [(value, value.shape[0]) for value in (near_batch, far_batch, batch)]
    last_rows = [(value, value.shape[0]) for value in (*other_pair, *last)]
    first_places = [(m, p) for m in (0, *inner) for p in range(2)]
    first_places += [(m, p) for p in range(2) for m in middle_masks]
    first_places += [(m, 0) for m in late_masks]
    last_places = [(m, 1) for m in late_masks] + [(m, p) for m in outer for p in range(2)]
    side = loop * block // 2
    columns = (
        (tuple(orders[:loop // 2]), tuple(first_places)),
        (tuple(orders[loop // 2:]), tuple(last_places)),
    )
    first_counts = tuple(n for _, n in first_rows)
    last_counts = tuple(n for _, n in last_rows)

    rows = loop * block
    rows_1 = jax.ShapeDtypeStruct((sum(first_counts), width), jnp.bfloat16)
    rows_2 = jax.ShapeDtypeStruct((sum(last_counts), width), jnp.bfloat16)
    payload = jax.ShapeDtypeStruct((side, width + 2 * LOSS), jnp.float32)
    scores, rows_1 = pl.pallas_call(
        functools.partial(early_kernel, first_counts),
        out_shape=[jax.ShapeDtypeStruct((count, rows_1.shape[0]), jnp.float32), rows_1],
        in_specs=[WHOLE] * (1 + len(first_rows)),
        out_specs=[WHOLE] * 2,
        compiler_params=budget(queries, rows_1, rows_1),
        cost_estimate=pl.CostEstimate(
            flops=2 * count * rows_1.size,
            bytes_accessed=2 * (queries.size + 2 * rows_1.size), transcendentals=0,
        ),
    )(queries, *[value for value, _ in first_rows])
    weights_1, weights_2, rows_2, send_part = pl.pallas_call(
        functools.partial(score_kernel, last_counts, len(other_pair), columns, slots),
        out_shape=[
            jax.ShapeDtypeStruct((count, rows_1.shape[0]), jnp.bfloat16),
            jax.ShapeDtypeStruct((count, rows_2.shape[0]), jnp.bfloat16),
            rows_2, payload,
        ],
        in_specs=[SCALARS] * 2 + [WHOLE] * (3 + len(last_rows)),
        out_specs=[WHOLE] * 4,
        compiler_params=budget(queries, rows_2, rows_2, payload, payload),
        cost_estimate=pl.CostEstimate(
            flops=2 * count * (rows_2.size + payload.size),
            bytes_accessed=2 * (queries.size + 2 * rows_2.size) + 4 * payload.size,
            transcendentals=2 * count * (rows_1.shape[0] + rows_2.shape[0]),
        ),
    )(
        meta, hard_counts, queries, positive.reshape(1, count), scores,
        *last, *other_pair,
    )

    sent = exchange(send_part, ("loop",), 1)
    kept = pl.pallas_call(
        keep_kernel,
        out_shape=jax.ShapeDtypeStruct((rows // 2, width + 2 * LOSS), jnp.float32),
        in_specs=[SCALARS] + [WHOLE] * 3,
        out_specs=WHOLE,
        compiler_params=budget(queries, payload, payload),
        cost_estimate=pl.CostEstimate(
            flops=count * rows * width,
            bytes_accessed=2 * count * width + 2 * rows * width, transcendentals=0,
        ),
    )(meta, weights_1, queries, send_part)
    query_grad, done = pl.pallas_call(
        grad_kernel,
        out_shape=[
            jax.ShapeDtypeStruct((count, width), jnp.float32),
            jax.ShapeDtypeStruct((8, 128), jnp.float32),
        ],
        in_specs=[WHOLE] * 4,
        out_specs=[WHOLE] * 2,
        compiler_params=budget(queries, queries, rows_1, rows_2),
        cost_estimate=pl.CostEstimate(
            flops=2 * count * (rows_1.size + rows_2.size),
            bytes_accessed=2 * (rows_1.size + rows_2.size) + 4 * count * width,
            transcendentals=0,
        ),
    )(weights_1, weights_2, rows_1, rows_2)
    part = half + LOSS
    quarter = rows // 4
    first = jax.ShapeDtypeStruct((quarter, part), jnp.float32)
    short = jax.ShapeDtypeStruct(first.shape, jnp.bfloat16)
    own, *going = pl.pallas_call(
        functools.partial(first_sum, block),
        out_shape=[first, short] + [
            jax.ShapeDtypeStruct((quarter // 2, part), dtype)
            for dtype in (jnp.float32, jnp.float32, jnp.bfloat16, jnp.bfloat16)
        ],
        in_specs=[WHOLE] * 2,
        out_specs=[WHOLE] * 6,
        compiler_params=budget(payload, payload, payload),
        cost_estimate=pl.CostEstimate(
            flops=payload.size, bytes_accessed=12 * payload.size, transcendentals=0
        ),
    )(kept, sent)
    came = [exchange(value, both, mask) for value, mask in zip(going, (5, 4, 1, 4, 1))]
    second = jax.ShapeDtypeStruct((block, part), jnp.float32)

    def summed(odd, from_x, from_y, after):
        shapes = [second] * (rest // 2)
        return pl.pallas_call(
            functools.partial(second_sum, odd),
            out_shape=shapes,
            in_specs=[WHOLE] * 5,
            out_specs=[WHOLE] * (rest // 2),
            compiler_params=budget(payload, payload),
            cost_estimate=pl.CostEstimate(
                flops=2 * first.size, bytes_accessed=10 * first.size, transcendentals=0
            ),
        )(own, came[0], from_x, from_y, after)

    far_sums = summed(1, came[1], came[2], done)
    total, *near_sums = summed(0, came[3], came[4], done)
    going = list(zip(far_sums, orders[1:rest:2])) + list(zip(near_sums, orders[2:rest:2]))
    for value, order in sorted(going, key=lambda pair: -pair[1]):
        total = total + exchange(value, ("loop",), order).astype(jnp.float32)
    mean_loss = (total[0, half] + total[0, half + LOSS // 2]) / (count * loop * reps)
    total = total[:, :half]
    opposite = exchange(total, ("rep",), 1)
    passage_grad = jnp.where(
        rep == 0,
        jnp.concatenate([total, opposite], axis=1),
        jnp.concatenate([opposite, total], axis=1),
    )

    return (query_grad, passage_grad, mean_loss)


def solution(mesh):
    placed = (
        P(("loop", "rep"), None),
        P("loop", None),
        P(("loop", "rep"), None),
        P(("loop", "rep")),
        P("loop", None, None),
        P("loop", None),
    )
    return jax.shard_map(
        shards,
        mesh=mesh,
        in_specs=placed,
        out_specs=(P(("loop", "rep"), None), P("loop", None), P()),
        check_vma=False,
    )
```
